32 devices in a mesh: group: 2 (over y), seq: 4 (over z), exp: 2 (over x), tp: 2 (over core).
Axes of the slice: x: 2, y: 2, z: 4, core: 2. Of those that a mesh axis runs over, the one named last changes fastest.
Arguments:
- queries: bfloat16 [4, 512, 4096], P(('group', 'exp'), ('seq', 'tp')), parts along dimension 0, may hold values from -18 to 18
- keys_values: bfloat16 [4, 768, 2, 1024], P(('group', 'exp'), ('seq', 'tp')), parts along dimension 0, may hold values from -18 to 18
- prompt_lengths: int32 [4], P(('group', 'exp')), parts along dimension 0, may hold values from 1 to 256, 384 in all
- routes: int32 [4, 512, 8], P(('group', 'exp'), ('seq', 'tp')), parts along dimension 0, may hold values from 0 to 63, all different within a row; in each aligned block of 64 rows (0 to 63, 64 to 127, ..., all dimensions but the last counted through in order) at most 16 rows name the same one
- gate_weights: float32 [4, 512, 8], P(('group', 'exp'), ('seq', 'tp')), parts along dimension 0, may hold values from 0.05 to 0.5
- norm_gain: float32 [4096], replicated, may hold values from 0.5 to 1.5
- w_gate: bfloat16 [2, 4096, 2048], P('tp', None, 'seq'), may hold values from -0.09375 to 0.09375
- w_up: bfloat16 [2, 4096, 2048], P('tp', None, 'seq'), may hold values from -0.09375 to 0.09375
- w_down: bfloat16 [2, 2048, 4096], P('tp', 'seq'), may hold values from -0.125 to 0.125
Outputs:
- mixed: bfloat16 [4, 512, 4096], P(('group', 'exp'), ('seq', 'tp')), parts along dimension 0
The draws below stay inside these ranges and needn't reach their ends.
There are 2 independent parts, one for each index of `group`. The reference program is written for one: setup_inputs(seed, part) draws one part's arguments, and reference() takes and returns one part's arrays. A program takes and returns all parts, laid end to end along the dimension named above; an argument that names none is the same for every part. Nothing has to cross between parts.
Inputs may be any that keep to these rules, and one draw needn't show every extreme that they name: Each token's 8 routes name different experts. Among the 64 consecutive tokens of one device no expert is named by more than 16 tokens, a bound that some block reaches.
All inputs are finite; a program needn't handle non-finite values. No bound on the sum of `prompt_lengths` on one device may be relied on, other than what follows from the above.
Results may differ from the reference program's by a relative error of at most 0.02.
Values may be sent and summed in bfloat16 or wider, within the bound.
No kernel may reach another device: no remote copies, remote signals or barrier semaphores. Data moves between devices by JAX's collectives and lax.ppermute only.
A program may use at most 128 MiB of HBM per device.

```python
import math
import jax
import jax.numpy as jnp
import numpy as np
from jax import lax

D = 4096
HEADS = 32
KV_HEADS = 8
HEAD_DIM = 128
EXPERTS = 64
TOP = 8
FF = 2048
PROMPT = 256
TOK_DEV = 64
IMAGES = 2
LEN = 512
KEYS = 768
WIN = 2
CAP = 16
N_SEQ = 4


def attention_pair(key):
    base_key = jax.random.fold_in(key, 7001)
    pair_width = KV_HEADS * HEAD_DIM
    pair_rows = jnp.clip(jax.random.normal(jax.random.fold_in(base_key, 1), (IMAGES, KEYS, 2, pair_width), jnp.float32), -3.0, 3.0)
    column_scale = jnp.exp(jax.random.uniform(jax.random.fold_in(base_key, 2), (pair_width,), jnp.float32, 0.0, math.log(10.0))) / 3.0
    query_rows = jnp.clip(jax.random.normal(jax.random.fold_in(base_key, 3), (IMAGES, LEN, HEADS * HEAD_DIM), jnp.float32), -3.0, 3.0)
    pair_rows = pair_rows.at[:, :, 1, :].multiply(column_scale)
    return (query_rows, pair_rows)


def draw_queries(key, part):
    return attention_pair(key)[0].astype(jnp.bfloat16)


def draw_keys_values(key, part):
    return attention_pair(key)[1].astype(jnp.bfloat16)


def levels(rng, extent, split, smallest, top_value):
    def one(dim, shards_of):
        steps = jax.random.uniform(jax.random.fold_in(jax.random.fold_in(rng, 6), dim), (shards_of,), jnp.float32, smallest / len(split), top_value / len(split))
        return jnp.repeat(jnp.exp(steps), extent[dim] // shards_of).reshape((-1,) + (1,) * (len(extent) - dim - 1))

    loudness = one(*split[0])
    for cut in split[1:]:
        loudness = loudness * one(*cut)
    return loudness


def split_up(amount, total, limit, lean):
    loads = [(1 << 20) // math.isqrt(grade ** lean) + 1 for grade in range(2, amount + 1)]
    rest, counts = total - limit - (amount - 1), [1] * (amount - 1)
    while rest > 0:
        free = [i for i in range(amount - 1) if counts[i] < limit]
        whole, budget = sum([loads[i] for i in free]), rest
        for i in free:
            addition = min(limit - counts[i], max(1, budget * loads[i] // whole), rest)
            counts[i] = counts[i] + addition
            rest = rest - addition
    return np.array([limit] + counts)


def ragged(key, number_of, total, reach, slope):
    if number_of == 2:
        one = jax.random.randint(key, (), max(1, total - reach), min(reach, total - 1) + 1)
        return jnp.stack([one, total - one])
    lengths = jnp.asarray(split_up(number_of, total, reach, slope), jnp.int32)
    couples = (number_of - 1) // 2
    donor, receiver = lengths[1:1 + 2 * couples:2], lengths[2:2 + 2 * couples:2]
    slack = jnp.minimum(donor - 1, reach - receiver)
    shifted = jax.random.randint(jax.random.fold_in(key, 1), (couples,), 0, 1 << 20) % (slack + 1)
    lengths = lengths.at[1:1 + 2 * couples:2].set(donor - shifted).at[2:2 + 2 * couples:2].set(receiver + shifted)
    return lengths[jax.random.permutation(jax.random.fold_in(key, 2), number_of)]


def assign_block(own_key, own, number, rows, number_of, top, limit, skew):
    ranking = jax.random.permutation(own_key, number_of)
    crowded, ordinary = portions_of(number_of, rows * top, limit, skew, True), portions_of(number_of, rows * top, limit, skew, False)
    places = jnp.arange(number_of)

    def named(tallies, rotation):
        used = int((tallies > 0).sum())
        fixed = max(1, used // 4)
        passed = fixed + (places - fixed + rotation * (used - fixed)) % max(1, number_of - fixed)
        return jnp.zeros((number_of,), jnp.int32).at[ranking[jnp.where(places < fixed, places, passed)]].set(jnp.asarray(tallies, jnp.int32))

    tallies = jnp.where(number % 4 == 0, named(crowded, number // 4), named(ordinary, number - number // 4 - 1))
    mixed = jax.random.permutation(jax.random.fold_in(own, 3), number_of)
    source_of, receiver = mixed[0:number_of // 2 * 2:2], mixed[1:number_of // 2 * 2:2]
    room = jnp.minimum(tallies[source_of] - 1, limit - tallies[receiver]) // 2
    room = jnp.where((source_of == ranking[0]) | (receiver == ranking[0]) | (tallies[receiver] == 0), 0, jnp.maximum(room, 0))
    passed = jax.random.randint(jax.random.fold_in(own, 4), (number_of // 2,), 0, 1 << 20) % (room + 1)
    tallies = tallies.at[source_of].add(-passed).at[receiver].add(passed)
    labels = jnp.searchsorted(jnp.cumsum(tallies), jnp.arange(rows * top), side="right").astype(jnp.int32)
    listing = labels.reshape(top, rows).T
    listing = listing[jax.random.permutation(jax.random.fold_in(own, 1), rows)]
    rotation = jax.random.randint(jax.random.fold_in(own, 2), (rows, 1), 0, top)
    return jnp.take_along_axis(listing, (jnp.arange(top)[None, :] + rotation) % top, axis=1)


def portions_of(amount, total, limit, slope, full):
    loads = [(1 << 20) // math.isqrt(grade ** slope) + 1 for grade in range(1, amount + 1)]
    largest = limit if full else min(limit, max(-(-total // amount), total * loads[0] // sum(loads)))
    least = 1 if total - largest >= amount - 1 else 0
    given, rest = [largest] + [least] * (amount - 1), total - largest - least * (amount - 1)
    while rest > 0:
        candidates = [i for i in range(1, amount) if given[i] < largest] or [i for i in range(1, amount) if given[i] < limit]
        mass, budget = sum([loads[i] for i in candidates]), rest
        for i in candidates:
            addition = min(limit - given[i], max(1, budget * loads[i] // mass), rest)
            given[i] = given[i] + addition
            rest = rest - addition
    return np.array(given)


def scatter_about(stream_key, shape, spread, limit, shards=(), dtype=jnp.bfloat16):
    values = jax.random.normal(stream_key, shape, jnp.float32) * spread
    if len(shards) > 0:
        values = levels(stream_key, shape, shards, -0.22, 0.18) * values
    return jnp.clip(values, min=-limit, max=limit).astype(dtype)


def setup_inputs(seed: int = 0, part: int = 0) -> dict:
    streams_of = jax.random.split(jax.random.key(seed), 10)
    own_keys = jax.random.split(jax.random.fold_in(streams_of[9], part), 10)
    queries = draw_queries(jax.random.fold_in(jax.random.fold_in(streams_of[9], part), 71), part)
    keys_values = draw_keys_values(jax.random.fold_in(jax.random.fold_in(streams_of[9], part), 71), part)
    prompt_lengths = ragged(own_keys[2], IMAGES, (IMAGES + 1) * PROMPT // 2, PROMPT, 0).astype(jnp.int32)
    routes_keys = jax.random.split(jax.random.fold_in(own_keys[3], 1), IMAGES * LEN // TOK_DEV)
    routes_turns = jax.random.permutation(jax.random.fold_in(own_keys[3], 3), IMAGES * LEN // TOK_DEV)
    routes = jax.vmap(lambda own, number: assign_block(jax.random.fold_in(own_keys[3], 2), own, number, TOK_DEV, EXPERTS, TOP, CAP, 2))(routes_keys, routes_turns).reshape((IMAGES, LEN, TOP))
    gate_weights = jnp.clip(jnp.exp(math.log(0.5) - 2.3025851 * jax.random.uniform(own_keys[4], (IMAGES, LEN, TOP), jnp.float32) ** levels(own_keys[4], (IMAGES, LEN, TOP), ((0, 2), (1, 8)), -0.2, 0.2)), 0.05, 0.5)
    norm_gain = jnp.clip(1.0 + 0.1 * jax.random.normal(streams_of[5], (D,), jnp.float32), 0.5, 1.5)
    w_gate = scatter_about(streams_of[6], (WIN, D, FF), D ** -0.5, 0.09375, ((0, 2), (2, 4)))
    w_up = scatter_about(streams_of[7], (WIN, D, FF), D ** -0.5, 0.09375, ((0, 2), (2, 4)))
    w_down = scatter_about(streams_of[8], (WIN, FF, D), FF ** -0.5, 0.125, ((0, 2), (1, 4)))
    return dict(queries=queries, keys_values=keys_values, prompt_lengths=prompt_lengths, routes=routes, gate_weights=gate_weights, norm_gain=norm_gain, w_gate=w_gate, w_up=w_up, w_down=w_down)


epsilon = 1e-06
masked_score = -1e+30

def rounded(values):
    return lax.optimization_barrier(values.astype(jnp.bfloat16)).astype(jnp.float32)

def attend_image(operands):
    queries_image, pairs_image, prompt_length = operands
    group = HEADS // KV_HEADS
    query_f = jnp.transpose(queries_image.astype(jnp.float32).reshape(LEN, KV_HEADS, group, HEAD_DIM), (1, 0, 2, 3))
    key_f = jnp.transpose(pairs_image[:, 0].astype(jnp.float32).reshape(KEYS, KV_HEADS, HEAD_DIM), (1, 0, 2))
    value_f = jnp.transpose(pairs_image[:, 1].astype(jnp.float32).reshape(KEYS, KV_HEADS, HEAD_DIM), (1, 0, 2))
    position = jnp.arange(KEYS).astype(jnp.int32)
    allowed = (position >= PROMPT) | (position < prompt_length)

    def one_head(pieces):
        query_head, key_head, value_head = pieces
        scores = jnp.einsum('lrd,kd->rlk', query_head, key_head) * (1.0 / math.sqrt(HEAD_DIM))
        scores = jnp.where(allowed, scores, masked_score)
        largest = lax.optimization_barrier(jnp.max(scores, axis=-1, keepdims=True))
        weights = jnp.where(allowed, jnp.exp(scores - largest), 0.0)
        totals = lax.optimization_barrier(jnp.sum(weights, axis=-1))
        summed = jnp.einsum('rlk,kd->lrd', rounded(weights), value_head)
        return summed / jnp.transpose(totals)[..., None]
    result = lax.map(one_head, (query_f, key_f, value_f))
    return jnp.transpose(result, (1, 0, 2, 3)).reshape(LEN, D).astype(jnp.bfloat16)

def reference(queries, keys_values, prompt_lengths, routes, gate_weights, norm_gain, w_gate, w_up, w_down):
    attended = lax.map(attend_image, (queries, keys_values, prompt_lengths))
    token_count = IMAGES * LEN
    flat_attended = attended.reshape(token_count, D).astype(jnp.float32)
    mean_square = lax.optimization_barrier(jnp.mean(flat_attended * flat_attended, axis=-1, keepdims=True))
    normed = (flat_attended * lax.rsqrt(mean_square + epsilon) * norm_gain).astype(jnp.bfloat16)
    route_ids = routes.reshape(token_count, TOP)
    route_gates = gate_weights.reshape(token_count, TOP)
    most_rows = token_count // TOK_DEV * CAP
    block_width = FF // N_SEQ
    combined = jnp.zeros((token_count, D), jnp.float32)
    for expert in range(WIN):
        hits = route_ids == expert
        member = jnp.any(hits, axis=1)
        weight = lax.optimization_barrier(jnp.sum(jnp.where(hits, route_gates, 0.0), axis=1))
        positions = jnp.nonzero(member, size=most_rows, fill_value=0)[0].astype(jnp.int32)
        filled = jnp.arange(most_rows) < jnp.sum(member.astype(jnp.int32))
        rows = normed[positions]
        gate_part = jnp.dot(rows, w_gate[expert], preferred_element_type=jnp.float32)
        up_part = jnp.dot(rows, w_up[expert], preferred_element_type=jnp.float32)
        hidden_units = (jax.nn.silu(gate_part) * up_part).astype(jnp.bfloat16)
        hidden_blocks = hidden_units.astype(jnp.float32).reshape(most_rows, N_SEQ, block_width)
        down_blocks = w_down[expert].astype(jnp.float32).reshape(N_SEQ, block_width, D)
        block_sums = rounded(jnp.einsum('rbf,bfd->rbd', hidden_blocks, down_blocks))
        expert_out = rounded(lax.optimization_barrier(jnp.sum(block_sums, axis=1)))
        scale_rows = jnp.where(filled, weight[positions], 0.0)
        combined = combined.at[positions].add(scale_rows[:, None] * expert_out)
    mixed = (flat_attended + combined).astype(jnp.bfloat16)
    return mixed.reshape(IMAGES, LEN, D)
```

```python
import functools
import math

import jax
import jax.numpy as jnp
from jax import lax
from jax.experimental import pallas as pl
from jax.experimental.pallas import tpu as pltpu
from jax.sharding import PartitionSpec as P

HEAD_DIM = 128
PROMPT = 256
CAP = 16
TILE = 16

epsilon = 1e-06
masked_score = -1e30
MIB = 1024 * 1024

VMEM = pl.BlockSpec(memory_space=pltpu.VMEM)
SMEM = pl.BlockSpec(memory_space=pltpu.SMEM)
ANY = pl.BlockSpec(memory_space=pl.ANY)


def params(mib):
    return pltpu.CompilerParams(vmem_limit_bytes=mib * MIB)


def cost(flops, moved, transcendentals=0):
    return pl.CostEstimate(
        flops=int(flops), bytes_accessed=int(moved), transcendentals=int(transcendentals)
    )


def pick_kernel(me_ref, routes_ref, gates_ref, q_ref, keep_ref, send_ref, comb_ref):
    tokens = routes_ref.shape[0]
    me = me_ref[0]
    routes = routes_ref[...]
    gates = gates_ref[...]
    column = lax.broadcasted_iota(jnp.int32, (tokens, 2 * CAP), 1)
    mine = column < CAP

    def of_expert(expert):
        hit = routes == expert
        member = jnp.sum(hit.astype(jnp.float32), axis=1, keepdims=True)
        weight = jnp.sum(jnp.where(hit, gates, 0.0), axis=1, keepdims=True)
        return member, weight

    member_a, weight_a = of_expert(me)
    member_b, weight_b = of_expert(1 - me)
    member = jnp.where(mine, member_a, member_b)
    weight = jnp.where(mine, weight_a, weight_b)
    row = lax.broadcasted_iota(jnp.int32, (tokens, tokens), 0)
    col = lax.broadcasted_iota(jnp.int32, (tokens, tokens), 1)
    before = (col < row).astype(jnp.float32).astype(jnp.bfloat16)
    slot = jnp.dot(before, member.astype(jnp.bfloat16), preferred_element_type=jnp.float32)
    wanted = jnp.where(mine, column, column - CAP).astype(jnp.float32)
    taken = jnp.where((member > 0.0) & (slot == wanted), 1.0, 0.0)
    comb_ref[...] = taken * weight
    rows = lax.dot_general(
        taken.astype(jnp.bfloat16),
        q_ref[...],
        (((0,), (0,)), ((), ())),
        preferred_element_type=jnp.float32,
    ).astype(jnp.bfloat16)
    keep_ref[...] = rows[:CAP]
    send_ref[...] = rows[CAP:]


def key_bias(place_ref, pieces, rows_each, rows_true):
    length = place_ref[pieces]
    parts = []
    lane = lax.broadcasted_iota(jnp.int32, (8, rows_each), 1)
    for i in range(pieces):
        position = lane + place_ref[i]
        allowed = (position >= PROMPT) | (position < length)
        allowed = allowed & (lane < rows_true)
        parts.append(jnp.where(allowed, 0.0, masked_score))
    return jnp.concatenate(parts, axis=1)[:1]


def attend(queries, kv_refs, bias, store, per_key):
    width = kv_refs[0].shape[1] // 2
    heads = width // HEAD_DIM
    factor = math.log2(math.e) / math.sqrt(HEAD_DIM)
    for head in range(heads):
        at = head * HEAD_DIM
        keys = jnp.concatenate([r[:, at : at + HEAD_DIM] for r in kv_refs], axis=0)
        values = jnp.concatenate(
            [r[:, width + at : width + at + HEAD_DIM] for r in kv_refs], axis=0
        )
        values = jnp.concatenate([values, jnp.ones_like(values)], axis=1)
        block = queries(head * per_key * HEAD_DIM, per_key * HEAD_DIM)
        rows = block.shape[0]
        stacked = jnp.concatenate(
            [block[:, j * HEAD_DIM : (j + 1) * HEAD_DIM] for j in range(per_key)], axis=0
        )
        scores = (
            lax.dot_general(
                stacked, keys, (((1,), (1,)), ((), ())), preferred_element_type=jnp.float32
            )
            * factor
            + bias
        )
        weights = jnp.exp2(scores - jnp.max(scores, axis=1, keepdims=True))
        summed = jnp.dot(
            weights.astype(jnp.bfloat16), values, preferred_element_type=jnp.float32
        )
        result = (summed[:, :HEAD_DIM] / summed[:, HEAD_DIM:]).astype(jnp.bfloat16)
        for j in range(per_key):
            store(
                (head * per_key + j) * HEAD_DIM, result[j * rows : (j + 1) * rows]
            )


def attend_kernel(pieces, blocks, per_key, rows_true, place_ref, *refs):
    q_refs = refs[:blocks]
    kv_refs = refs[blocks : blocks + pieces]
    out_refs = refs[blocks + pieces :]
    bias = key_bias(place_ref, pieces, kv_refs[0].shape[0], rows_true)

    def queries(at, size):
        return jnp.concatenate([r[:, at : at + size] for r in q_refs], axis=0)

    def store(at, result):
        begin = 0
        for r in out_refs:
            r[:, at : at + HEAD_DIM] = result[begin : begin + r.shape[0]]
            begin += r.shape[0]

    attend(queries, kv_refs, bias, store, per_key)


def attend_call(place, q_blocks, kv_pieces, out_rows, rows_true):
    width = q_blocks[0].shape[1]
    per_key = width // (kv_pieces[0].shape[1] // 2)
    rows = sum(q.shape[0] for q in q_blocks)
    keys = sum(p.shape[0] for p in kv_pieces)
    return pl.pallas_call(
        functools.partial(
            attend_kernel, len(kv_pieces), len(q_blocks), per_key, rows_true
        ),
        out_shape=[jax.ShapeDtypeStruct((r, width), jnp.bfloat16) for r in out_rows],
        in_specs=[SMEM] + [VMEM] * (len(q_blocks) + len(kv_pieces)),
        out_specs=[VMEM] * len(out_rows),
        compiler_params=params(40),
        cost_estimate=cost(
            4 * rows * width * keys,
            4 * rows * width + 2 * keys * kv_pieces[0].shape[1],
            rows * keys * width // HEAD_DIM,
        ),
        name="attend",
    )(place, *q_blocks, *kv_pieces)


def expert_kernel(
    pieces, homes, per_key, rows_true, place_ref, done_ref, last_ref, *refs
):
    kv_refs = refs[:pieces]
    gain_ref, gate_hbm, up_hbm, down_hbm = refs[pieces : pieces + 4]
    out_refs = refs[pieces + 4 : pieces + 4 + homes]
    x_ref, gate_ref, up_ref, down_ref, sems = refs[pieces + 4 + homes :]
    copies = [
        pltpu.make_async_copy(src, dst, sems.at[i])
        for i, (src, dst) in enumerate(
            ((gate_hbm, gate_ref), (up_hbm, up_ref), (down_hbm, down_ref))
        )
    ]
    for c in copies:
        c.start()
    bias = key_bias(place_ref, pieces, kv_refs[0].shape[0], rows_true)
    ahead = done_ref.shape[0]
    rows = x_ref.shape[0]

    def queries(at, size):
        return last_ref[:, at : at + size]

    def store(at, result):
        x_ref[ahead:rows, at : at + HEAD_DIM] = result

    attend(queries, kv_refs, bias, store, per_key)
    x_ref[:ahead, :] = done_ref[...]
    x = x_ref[...].astype(jnp.float32)
    square = jnp.mean(x * x, axis=1, keepdims=True)
    normed = (x * lax.rsqrt(square + epsilon) * gain_ref[...]).astype(jnp.bfloat16)
    copies[0].wait()
    gate = jnp.dot(normed, gate_ref[...], preferred_element_type=jnp.float32)
    copies[1].wait()
    up = jnp.dot(normed, up_ref[...], preferred_element_type=jnp.float32)
    hidden = (gate / (1.0 + jnp.exp(-gate)) * up).astype(jnp.bfloat16)
    copies[2].wait()
    part = jnp.dot(hidden, down_ref[...], preferred_element_type=jnp.float32).astype(
        jnp.bfloat16
    )
    each = rows // homes
    for i, r in enumerate(out_refs):
        r[...] = part[i * each : (i + 1) * each]


def expert_call(place, done, last, kv_pieces, gain, w_gate, w_up, w_down, rows_true):
    each, width = last.shape
    homes = done.shape[0] // each + 1
    rows = homes * each
    hidden = w_gate.shape[1]
    per_key = width // (kv_pieces[0].shape[1] // 2)
    return pl.pallas_call(
        functools.partial(expert_kernel, len(kv_pieces), homes, per_key, rows_true),
        out_shape=[jax.ShapeDtypeStruct((each, width), jnp.bfloat16)] * homes,
        in_specs=[SMEM] + [VMEM] * (3 + len(kv_pieces)) + [ANY] * 3,
        out_specs=[VMEM] * homes,
        scratch_shapes=[
            pltpu.VMEM((rows, width), jnp.bfloat16),
            pltpu.VMEM(w_gate.shape, jnp.bfloat16),
            pltpu.VMEM(w_up.shape, jnp.bfloat16),
            pltpu.VMEM(w_down.shape, jnp.bfloat16),
            pltpu.SemaphoreType.DMA((3,)),
        ],
        compiler_params=params(48),
        cost_estimate=cost(6 * rows * width * hidden, 6 * width * hidden),
        name="experts",
    )(place, done, last, *kv_pieces, gain, w_gate, w_up, w_down)


def combine_kernel(count, comb_ref, attended_ref, *refs):
    out_ref = refs[-1]

    def total(terms):
        first = terms[0][...].astype(jnp.float32)
        for t in terms[1:]:
            first = first + t[...].astype(jnp.float32)
        return first.astype(jnp.bfloat16)

    rows = jnp.concatenate([total(refs[:count]), total(refs[count:-1])], axis=0)
    comb = comb_ref[...]
    high = comb.astype(jnp.bfloat16)
    low = (comb - high.astype(jnp.float32)).astype(jnp.bfloat16)
    added = jnp.dot(high, rows, preferred_element_type=jnp.float32) + jnp.dot(
        low, rows, preferred_element_type=jnp.float32
    )
    out_ref[...] = (attended_ref[...].astype(jnp.float32) + added).astype(jnp.bfloat16)


def across(x, stride):
    n = lax.axis_size("seq")
    return lax.ppermute(x, "seq", [(i, i ^ stride) for i in range(n)])


def swap(x):
    return lax.ppermute(x, "tp", [(0, 1), (1, 0)])


def across_and_swap(x, stride):
    n = lax.axis_size("seq")
    pairs = [
        (2 * i + c, 2 * (i ^ stride) + 1 - c) for i in range(n) for c in range(2)
    ]
    return lax.ppermute(x, ("seq", "tp"), pairs)


def strides_of(n):
    return [1 << b for b in reversed(range(n.bit_length() - 1))]


def gather(own):
    blocks, order = [own], [0]
    for stride in strides_of(lax.axis_size("seq")):
        blocks = blocks + [across(b, stride) for b in blocks]
        order = order + [k ^ stride for k in order]
    return blocks, order


def body(
    queries, keys_values, prompt_lengths, routes, gate_weights, norm_gain, w_gate, w_up, w_down
):
    tokens, width = queries.shape[1:]
    rows_true = keys_values.shape[1]
    pad = -rows_true % TILE
    seq, core = lax.axis_index("seq"), lax.axis_index("tp")
    own_queries = queries[0]

    kv = keys_values[0].reshape(rows_true, -1)
    if pad:
        kv = jnp.pad(kv, ((0, pad), (0, 0)))
    kv_blocks, order = gather(kv)

    keep, send, comb = pl.pallas_call(
        pick_kernel,
        out_shape=[
            jax.ShapeDtypeStruct((CAP, width), jnp.bfloat16),
            jax.ShapeDtypeStruct((CAP, width), jnp.bfloat16),
            jax.ShapeDtypeStruct((tokens, 2 * CAP), jnp.float32),
        ],
        in_specs=[SMEM] + [VMEM] * 3,
        out_specs=[VMEM] * 3,
        compiler_params=params(16),
        cost_estimate=cost(4 * CAP * tokens * width, 4 * tokens * width),
        name="pick",
    )(core.reshape(1), routes[0], gate_weights[0], own_queries)
    routed = jnp.concatenate([keep, swap(send)], axis=0)
    routed_blocks, _ = gather(routed)

    pieces, places = [], []
    for block, k in zip(kv_blocks, order):
        pieces += [block, swap(block)]
        places += [2 * (seq ^ k) + core, 2 * (seq ^ k) + 1 - core]
    place = jnp.stack([p * rows_true for p in places] + [prompt_lengths[0]]).astype(jnp.int32)

    each = 2 * CAP
    done, attended = attend_call(
        place,
        routed_blocks[:-1] + [own_queries],
        pieces,
        [each * (len(order) - 1), tokens],
        rows_true,
    )
    parts = expert_call(
        place,
        done,
        routed_blocks[-1],
        pieces,
        norm_gain.reshape(1, width),
        w_gate[0],
        w_up[0],
        w_down[0],
        rows_true,
    )

    held = dict(zip(order, parts))
    strides = strides_of(len(order))[::-1]
    for stride in strides[:-1]:
        sent = {k: across(v, stride) for k, v in held.items() if k & stride}
        held = {
            k: (v.astype(jnp.float32) + sent[k ^ stride].astype(jnp.float32)).astype(jnp.bfloat16)
            for k, v in held.items()
            if not k & stride
        }
    mine, theirs = held[0], held[strides[-1]]
    terms = [
        mine[:CAP],
        across(theirs[:CAP], strides[-1]),
        swap(mine[CAP:]),
        across_and_swap(theirs[CAP:], strides[-1]),
    ]
    mixed = pl.pallas_call(
        functools.partial(combine_kernel, 2),
        out_shape=jax.ShapeDtypeStruct((tokens, width), jnp.bfloat16),
        in_specs=[VMEM] * 6,
        out_specs=VMEM,
        compiler_params=params(16),
        cost_estimate=cost(8 * CAP * tokens * width, 4 * tokens * width),
        name="combine",
    )(comb, attended, *terms)
    return mixed[None]


def solution(mesh):
    return jax.shard_map(
        body,
        mesh=mesh,
        in_specs=(
            P(("group", "exp"), ("seq", "tp"), None),
            P(("group", "exp"), ("seq", "tp"), None, None),
            P(("group", "exp")),
            P(("group", "exp"), ("seq", "tp"), None),
            P(("group", "exp"), ("seq", "tp"), None),
            P(),
            P("tp", None, "seq"),
            P("tp", None, "seq"),
            P("tp", "seq", None),
        ),
        out_specs=P(("group", "exp"), ("seq", "tp"), None),
        check_vma=False,
    )
```

```python
import functools
import math

import jax
import jax.numpy as jnp
from jax import lax
from jax.experimental import pallas as pl
from jax.experimental.pallas import tpu as pltpu
from jax.sharding import PartitionSpec as P

HEAD_DIM = 128
PROMPT = 256
CAP = 16
TILE = 16

epsilon = 1e-06
masked_score = -1e30
MIB = 1024 * 1024

VMEM = pl.BlockSpec(memory_space=pltpu.VMEM)
SMEM = pl.BlockSpec(memory_space=pltpu.SMEM)
ANY = pl.BlockSpec(memory_space=pl.ANY)


def params(mib):
    return pltpu.CompilerParams(vmem_limit_bytes=mib * MIB)


def cost(flops, moved, transcendentals=0):
    return pl.CostEstimate(
        flops=int(flops), bytes_accessed=int(moved), transcendentals=int(transcendentals)
    )


def pick_kernel(me_ref, routes_ref, gates_ref, q_ref, keep_ref, send_ref, comb_ref):
    top, tokens = routes_ref.shape
    me = me_ref[0]
    routes = routes_ref[...]
    gates = gates_ref[...]

    def of_expert(expert):
        hit = routes == expert
        member = jnp.sum(hit.astype(jnp.float32), axis=0, keepdims=True)
        weight = jnp.sum(jnp.where(hit, gates, 0.0), axis=0, keepdims=True)
        return member, weight

    member_a, weight_a = of_expert(me)
    member_b, weight_b = of_expert(1 - me)
    slot_of = lax.broadcasted_iota(jnp.int32, (2 * CAP, tokens), 0)
    mine = slot_of < CAP
    member = jnp.where(mine, member_a, member_b)
    weight = jnp.where(mine, weight_a, weight_b)
    row = lax.broadcasted_iota(jnp.int32, (tokens, tokens), 0)
    col = lax.broadcasted_iota(jnp.int32, (tokens, tokens), 1)
    before = jnp.where(row < col, 1.0, 0.0).astype(jnp.bfloat16)
    slot = jnp.dot(member.astype(jnp.bfloat16), before, preferred_element_type=jnp.float32)
    wanted = jnp.where(mine, slot_of, slot_of - CAP).astype(jnp.float32)
    taken = jnp.where((member > 0.0) & (slot == wanted), 1.0, 0.0)
    comb_ref[...] = taken * weight
    rows = jnp.dot(
        taken.astype(jnp.bfloat16), q_ref[...], preferred_element_type=jnp.float32
    ).astype(jnp.bfloat16)
    keep_ref[...] = rows[:CAP]
    send_ref[...] = rows[CAP:]


def key_bias(place_ref, pieces, rows_each, rows_true):
    length = place_ref[pieces]
    parts = []
    lane = lax.broadcasted_iota(jnp.int32, (8, rows_each), 1)
    for i in range(pieces):
        position = lane + place_ref[i]
        allowed = (position >= PROMPT) | (position < length)
        allowed = allowed & (lane < rows_true)
        parts.append(jnp.where(allowed, 0.0, masked_score))
    return jnp.concatenate(parts, axis=1)[:1]


def attend(queries, kv_refs, bias, store, per_key):
    width = kv_refs[0].shape[1] // 2
    heads = width // HEAD_DIM
    factor = math.log2(math.e) / math.sqrt(HEAD_DIM)

    def one(head, _):
        at = head * HEAD_DIM
        if not isinstance(head, int):
            at = pl.multiple_of(at, HEAD_DIM)
        keys = jnp.concatenate([r[:, pl.ds(at, HEAD_DIM)] for r in kv_refs], axis=0)
        values = jnp.concatenate(
            [r[:, pl.ds(width + at, HEAD_DIM)] for r in kv_refs], axis=0
        )
        values = jnp.concatenate([values, jnp.ones_like(values)], axis=1)
        block = queries(at * per_key, per_key * HEAD_DIM)
        rows = block.shape[0]
        stacked = jnp.concatenate(
            [block[:, j * HEAD_DIM : (j + 1) * HEAD_DIM] for j in range(per_key)], axis=0
        )
        scores = (
            lax.dot_general(
                stacked, keys, (((1,), (1,)), ((), ())), preferred_element_type=jnp.float32
            )
            * factor
            + bias
        )
        weights = jnp.exp2(scores - jnp.max(scores, axis=1, keepdims=True))
        summed = jnp.dot(
            weights.astype(jnp.bfloat16), values, preferred_element_type=jnp.float32
        )
        result = (summed[:, :HEAD_DIM] / summed[:, HEAD_DIM:]).astype(jnp.bfloat16)
        for j in range(per_key):
            store(at * per_key + j * HEAD_DIM, result[j * rows : (j + 1) * rows])

    if bias.shape[1] > 1024:
        lax.fori_loop(0, heads, one, None)
    else:
        for head in range(heads):
            one(head, None)


def norm(rows, gain):
    x = rows.astype(jnp.float32)
    square = jnp.mean(x * x, axis=1, keepdims=True)
    return (x * lax.rsqrt(square + epsilon) * gain).astype(jnp.bfloat16)


def attend_kernel(pieces, blocks, per_key, rows_true, place_ref, *refs):
    q_refs = refs[:blocks]
    kv_refs = refs[blocks : blocks + pieces]
    out_ref = refs[-1]
    bias = key_bias(place_ref, pieces, kv_refs[0].shape[0], rows_true)

    def queries(at, size):
        return jnp.concatenate([r[:, pl.ds(at, size)] for r in q_refs], axis=0)

    def store(at, result):
        out_ref[:, pl.ds(at, HEAD_DIM)] = result

    attend(queries, kv_refs, bias, store, per_key)
    if len(refs) > blocks + pieces + 1:
        out_ref[...] = norm(out_ref[...], refs[blocks + pieces][...])


def attend_call(place, q_blocks, kv_pieces, rows_true, *gain):
    width = q_blocks[0].shape[1]
    per_key = width // (kv_pieces[0].shape[1] // 2)
    rows = sum(q.shape[0] for q in q_blocks)
    keys = sum(p.shape[0] for p in kv_pieces)
    return pl.pallas_call(
        functools.partial(
            attend_kernel, len(kv_pieces), len(q_blocks), per_key, rows_true
        ),
        out_shape=jax.ShapeDtypeStruct((rows, width), jnp.bfloat16),
        in_specs=[SMEM] + [VMEM] * (len(q_blocks) + len(kv_pieces) + len(gain)),
        out_specs=VMEM,
        compiler_params=params(20 if rows * keys < 1 << 18 else 56),
        cost_estimate=cost(
            4 * rows * width * keys,
            4 * rows * width + 2 * keys * kv_pieces[0].shape[1],
            rows * keys * width // HEAD_DIM,
        ),
        name="attend",
    )(place, *q_blocks, *kv_pieces, *gain)


def split_of(k, width):
    half = width // 2
    return [(0, width)] if k < 2 else [(0, half), (half, width)]


def expert_kernel(
    pieces, order, per_key, rows_true, last_ref, place_ref, done_ref, *refs
):
    kv_refs = refs[:pieces]
    gain_ref, gate_hbm, up_hbm, down_hbm = refs[pieces : pieces + 4]
    out_refs = refs[pieces + 4 : -5]
    x_ref, gate_ref, up_ref, down_ref, sems = refs[-5:]
    copies = [
        pltpu.make_async_copy(src, dst, sems.at[i])
        for i, (src, dst) in enumerate(
            ((gate_hbm, gate_ref), (up_hbm, up_ref), (down_hbm, down_ref))
        )
    ]
    for c in copies:
        c.start()
    bias = key_bias(place_ref, pieces, kv_refs[0].shape[0], rows_true)

    def queries(at, size):
        return last_ref[:, pl.ds(at, size)]

    def store(at, result):
        x_ref[:, pl.ds(at, HEAD_DIM)] = result

    attend(queries, kv_refs, bias, store, per_key)
    normed = jnp.concatenate([done_ref[...], norm(x_ref[...], gain_ref[...])], axis=0)
    copies[0].wait()
    gate = jnp.dot(normed, gate_ref[...], preferred_element_type=jnp.float32)
    copies[1].wait()
    up = jnp.dot(normed, up_ref[...], preferred_element_type=jnp.float32)
    hidden = (gate / (1.0 + jnp.exp(-gate)) * up).astype(jnp.bfloat16)
    copies[2].wait()
    part = jnp.dot(hidden, down_ref[...], preferred_element_type=jnp.float32).astype(
        jnp.bfloat16
    )
    each, width = last_ref.shape
    out = iter(out_refs)
    for i, k in enumerate(order):
        for begin, end in split_of(k, width):
            next(out)[...] = part[i * each : (i + 1) * each, begin:end]


def expert_call(place, done, last, kv_pieces, gain, w_gate, w_up, w_down, order, rows_true):
    each, width = last.shape
    rows = len(order) * each
    hidden = w_gate.shape[1]
    per_key = width // (kv_pieces[0].shape[1] // 2)
    splits = [split_of(k, width) for k in order]
    shapes = [
        jax.ShapeDtypeStruct((each, end - begin), jnp.bfloat16)
        for split in splits
        for begin, end in split
    ]
    outs = iter(
        pl.pallas_call(
            functools.partial(expert_kernel, len(kv_pieces), tuple(order), per_key, rows_true),
            out_shape=shapes,
            in_specs=[VMEM, SMEM] + [VMEM] * (2 + len(kv_pieces)) + [ANY] * 3,
            out_specs=[VMEM] * len(shapes),
            scratch_shapes=[
                pltpu.VMEM((each, width), jnp.bfloat16),
                pltpu.VMEM(w_gate.shape, jnp.bfloat16),
                pltpu.VMEM(w_up.shape, jnp.bfloat16),
                pltpu.VMEM(w_down.shape, jnp.bfloat16),
                pltpu.SemaphoreType.DMA((3,)),
            ],
            compiler_params=params(48),
            cost_estimate=cost(6 * rows * width * hidden, 6 * width * hidden),
            name="experts",
        )(last, place, done, *kv_pieces, gain, w_gate, w_up, w_down)
    )
    return [[next(outs) for _ in split] for split in splits]


def add(*terms):
    total = terms[0].astype(jnp.float32)
    for t in terms[1:]:
        total = total + t.astype(jnp.float32)
    return total.astype(jnp.bfloat16)


def combine_kernel(
    late_ref, late_theirs_ref, comb_ref, attended_ref, mine_ref, theirs_ref, out_ref
):
    width = out_ref.shape[1]
    half = width - late_ref.shape[1]
    comb = comb_ref[...]
    high = comb.astype(jnp.bfloat16)
    low = (comb - high.astype(jnp.float32)).astype(jnp.bfloat16)
    both = (((0,), (0,)), ((), ()))

    def finish(rows, begin, end):
        rows = jnp.concatenate(rows, axis=0)
        added = lax.dot_general(
            high, rows, both, preferred_element_type=jnp.float32
        ) + lax.dot_general(low, rows, both, preferred_element_type=jnp.float32)
        out_ref[:, begin:end] = (
            attended_ref[:, begin:end].astype(jnp.float32) + added
        ).astype(jnp.bfloat16)

    finish([mine_ref[:, :half], theirs_ref[:, :half]], 0, half)
    finish(
        [
            add(mine_ref[:, half:], late_ref[...]),
            add(theirs_ref[:, half:], late_theirs_ref[...]),
        ],
        half,
        width,
    )


def across(x, stride):
    n = lax.axis_size("seq")
    return lax.ppermute(x, "seq", [(i, i ^ stride) for i in range(n)])


def swap(x):
    return lax.ppermute(x, "tp", [(0, 1), (1, 0)])


def across_and_swap(x, stride):
    n = lax.axis_size("seq")
    pairs = [
        (2 * i + c, 2 * (i ^ stride) + 1 - c) for i in range(n) for c in range(2)
    ]
    return lax.ppermute(x, ("seq", "tp"), pairs)


def tied(*values):
    return lax.optimization_barrier(values)


def body(
    queries, keys_values, prompt_lengths, routes, gate_weights, norm_gain, w_gate, w_up, w_down
):
    tokens, width = queries.shape[1:]
    rows_true = keys_values.shape[1]
    pad = -rows_true % TILE
    seq, core = lax.axis_index("seq"), lax.axis_index("tp")
    own_queries = queries[0]
    strides = [1 << b for b in reversed(range(lax.axis_size("seq").bit_length() - 1))]

    kv = keys_values[0].reshape(rows_true, -1)
    if pad:
        kv = jnp.pad(kv, ((0, pad), (0, 0)))
    keep, send, comb = pl.pallas_call(
        pick_kernel,
        out_shape=[
            jax.ShapeDtypeStruct((CAP, width), jnp.bfloat16),
            jax.ShapeDtypeStruct((CAP, width), jnp.bfloat16),
            jax.ShapeDtypeStruct((2 * CAP, tokens), jnp.float32),
        ],
        in_specs=[SMEM] + [VMEM] * 3,
        out_specs=[VMEM] * 3,
        compiler_params=params(16),
        cost_estimate=cost(4 * CAP * tokens * width, 4 * tokens * width),
        name="pick",
    )(core.reshape(1), routes[0].T, gate_weights[0].T, own_queries)
    routed = jnp.concatenate([keep, swap(send)], axis=0)

    kv_blocks, routed_blocks, order = [kv], [routed], [0]
    for stride in strides[:-1]:
        kv_blocks = kv_blocks + [across(b, stride) for b in kv_blocks]
        routed_blocks = routed_blocks + [across(b, stride) for b in routed_blocks]
        order = order + [k ^ stride for k in order]
    first_kv, first_routed = across(kv, strides[-1]), across(routed, strides[-1])
    kv_blocks, routed_blocks, first_kv, first_routed = tied(
        kv_blocks, routed_blocks, first_kv, first_routed
    )
    kv_blocks = kv_blocks + [first_kv] + [across(b, strides[-1]) for b in kv_blocks[1:]]
    routed_blocks = (
        routed_blocks + [first_routed] + [across(b, strides[-1]) for b in routed_blocks[1:]]
    )
    order = order + [k ^ strides[-1] for k in order]

    pieces, places = [], []
    for block, k in zip([kv] + kv_blocks[1:], order):
        pieces += [block, swap(block)]
        places += [2 * (seq ^ k) + core, 2 * (seq ^ k) + 1 - core]
    place = jnp.stack([p * rows_true for p in places] + [prompt_lengths[0]]).astype(jnp.int32)

    gain = norm_gain.reshape(1, width)
    done = attend_call(place, routed_blocks[:-1], pieces, rows_true, gain)
    parts = expert_call(
        place, done, routed_blocks[-1], pieces, gain, w_gate[0], w_up[0], w_down[0], order, rows_true
    )

    own_queries, parts = tied(own_queries, parts)
    attended = attend_call(place, [own_queries], pieces, rows_true)
    parts = dict(zip(order, parts))
    straight = {k: v[0] for k, v in parts.items()}
    half = width // 2
    held = {k: v[-1][:, -half:] for k, v in parts.items()}
    for stride in strides[::-1][:-1]:
        sent = {k: across(v, stride) for k, v in held.items() if k & stride and k != 1}
        held = {
            k: add(v, sent[k ^ stride]) if k ^ stride in sent else v
            for k, v in held.items()
            if not k & stride
        }
    late, attended = tied(held[strides[0]], attended)
    late_mine = across(late[:CAP], strides[0])
    late_theirs = across_and_swap(late[CAP:], strides[0])
    arrived = [across(v, k) for k, v in straight.items() if k]
    arrived, late = tied(arrived, late)
    so_far = [
        jnp.concatenate(
            [
                add(straight[0][rows, :half], *[a[rows, :half] for a in arrived]),
                add(
                    held[0][rows],
                    *[a[rows, half:] for a in arrived if a.shape[1] == width],
                ),
            ],
            axis=1,
        )
        for rows in (slice(None, CAP), slice(CAP, None))
    ]
    theirs = swap(so_far[1])
    mixed = pl.pallas_call(
        combine_kernel,
        out_shape=jax.ShapeDtypeStruct((tokens, width), jnp.bfloat16),
        in_specs=[VMEM] * 6,
        out_specs=VMEM,
        compiler_params=params(16),
        cost_estimate=cost(8 * CAP * tokens * width, 4 * tokens * width),
        name="combine",
    )(late_mine, late_theirs, comb, attended, so_far[0], theirs)
    return mixed[None]


def solution(mesh):
    return jax.shard_map(
        body,
        mesh=mesh,
        in_specs=(
            P(("group", "exp"), ("seq", "tp"), None),
            P(("group", "exp"), ("seq", "tp"), None, None),
            P(("group", "exp")),
            P(("group", "exp"), ("seq", "tp"), None),
            P(("group", "exp"), ("seq", "tp"), None),
            P(),
            P("tp", None, "seq"),
            P("tp", None, "seq"),
            P("tp", "seq", None),
        ),
        out_specs=P(("group", "exp"), ("seq", "tp"), None),
        check_vma=False,
    )
```

```python
import functools
import math

import jax
import jax.numpy as jnp
from jax import lax
from jax.experimental import pallas as pl
from jax.experimental.pallas import tpu as pltpu
from jax.sharding import PartitionSpec as P

HEAD_DIM = 128
PROMPT = 256
CAP = 16
TILE = 16

epsilon = 1e-06
masked_score = -1e30
MIB = 1024 * 1024

VMEM = pl.BlockSpec(memory_space=pltpu.VMEM)
SMEM = pl.BlockSpec(memory_space=pltpu.SMEM)
ANY = pl.BlockSpec(memory_space=pl.ANY)


def params(mib):
    return pltpu.CompilerParams(vmem_limit_bytes=mib * MIB)


def cost(flops, moved, transcendentals=0):
    return pl.CostEstimate(
        flops=int(flops), bytes_accessed=int(moved), transcendentals=int(transcendentals)
    )


def pick_kernel(me_ref, routes_ref, gates_ref, q_ref, keep_ref, send_ref, comb_ref):
    top, tokens = routes_ref.shape
    me = me_ref[0]
    routes = routes_ref[...]
    gates = gates_ref[...]

    def of_expert(expert):
        hit = routes == expert
        member = jnp.sum(hit.astype(jnp.float32), axis=0, keepdims=True)
        weight = jnp.sum(jnp.where(hit, gates, 0.0), axis=0, keepdims=True)
        return member, weight

    member_a, weight_a = of_expert(me)
    member_b, weight_b = of_expert(1 - me)
    slot_of = lax.broadcasted_iota(jnp.int32, (2 * CAP, tokens), 0)
    mine = slot_of < CAP
    member = jnp.where(mine, member_a, member_b)
    weight = jnp.where(mine, weight_a, weight_b)
    row = lax.broadcasted_iota(jnp.int32, (tokens, tokens), 0)
    col = lax.broadcasted_iota(jnp.int32, (tokens, tokens), 1)
    before = jnp.where(row < col, 1.0, 0.0).astype(jnp.bfloat16)
    slot = jnp.dot(member.astype(jnp.bfloat16), before, preferred_element_type=jnp.float32)
    wanted = jnp.where(mine, slot_of, slot_of - CAP).astype(jnp.float32)
    taken = jnp.where((member > 0.0) & (slot == wanted), 1.0, 0.0)
    comb_ref[...] = taken * weight
    rows = jnp.dot(
        taken.astype(jnp.bfloat16), q_ref[...], preferred_element_type=jnp.float32
    ).astype(jnp.bfloat16)
    keep_ref[...] = rows[:CAP]
    send_ref[...] = rows[CAP:]


def key_bias(place_ref, pieces, rows_each, rows_true):
    length = place_ref[pieces]
    parts = []
    lane = lax.broadcasted_iota(jnp.int32, (8, rows_each), 1)
    for i in range(pieces):
        position = lane + place_ref[i]
        allowed = (position >= PROMPT) | (position < length)
        allowed = allowed & (lane < rows_true)
        parts.append(jnp.where(allowed, 0.0, masked_score))
    return jnp.concatenate(parts, axis=1)[:1]


def attend(queries, kv_refs, bias, store, per_key):
    width = kv_refs[0].shape[1] // 2
    heads = width // HEAD_DIM
    factor = math.log2(math.e) / math.sqrt(HEAD_DIM)

    def one(head, _):
        at = head * HEAD_DIM
        if not isinstance(head, int):
            at = pl.multiple_of(at, HEAD_DIM)
        keys = jnp.concatenate([r[:, pl.ds(at, HEAD_DIM)] for r in kv_refs], axis=0)
        values = jnp.concatenate(
            [r[:, pl.ds(width + at, HEAD_DIM)] for r in kv_refs], axis=0
        )
        values = jnp.concatenate([values, jnp.ones_like(values)], axis=1)
        block = queries(at * per_key, per_key * HEAD_DIM)
        rows = block.shape[0]
        stacked = jnp.concatenate(
            [block[:, j * HEAD_DIM : (j + 1) * HEAD_DIM] for j in range(per_key)], axis=0
        )
        scores = (
            lax.dot_general(
                stacked, keys, (((1,), (1,)), ((), ())), preferred_element_type=jnp.float32
            )
            * factor
            + bias
        )
        weights = jnp.exp2(scores - jnp.max(scores, axis=1, keepdims=True))
        summed = jnp.dot(
            weights.astype(jnp.bfloat16), values, preferred_element_type=jnp.float32
        )
        result = (summed[:, :HEAD_DIM] / summed[:, HEAD_DIM:]).astype(jnp.bfloat16)
        for j in range(per_key):
            store(at * per_key + j * HEAD_DIM, result[j * rows : (j + 1) * rows])

    if bias.shape[1] > 1024:
        lax.fori_loop(0, heads, one, None)
    else:
        for head in range(heads):
            one(head, None)


def norm(rows, gain):
    x = rows.astype(jnp.float32)
    square = jnp.mean(x * x, axis=1, keepdims=True)
    return (x * lax.rsqrt(square + epsilon) * gain).astype(jnp.bfloat16)


def attend_kernel(pieces, blocks, per_key, rows_true, place_ref, *refs):
    q_refs = refs[:blocks]
    kv_refs = refs[blocks : blocks + pieces]
    out_ref = refs[-1]
    bias = key_bias(place_ref, pieces, kv_refs[0].shape[0], rows_true)

    def queries(at, size):
        return jnp.concatenate([r[:, pl.ds(at, size)] for r in q_refs], axis=0)

    def store(at, result):
        out_ref[:, pl.ds(at, HEAD_DIM)] = result

    attend(queries, kv_refs, bias, store, per_key)
    if len(refs) > blocks + pieces + 1:
        out_ref[...] = norm(out_ref[...], refs[blocks + pieces][...])


def attend_call(place, q_blocks, kv_pieces, rows_true, *gain):
    width = q_blocks[0].shape[1]
    per_key = width // (kv_pieces[0].shape[1] // 2)
    rows = sum(q.shape[0] for q in q_blocks)
    keys = sum(p.shape[0] for p in kv_pieces)
    return pl.pallas_call(
        functools.partial(
            attend_kernel, len(kv_pieces), len(q_blocks), per_key, rows_true
        ),
        out_shape=jax.ShapeDtypeStruct((rows, width), jnp.bfloat16),
        in_specs=[SMEM] + [VMEM] * (len(q_blocks) + len(kv_pieces) + len(gain)),
        out_specs=VMEM,
        compiler_params=params(20 if rows * keys < 1 << 18 else 56),
        cost_estimate=cost(1, 1),
        name="attend",
    )(place, *q_blocks, *kv_pieces, *gain)


def cut_of(width):
    return width * 3 // 8 // HEAD_DIM * HEAD_DIM


def split_of(k, width):
    return [(0, width)] if k < 2 else [(0, cut_of(width)), (cut_of(width), width)]


def start_copies(pairs, sems):
    copies = [pltpu.make_async_copy(s, d, sems.at[i]) for i, (s, d) in enumerate(pairs)]
    for c in copies:
        c.start()
    return copies


def gated(normed, gate_copy, gate_ref, up_copy, up_ref):
    gate_copy.wait()
    gate = jnp.dot(normed, gate_ref[...], preferred_element_type=jnp.float32)
    up_copy.wait()
    up = jnp.dot(normed, up_ref[...], preferred_element_type=jnp.float32)
    return (gate / (1.0 + jnp.exp(-gate)) * up).astype(jnp.bfloat16)


def attend_block(place_ref, block_ref, kv_refs, gain_ref, x_ref, per_key, rows_true):
    bias = key_bias(place_ref, len(kv_refs), kv_refs[0].shape[0], rows_true)

    def queries(at, size):
        return block_ref[:, pl.ds(at, size)]

    def store(at, result):
        x_ref[:, pl.ds(at, HEAD_DIM)] = result

    attend(queries, kv_refs, bias, store, per_key)
    return norm(x_ref[...], gain_ref[...])


def hidden_kernel(pieces, per_key, rows_true, block_ref, place_ref, done_ref, *refs):
    kv_refs = refs[:pieces]
    gain_ref, gate_hbm, up_hbm, out_ref, x_ref, gate_ref, up_ref, sems = refs[pieces:]
    copies = start_copies(((gate_hbm, gate_ref), (up_hbm, up_ref)), sems)
    last = attend_block(place_ref, block_ref, kv_refs, gain_ref, x_ref, per_key, rows_true)
    normed = jnp.concatenate([done_ref[...], last], axis=0)
    out_ref[...] = gated(normed, copies[0], gate_ref, copies[1], up_ref)


def expert_kernel(pieces, order, per_key, rows_true, block_ref, place_ref, done_ref, *refs):
    kv_refs = refs[:pieces]
    gain_ref, gate_hbm, up_hbm, down_hbm = refs[pieces : pieces + 4]
    out_refs = refs[pieces + 4 : -5]
    x_ref, gate_ref, up_ref, down_ref, sems = refs[-5:]
    copies = start_copies(
        ((gate_hbm, gate_ref), (up_hbm, up_ref), (down_hbm, down_ref)), sems
    )
    last = attend_block(place_ref, block_ref, kv_refs, gain_ref, x_ref, per_key, rows_true)
    hidden = jnp.concatenate(
        [done_ref[...], gated(last, copies[0], gate_ref, copies[1], up_ref)], axis=0
    )
    copies[2].wait()
    part = jnp.dot(hidden, down_ref[...], preferred_element_type=jnp.float32).astype(
        jnp.bfloat16
    )
    each, width = block_ref.shape
    out = iter(out_refs)
    for i, k in enumerate(order):
        for begin, end in split_of(k, width):
            next(out)[...] = part[i * each : (i + 1) * each, begin:end]


def hidden_call(place, done, block, kv_pieces, gain, w_gate, w_up, rows_true):
    each, width = block.shape
    rows, hidden = done.shape[0] + each, w_gate.shape[1]
    per_key = width // (kv_pieces[0].shape[1] // 2)
    return pl.pallas_call(
        functools.partial(hidden_kernel, len(kv_pieces), per_key, rows_true),
        out_shape=jax.ShapeDtypeStruct((rows, hidden), jnp.bfloat16),
        in_specs=[VMEM, SMEM] + [VMEM] * (2 + len(kv_pieces)) + [ANY] * 2,
        out_specs=VMEM,
        scratch_shapes=[
            pltpu.VMEM((each, width), jnp.bfloat16),
            pltpu.VMEM(w_gate.shape, jnp.bfloat16),
            pltpu.VMEM(w_up.shape, jnp.bfloat16),
            pltpu.SemaphoreType.DMA((2,)),
        ],
        compiler_params=params(44),
        cost_estimate=cost(1, 1),
        name="hidden",
    )(block, place, done, *kv_pieces, gain, w_gate, w_up)


def expert_call(place, done, block, kv_pieces, gain, w_gate, w_up, w_down, order, rows_true):
    each, width = block.shape
    rows = len(order) * each
    hidden = w_gate.shape[1]
    per_key = width // (kv_pieces[0].shape[1] // 2)
    splits = [split_of(k, width) for k in order]
    shapes = [
        jax.ShapeDtypeStruct((each, end - begin), jnp.bfloat16)
        for split in splits
        for begin, end in split
    ]
    outs = iter(
        pl.pallas_call(
            functools.partial(expert_kernel, len(kv_pieces), tuple(order), per_key, rows_true),
            out_shape=shapes,
            in_specs=[VMEM, SMEM] + [VMEM] * (2 + len(kv_pieces)) + [ANY] * 3,
            out_specs=[VMEM] * len(shapes),
            scratch_shapes=[
                pltpu.VMEM((each, width), jnp.bfloat16),
                pltpu.VMEM(w_gate.shape, jnp.bfloat16),
                pltpu.VMEM(w_up.shape, jnp.bfloat16),
                pltpu.VMEM(w_down.shape, jnp.bfloat16),
                pltpu.SemaphoreType.DMA((3,)),
            ],
            compiler_params=params(48),
            cost_estimate=cost(6 * rows * width * hidden, 6 * width * hidden),
            name="experts",
        )(block, place, done, *kv_pieces, gain, w_gate, w_up, w_down)
    )
    return [[next(outs) for _ in split] for split in splits]


def add(*terms):
    total = terms[0].astype(jnp.float32)
    for t in terms[1:]:
        total = total + t.astype(jnp.float32)
    return total.astype(jnp.bfloat16)


def combine_kernel(
    late_ref, late_theirs_ref, comb_ref, attended_ref, mine_ref, theirs_ref, out_ref
):
    width = out_ref.shape[1]
    half = width - late_ref.shape[1]
    comb = comb_ref[...]
    high = comb.astype(jnp.bfloat16)
    low = (comb - high.astype(jnp.float32)).astype(jnp.bfloat16)
    both = (((0,), (0,)), ((), ()))

    def finish(rows, begin, end):
        rows = jnp.concatenate(rows, axis=0)
        added = lax.dot_general(
            high, rows, both, preferred_element_type=jnp.float32
        ) + lax.dot_general(low, rows, both, preferred_element_type=jnp.float32)
        out_ref[:, begin:end] = (
            attended_ref[:, begin:end].astype(jnp.float32) + added
        ).astype(jnp.bfloat16)

    finish([mine_ref[:, :half], theirs_ref[:, :half]], 0, half)
    finish(
        [
            add(mine_ref[:, half:], late_ref[...]),
            add(theirs_ref[:, half:], late_theirs_ref[...]),
        ],
        half,
        width,
    )


def across(x, stride):
    n = lax.axis_size("seq")
    return lax.ppermute(x, "seq", [(i, i ^ stride) for i in range(n)])


def swap(x):
    return lax.ppermute(x, "tp", [(0, 1), (1, 0)])


def across_and_swap(x, stride):
    n = lax.axis_size("seq")
    pairs = [
        (2 * i + c, 2 * (i ^ stride) + 1 - c) for i in range(n) for c in range(2)
    ]
    return lax.ppermute(x, ("seq", "tp"), pairs)


def tied(*values):
    return lax.optimization_barrier(values)


def body(
    queries, keys_values, prompt_lengths, routes, gate_weights, norm_gain, w_gate, w_up, w_down
):
    tokens, width = queries.shape[1:]
    rows_true = keys_values.shape[1]
    pad = -rows_true % TILE
    seq, core = lax.axis_index("seq"), lax.axis_index("tp")
    own_queries = queries[0]
    strides = [1 << b for b in reversed(range(lax.axis_size("seq").bit_length() - 1))]

    kv = keys_values[0].reshape(rows_true, -1)
    if pad:
        kv = jnp.pad(kv, ((0, pad), (0, 0)))
    keep, send, comb = pl.pallas_call(
        pick_kernel,
        out_shape=[
            jax.ShapeDtypeStruct((CAP, width), jnp.bfloat16),
            jax.ShapeDtypeStruct((CAP, width), jnp.bfloat16),
            jax.ShapeDtypeStruct((2 * CAP, tokens), jnp.float32),
        ],
        in_specs=[SMEM] + [VMEM] * 3,
        out_specs=[VMEM] * 3,
        compiler_params=params(16),
        cost_estimate=cost(4 * CAP * tokens * width, 4 * tokens * width),
        name="pick",
    )(core.reshape(1), routes[0].T, gate_weights[0].T, own_queries)
    came = swap(send)

    kv_blocks, order = [kv], [0]
    for stride in strides[:-1]:
        kv_blocks = kv_blocks + [across(b, stride) for b in kv_blocks]
        order = order + [k ^ stride for k in order]
    first_kv, own_swapped = across(kv, strides[-1]), swap(kv)
    kv_blocks, first_kv, own_swapped, came = tied(kv_blocks, first_kv, own_swapped, came)
    kv_blocks = kv_blocks + [first_kv] + [across(b, strides[-1]) for b in kv_blocks[1:]]
    order = order + [k ^ strides[-1] for k in order]
    routed_blocks = [jnp.concatenate([keep, came], axis=0)]
    for stride in strides:
        routed_blocks = routed_blocks + [across(b, stride) for b in routed_blocks]

    pieces, places = [], []
    for block, k in zip(kv_blocks, order):
        pieces += [block, swap(block) if k else own_swapped]
        places += [2 * (seq ^ k) + core, 2 * (seq ^ k) + 1 - core]
    place = jnp.stack([p * rows_true for p in places] + [prompt_lengths[0]]).astype(jnp.int32)

    gain = norm_gain.reshape(1, width)
    weights = w_gate[0], w_up[0]
    done = attend_call(place, routed_blocks[:-2], pieces, rows_true, gain)
    done = hidden_call(place, done, routed_blocks[-2], pieces, gain, *weights, rows_true)
    parts = expert_call(
        place, done, routed_blocks[-1], pieces, gain, *weights, w_down[0], order, rows_true
    )

    parts = dict(zip(order, parts))
    straight = {k: v[0] for k, v in parts.items()}
    cut = cut_of(width)
    held = {k: v[-1][:, cut - width :] for k, v in parts.items()}
    for stride in strides[::-1][:-1]:
        sent = {k: across(v, stride) for k, v in held.items() if k & stride and k != 1}
        held = {
            k: add(v, sent[k ^ stride]) if k ^ stride in sent else v
            for k, v in held.items()
            if not k & stride
        }
    late, own_queries = tied(held[strides[0]], own_queries)
    attended = attend_call(place, [own_queries], pieces, rows_true)
    late_mine = across(late[:CAP], strides[0])
    late_theirs = across_and_swap(late[CAP:], strides[0])
    arrived = [across(v, k) for k, v in straight.items() if k]
    arrived, late = tied(arrived, late)
    so_far = [
        jnp.concatenate(
            [
                add(straight[0][rows, :cut], *[a[rows, :cut] for a in arrived]),
                add(
                    held[0][rows],
                    *[a[rows, cut:] for a in arrived if a.shape[1] == width],
                ),
            ],
            axis=1,
        )
        for rows in (slice(None, CAP), slice(CAP, None))
    ]
    theirs = swap(so_far[1])
    mixed = pl.pallas_call(
        combine_kernel,
        out_shape=jax.ShapeDtypeStruct((tokens, width), jnp.bfloat16),
        in_specs=[VMEM] * 6,
        out_specs=VMEM,
        compiler_params=params(16),
        cost_estimate=cost(8 * CAP * tokens * width, 4 * tokens * width),
        name="combine",
    )(late_mine, late_theirs, comb, attended, so_far[0], theirs)
    return mixed[None]


def solution(mesh):
    return jax.shard_map(
        body,
        mesh=mesh,
        in_specs=(
            P(("group", "exp"), ("seq", "tp"), None),
            P(("group", "exp"), ("seq", "tp"), None, None),
            P(("group", "exp")),
            P(("group", "exp"), ("seq", "tp"), None),
            P(("group", "exp"), ("seq", "tp"), None),
            P(),
            P("tp", None, "seq"),
            P("tp", None, "seq"),
            P("tp", "seq", None),
        ),
        out_specs=P(("group", "exp"), ("seq", "tp"), None),
        check_vma=False,
    )
```

```python
import functools
import math

import jax
import jax.numpy as jnp
from jax import lax
from jax.experimental import pallas as pl
from jax.experimental.pallas import tpu as pltpu
from jax.sharding import PartitionSpec as P

HEAD_DIM = 128
PROMPT = 256
CAP = 16
TILE = 16

epsilon = 1e-06
masked_score = -1e30
MIB = 1024 * 1024

VMEM = pl.BlockSpec(memory_space=pltpu.VMEM)
SMEM = pl.BlockSpec(memory_space=pltpu.SMEM)
HBM = pl.BlockSpec(memory_space=pltpu.HBM)


def params(mib):
    return pltpu.CompilerParams(vmem_limit_bytes=mib * MIB)


def cost(flops, moved, transcendentals=0):
    return pl.CostEstimate(
        flops=int(flops), bytes_accessed=int(moved), transcendentals=int(transcendentals)
    )


def pick_kernel(me_ref, routes_ref, gates_ref, q_ref, keep_ref, send_ref, comb_ref):
    top, tokens = routes_ref.shape
    me = me_ref[0]
    routes = routes_ref[...]
    gates = gates_ref[...]

    def of_expert(expert):
        hit = routes == expert
        member = jnp.sum(hit.astype(jnp.float32), axis=0, keepdims=True)
        weight = jnp.sum(jnp.where(hit, gates, 0.0), axis=0, keepdims=True)
        return member, weight

    member_a, weight_a = of_expert(me)
    member_b, weight_b = of_expert(1 - me)
    slot_of = lax.broadcasted_iota(jnp.int32, (2 * CAP, tokens), 0)
    mine = slot_of < CAP
    member = jnp.where(mine, member_a, member_b)
    weight = jnp.where(mine, weight_a, weight_b)
    row = lax.broadcasted_iota(jnp.int32, (tokens, tokens), 0)
    col = lax.broadcasted_iota(jnp.int32, (tokens, tokens), 1)
    before = jnp.where(row < col, 1.0, 0.0).astype(jnp.bfloat16)
    slot = jnp.dot(member.astype(jnp.bfloat16), before, preferred_element_type=jnp.float32)
    wanted = jnp.where(mine, slot_of, slot_of - CAP).astype(jnp.float32)
    taken = jnp.where((member > 0.0) & (slot == wanted), 1.0, 0.0)
    comb_ref[...] = taken * weight
    rows = jnp.dot(
        taken.astype(jnp.bfloat16), q_ref[...], preferred_element_type=jnp.float32
    ).astype(jnp.bfloat16)
    keep_ref[...] = rows[:CAP]
    send_ref[...] = rows[CAP:]


def key_bias(place_ref, pieces, rows_each, rows_true):
    length = place_ref[pieces]
    parts = []
    lane = lax.broadcasted_iota(jnp.int32, (8, rows_each), 1)
    for i in range(pieces):
        position = lane + place_ref[i]
        allowed = (position >= PROMPT) | (position < length)
        allowed = allowed & (lane < rows_true)
        parts.append(jnp.where(allowed, 0.0, masked_score))
    return jnp.concatenate(parts, axis=1)[:1]


def attend(queries, kv_refs, bias, store, per_key):
    width = kv_refs[0].shape[1] // 2
    heads = width // HEAD_DIM
    factor = math.log2(math.e) / math.sqrt(HEAD_DIM)

    def one(head, _):
        at = head * HEAD_DIM
        if not isinstance(head, int):
            at = pl.multiple_of(at, HEAD_DIM)
        keys = jnp.concatenate([r[:, pl.ds(at, HEAD_DIM)] for r in kv_refs], axis=0)
        values = jnp.concatenate(
            [r[:, pl.ds(width + at, HEAD_DIM)] for r in kv_refs], axis=0
        )
        values = jnp.concatenate([values, jnp.ones_like(values)], axis=1)
        block = queries(at * per_key, per_key * HEAD_DIM)
        rows = block.shape[0]
        stacked = jnp.concatenate(
            [block[:, j * HEAD_DIM : (j + 1) * HEAD_DIM] for j in range(per_key)], axis=0
        )
        scores = (
            lax.dot_general(
                stacked, keys, (((1,), (1,)), ((), ())), preferred_element_type=jnp.float32
            )
            * factor
            + bias
        )
        weights = jnp.exp2(scores - jnp.max(scores, axis=1, keepdims=True))
        summed = jnp.dot(
            weights.astype(jnp.bfloat16), values, preferred_element_type=jnp.float32
        )
        result = (summed[:, :HEAD_DIM] / summed[:, HEAD_DIM:]).astype(jnp.bfloat16)
        for j in range(per_key):
            store(at * per_key + j * HEAD_DIM, result[j * rows : (j + 1) * rows])

    if bias.shape[1] > 1024:
        lax.fori_loop(0, heads, one, None)
    else:
        for head in range(heads):
            one(head, None)


def norm(rows, gain):
    x = rows.astype(jnp.float32)
    square = jnp.mean(x * x, axis=1, keepdims=True)
    return (x * lax.rsqrt(square + epsilon) * gain).astype(jnp.bfloat16)


def attend_kernel(pieces, blocks, per_key, rows_true, place_ref, *refs):
    q_refs = refs[:blocks]
    kv_refs = refs[blocks : blocks + pieces]
    out_ref = refs[-1]
    bias = key_bias(place_ref, pieces, kv_refs[0].shape[0], rows_true)

    def queries(at, size):
        return jnp.concatenate([r[:, pl.ds(at, size)] for r in q_refs], axis=0)

    def store(at, result):
        out_ref[:, pl.ds(at, HEAD_DIM)] = result

    attend(queries, kv_refs, bias, store, per_key)
    if len(refs) > blocks + pieces + 1:
        out_ref[...] = norm(out_ref[...], refs[blocks + pieces][...])


def attend_call(place, q_blocks, kv_pieces, rows_true, *gain):
    width = q_blocks[0].shape[1]
    per_key = width // (kv_pieces[0].shape[1] // 2)
    rows = sum(q.shape[0] for q in q_blocks)
    keys = sum(p.shape[0] for p in kv_pieces)
    return pl.pallas_call(
        functools.partial(
            attend_kernel, len(kv_pieces), len(q_blocks), per_key, rows_true
        ),
        out_shape=jax.ShapeDtypeStruct((rows, width), jnp.bfloat16),
        in_specs=[SMEM] + [VMEM] * (len(q_blocks) + len(kv_pieces) + len(gain)),
        out_specs=VMEM,
        compiler_params=params(20 if rows * keys < 1 << 18 else 56),
        cost_estimate=cost(
            4 * rows * width * keys,
            4 * rows * width + 2 * keys * kv_pieces[0].shape[1],
            rows * keys * width // HEAD_DIM,
        ),
        name="attend",
    )(place, *q_blocks, *kv_pieces, *gain)


def cut_of(width):
    return width * 3 // 8 // HEAD_DIM * HEAD_DIM


def split_of(k, width):
    return [(0, width)] if k < 2 else [(0, cut_of(width)), (cut_of(width), width)]


def expert_kernel(
    pieces, order, per_key, rows_true, last_ref, place_ref, done_ref, *refs
):
    kv_refs = refs[:pieces]
    gain_ref, gate_ref, up_hbm, down_hbm = refs[pieces : pieces + 4]
    out_refs = refs[pieces + 4 : -4]
    x_ref, up_ref, down_ref, sems = refs[-4:]
    copies = [
        pltpu.make_async_copy(src, dst, sems.at[i])
        for i, (src, dst) in enumerate(
            ((up_hbm, up_ref), (down_hbm, down_ref))
        )
    ]
    for c in copies:
        c.start()
    bias = key_bias(place_ref, pieces, kv_refs[0].shape[0], rows_true)

    def queries(at, size):
        return last_ref[:, pl.ds(at, size)]

    def store(at, result):
        x_ref[:, pl.ds(at, HEAD_DIM)] = result

    attend(queries, kv_refs, bias, store, per_key)
    normed = jnp.concatenate([done_ref[...], norm(x_ref[...], gain_ref[...])], axis=0)
    gate = jnp.dot(normed, gate_ref[...], preferred_element_type=jnp.float32)
    copies[0].wait()
    up = jnp.dot(normed, up_ref[...], preferred_element_type=jnp.float32)
    hidden = (gate / (1.0 + jnp.exp(-gate)) * up).astype(jnp.bfloat16)
    copies[1].wait()
    part = jnp.dot(hidden, down_ref[...], preferred_element_type=jnp.float32).astype(
        jnp.bfloat16
    )
    each, width = last_ref.shape
    out = iter(out_refs)
    for i, k in enumerate(order):
        for begin, end in split_of(k, width):
            next(out)[...] = part[i * each : (i + 1) * each, begin:end]


def expert_call(place, done, last, kv_pieces, gain, w_gate, w_up, w_down, order, rows_true):
    each, width = last.shape
    rows = len(order) * each
    hidden = w_gate.shape[1]
    per_key = width // (kv_pieces[0].shape[1] // 2)
    splits = [split_of(k, width) for k in order]
    shapes = [
        jax.ShapeDtypeStruct((each, end - begin), jnp.bfloat16)
        for split in splits
        for begin, end in split
    ]
    outs = iter(
        pl.pallas_call(
            functools.partial(expert_kernel, len(kv_pieces), tuple(order), per_key, rows_true),
            out_shape=shapes,
            in_specs=[VMEM, SMEM] + [VMEM] * (3 + len(kv_pieces)) + [HBM] * 2,
            out_specs=[VMEM] * len(shapes),
            scratch_shapes=[
                pltpu.VMEM((each, width), jnp.bfloat16),
                pltpu.VMEM(w_up.shape, jnp.bfloat16),
                pltpu.VMEM(w_down.shape, jnp.bfloat16),
                pltpu.SemaphoreType.DMA((2,)),
            ],
            compiler_params=params(26 if rows * hidden < 1 << 17 else 44),
            cost_estimate=cost(6 * rows * width * hidden, 6 * width * hidden),
            name="experts",
        )(last, place, done, *kv_pieces, gain, w_gate, w_up, w_down)
    )
    return [[next(outs) for _ in split] for split in splits]


def add(*terms):
    total = terms[0].astype(jnp.float32)
    for t in terms[1:]:
        total = total + t.astype(jnp.float32)
    return total.astype(jnp.bfloat16)


def combine_kernel(
    late_ref, late_theirs_ref, comb_ref, attended_ref, mine_ref, theirs_ref, out_ref
):
    width = out_ref.shape[1]
    half = width - late_ref.shape[1]
    comb = comb_ref[...]
    high = comb.astype(jnp.bfloat16)
    low = (comb - high.astype(jnp.float32)).astype(jnp.bfloat16)
    both = (((0,), (0,)), ((), ()))

    def finish(rows, begin, end):
        rows = jnp.concatenate(rows, axis=0)
        added = lax.dot_general(
            high, rows, both, preferred_element_type=jnp.float32
        ) + lax.dot_general(low, rows, both, preferred_element_type=jnp.float32)
        out_ref[:, begin:end] = (
            attended_ref[:, begin:end].astype(jnp.float32) + added
        ).astype(jnp.bfloat16)

    finish([mine_ref[:, :half], theirs_ref[:, :half]], 0, half)
    finish(
        [
            add(mine_ref[:, half:], late_ref[...]),
            add(theirs_ref[:, half:], late_theirs_ref[...]),
        ],
        half,
        width,
    )


def across(x, stride):
    n = lax.axis_size("seq")
    return lax.ppermute(x, "seq", [(i, i ^ stride) for i in range(n)])


def swap(x):
    return lax.ppermute(x, "tp", [(0, 1), (1, 0)])


def across_and_swap(x, stride):
    n = lax.axis_size("seq")
    pairs = [
        (2 * i + c, 2 * (i ^ stride) + 1 - c) for i in range(n) for c in range(2)
    ]
    return lax.ppermute(x, ("seq", "tp"), pairs)


def in_hbm(x):
    return pltpu.with_memory_space_constraint(x, pltpu.HBM)


def tied(*values):
    return lax.optimization_barrier(values)


def body(
    queries, keys_values, prompt_lengths, routes, gate_weights, norm_gain, w_gate, w_up, w_down
):
    tokens, width = queries.shape[1:]
    rows_true = keys_values.shape[1]
    pad = -rows_true % TILE
    seq, core = lax.axis_index("seq"), lax.axis_index("tp")
    own_queries = queries[0]
    strides = [1 << b for b in reversed(range(lax.axis_size("seq").bit_length() - 1))]

    kv = keys_values[0].reshape(rows_true, -1)
    if pad:
        kv = jnp.pad(kv, ((0, pad), (0, 0)))
    keep, send, comb = pl.pallas_call(
        pick_kernel,
        out_shape=[
            jax.ShapeDtypeStruct((CAP, width), jnp.bfloat16),
            jax.ShapeDtypeStruct((CAP, width), jnp.bfloat16),
            jax.ShapeDtypeStruct((2 * CAP, tokens), jnp.float32),
        ],
        in_specs=[SMEM] + [VMEM] * 3,
        out_specs=[VMEM] * 3,
        compiler_params=params(16),
        cost_estimate=cost(4 * CAP * tokens * width, 4 * tokens * width),
        name="pick",
    )(core.reshape(1), routes[0].T, gate_weights[0].T, own_queries)
    routed = jnp.concatenate([keep, swap(send)], axis=0)

    kv_blocks, routed_blocks, order = [kv], [routed], [0]
    for stride in strides[:-1]:
        kv_blocks = kv_blocks + [across(b, stride) for b in kv_blocks]
        routed_blocks = routed_blocks + [across(b, stride) for b in routed_blocks]
        order = order + [k ^ stride for k in order]
    first_kv, first_routed = across(kv, strides[-1]), across(routed, strides[-1])
    kv_blocks, routed_blocks, first_kv, first_routed = tied(
        kv_blocks, routed_blocks, first_kv, first_routed
    )
    kv_blocks = kv_blocks + [first_kv] + [across(b, strides[-1]) for b in kv_blocks[1:]]
    routed_blocks = (
        routed_blocks + [first_routed] + [across(b, strides[-1]) for b in routed_blocks[1:]]
    )
    order = order + [k ^ strides[-1] for k in order]

    pieces, places = [], []
    for block, k in zip([kv] + kv_blocks[1:], order):
        pieces += [block, swap(block)]
        places += [2 * (seq ^ k) + core, 2 * (seq ^ k) + 1 - core]
    place = jnp.stack([p * rows_true for p in places] + [prompt_lengths[0]]).astype(jnp.int32)

    gain = norm_gain.reshape(1, width)
    done = attend_call(place, routed_blocks[:-1], pieces, rows_true, gain)
    parts = expert_call(
        place, done, routed_blocks[-1], pieces, gain, w_gate[0], in_hbm(w_up[0]), in_hbm(w_down[0]), order, rows_true
    )

    own_queries, parts = tied(own_queries, parts)
    attended = attend_call(place, [own_queries], pieces, rows_true)
    parts = dict(zip(order, parts))
    straight = {k: v[0] for k, v in parts.items()}
    cut = cut_of(width)
    held = {k: v[-1][:, cut - width :] for k, v in parts.items()}
    for stride in strides[::-1][:-1]:
        sent = {k: across(v, stride) for k, v in held.items() if k & stride and k != 1}
        held = {
            k: add(v, sent[k ^ stride]) if k ^ stride in sent else v
            for k, v in held.items()
            if not k & stride
        }
    late, attended = tied(held[strides[0]], attended)
    late_mine = across(late[:CAP], strides[0])
    late_theirs = across_and_swap(late[CAP:], strides[0])
    arrived = [across(v, k) for k, v in straight.items() if k]
    arrived, late = tied(arrived, late)
    so_far = [
        jnp.concatenate(
            [
                add(straight[0][rows, :cut], *[a[rows, :cut] for a in arrived]),
                add(
                    held[0][rows],
                    *[a[rows, cut:] for a in arrived if a.shape[1] == width],
                ),
            ],
            axis=1,
        )
        for rows in (slice(None, CAP), slice(CAP, None))
    ]
    theirs = swap(so_far[1])
    mixed = pl.pallas_call(
        combine_kernel,
        out_shape=jax.ShapeDtypeStruct((tokens, width), jnp.bfloat16),
        in_specs=[VMEM] * 6,
        out_specs=VMEM,
        compiler_params=params(16),
        cost_estimate=cost(8 * CAP * tokens * width, 4 * tokens * width),
        name="combine",
    )(late_mine, late_theirs, comb, attended, so_far[0], theirs)
    return mixed[None]


def solution(mesh):
    return jax.shard_map(
        body,
        mesh=mesh,
        in_specs=(
            P(("group", "exp"), ("seq", "tp"), None),
            P(("group", "exp"), ("seq", "tp"), None, None),
            P(("group", "exp")),
            P(("group", "exp"), ("seq", "tp"), None),
            P(("group", "exp"), ("seq", "tp"), None),
            P(),
            P("tp", None, "seq"),
            P("tp", None, "seq"),
            P("tp", "seq", None),
        ),
        out_specs=P(("group", "exp"), ("seq", "tp"), None),
        check_vma=False,
    )
```

```python
import functools
import math

import jax
import jax.numpy as jnp
from jax import lax
from jax.experimental import pallas as pl
from jax.experimental.pallas import tpu as pltpu
from jax.sharding import PartitionSpec as P

HEAD_DIM = 128
PROMPT = 256
CAP = 16
TILE = 16

epsilon = 1e-06
masked_score = -1e30
MIB = 1024 * 1024

VMEM = pl.BlockSpec(memory_space=pltpu.VMEM)
SMEM = pl.BlockSpec(memory_space=pltpu.SMEM)
HBM = pl.BlockSpec(memory_space=pltpu.HBM)
ANY = pl.BlockSpec(memory_space=pl.ANY)


def params(mib):
    return pltpu.CompilerParams(vmem_limit_bytes=mib * MIB)


def cost(flops, moved, transcendentals=0):
    return pl.CostEstimate(
        flops=int(flops), bytes_accessed=int(moved), transcendentals=int(transcendentals)
    )


def pick_kernel(me_ref, routes_ref, gates_ref, q_ref, keep_ref, send_ref, comb_ref):
    top, tokens = routes_ref.shape
    me = me_ref[0]
    routes = routes_ref[...]
    gates = gates_ref[...]

    def of_expert(expert):
        hit = routes == expert
        member = jnp.sum(hit.astype(jnp.float32), axis=0, keepdims=True)
        weight = jnp.sum(jnp.where(hit, gates, 0.0), axis=0, keepdims=True)
        return member, weight

    member_a, weight_a = of_expert(me)
    member_b, weight_b = of_expert(1 - me)
    slot_of = lax.broadcasted_iota(jnp.int32, (2 * CAP, tokens), 0)
    mine = slot_of < CAP
    member = jnp.where(mine, member_a, member_b)
    weight = jnp.where(mine, weight_a, weight_b)
    row = lax.broadcasted_iota(jnp.int32, (tokens, tokens), 0)
    col = lax.broadcasted_iota(jnp.int32, (tokens, tokens), 1)
    before = jnp.where(row < col, 1.0, 0.0).astype(jnp.bfloat16)
    slot = jnp.dot(member.astype(jnp.bfloat16), before, preferred_element_type=jnp.float32)
    wanted = jnp.where(mine, slot_of, slot_of - CAP).astype(jnp.float32)
    taken = jnp.where((member > 0.0) & (slot == wanted), 1.0, 0.0)
    comb_ref[...] = taken * weight
    rows = jnp.dot(
        taken.astype(jnp.bfloat16), q_ref[...], preferred_element_type=jnp.float32
    ).astype(jnp.bfloat16)
    keep_ref[...] = rows[:CAP]
    send_ref[...] = rows[CAP:]


def key_bias(place_ref, kv_refs, rows_true):
    pieces = len(kv_refs)
    length = place_ref[pieces]
    parts = []
    for i, r in enumerate(kv_refs):
        lane = lax.broadcasted_iota(jnp.int32, (8, r.shape[0]), 1)
        position = lane + place_ref[i]
        allowed = (position >= PROMPT) | (position < length)
        allowed = allowed & (lane < rows_true)
        parts.append(jnp.where(allowed, 0.0, masked_score))
    return jnp.concatenate(parts, axis=1)[:1]


def attend(queries, kv_refs, bias, store, per_key):
    width = kv_refs[0].shape[1] // 2
    heads = width // HEAD_DIM
    factor = math.log2(math.e) / math.sqrt(HEAD_DIM)

    def one(head, _):
        at = head * HEAD_DIM
        if not isinstance(head, int):
            at = pl.multiple_of(at, HEAD_DIM)
        keys = jnp.concatenate([r[:, pl.ds(at, HEAD_DIM)] for r in kv_refs], axis=0)
        values = jnp.concatenate(
            [r[:, pl.ds(width + at, HEAD_DIM)] for r in kv_refs], axis=0
        )
        values = jnp.concatenate([values, jnp.ones_like(values)], axis=1)
        block = queries(at * per_key, per_key * HEAD_DIM)
        rows = block.shape[0]
        stacked = jnp.concatenate(
            [block[:, j * HEAD_DIM : (j + 1) * HEAD_DIM] for j in range(per_key)], axis=0
        )
        scores = (
            lax.dot_general(
                stacked, keys, (((1,), (1,)), ((), ())), preferred_element_type=jnp.float32
            )
            * factor
            + bias
        )
        weights = jnp.exp2(scores - jnp.max(scores, axis=1, keepdims=True))
        summed = jnp.dot(
            weights.astype(jnp.bfloat16), values, preferred_element_type=jnp.float32
        )
        result = (summed[:, :HEAD_DIM] / summed[:, HEAD_DIM:]).astype(jnp.bfloat16)
        for j in range(per_key):
            store(at * per_key + j * HEAD_DIM, result[j * rows : (j + 1) * rows])

    if bias.shape[1] > 1024:
        lax.fori_loop(0, heads, one, None)
    else:
        for head in range(heads):
            one(head, None)


def norm(rows, gain):
    x = rows.astype(jnp.float32)
    square = jnp.mean(x * x, axis=1, keepdims=True)
    return (x * lax.rsqrt(square + epsilon) * gain).astype(jnp.bfloat16)


def attend_kernel(pieces, blocks, per_key, rows_true, place_ref, *refs):
    q_blocks = refs[:blocks]
    kv_refs = refs[blocks : blocks + pieces]
    *gain, out_ref, q_ref, gain_ref, sems = refs[blocks + pieces :]
    copies = []
    for i, r in enumerate(q_blocks):
        rows = pl.ds(i * r.shape[0], r.shape[0])
        copies.append(pltpu.make_async_copy(r, q_ref.at[rows], sems.at[i]))
    for g in gain:
        copies.append(pltpu.make_async_copy(g, gain_ref, sems.at[blocks]))
    for c in copies:
        c.start()
    bias = key_bias(place_ref, kv_refs, rows_true)
    for c in copies[:blocks]:
        c.wait()

    def queries(at, size):
        return q_ref[:, pl.ds(at, size)]

    def store(at, result):
        out_ref[:, pl.ds(at, HEAD_DIM)] = result

    attend(queries, kv_refs, bias, store, per_key)
    for c in copies[blocks:]:
        c.wait()
        out_ref[...] = norm(out_ref[...], gain_ref[...])


def attend_call(place, q_blocks, kv_pieces, rows_true, *gain):
    width = q_blocks[0].shape[1]
    per_key = width // (kv_pieces[0].shape[1] // 2)
    rows = sum(q.shape[0] for q in q_blocks)
    keys = sum(p.shape[0] for p in kv_pieces)
    return pl.pallas_call(
        functools.partial(
            attend_kernel, len(kv_pieces), len(q_blocks), per_key, rows_true
        ),
        out_shape=jax.ShapeDtypeStruct((rows, width), jnp.bfloat16),
        in_specs=[SMEM]
        + [ANY] * len(q_blocks)
        + [VMEM] * len(kv_pieces)
        + [HBM] * len(gain),
        out_specs=VMEM,
        scratch_shapes=[
            pltpu.VMEM((rows, width), jnp.bfloat16),
            pltpu.VMEM((1, width), jnp.float32),
            pltpu.SemaphoreType.DMA((len(q_blocks) + 1,)),
        ],
        compiler_params=params(20 if rows * keys < 1 << 18 else 56),
        cost_estimate=cost(1, 1) if gain else cost(
            4 * rows * width * keys,
            4 * rows * width + 2 * keys * kv_pieces[0].shape[1],
            rows * keys * width // HEAD_DIM,
        ),
        name="attend",
    )(place, *q_blocks, *kv_pieces, *gain)


def cut_of(width):
    return width * 3 // 8 // HEAD_DIM * HEAD_DIM


def split_of(k, width):
    return [(0, width)] if k < 2 else [(0, cut_of(width)), (cut_of(width), width)]


def expert_kernel(
    pieces, order, per_key, rows_true, last_ref, place_ref, done_ref, *refs
):
    kv_refs = refs[:pieces]
    gain_ref, gate_ref, up_hbm, down_hbm = refs[pieces : pieces + 4]
    out_refs = refs[pieces + 4 : -4]
    x_ref, up_ref, down_ref, sems = refs[-4:]
    copies = [
        pltpu.make_async_copy(src, dst, sems.at[i])
        for i, (src, dst) in enumerate(
            ((up_hbm, up_ref), (down_hbm, down_ref))
        )
    ]
    for c in copies:
        c.start()
    bias = key_bias(place_ref, kv_refs, rows_true)

    def queries(at, size):
        return last_ref[:, pl.ds(at, size)]

    def store(at, result):
        x_ref[:, pl.ds(at, HEAD_DIM)] = result

    attend(queries, kv_refs, bias, store, per_key)
    normed = jnp.concatenate([done_ref[...], norm(x_ref[...], gain_ref[...])], axis=0)
    gate = jnp.dot(normed, gate_ref[...], preferred_element_type=jnp.float32)
    copies[0].wait()
    up = jnp.dot(normed, up_ref[...], preferred_element_type=jnp.float32)
    hidden = (gate / (1.0 + jnp.exp(-gate)) * up).astype(jnp.bfloat16)
    copies[1].wait()
    part = jnp.dot(hidden, down_ref[...], preferred_element_type=jnp.float32).astype(
        jnp.bfloat16
    )
    each, width = last_ref.shape
    out = iter(out_refs)
    for i, k in enumerate(order):
        for begin, end in split_of(k, width):
            next(out)[...] = part[i * each : (i + 1) * each, begin:end]


def expert_call(place, done, last, kv_pieces, gain, w_gate, w_up, w_down, order, rows_true):
    each, width = last.shape
    rows = len(order) * each
    hidden = w_gate.shape[1]
    per_key = width // (kv_pieces[0].shape[1] // 2)
    splits = [split_of(k, width) for k in order]
    shapes = [
        jax.ShapeDtypeStruct((each, end - begin), jnp.bfloat16)
        for split in splits
        for begin, end in split
    ]
    outs = iter(
        pl.pallas_call(
            functools.partial(expert_kernel, len(kv_pieces), tuple(order), per_key, rows_true),
            out_shape=shapes,
            in_specs=[VMEM, SMEM] + [VMEM] * (3 + len(kv_pieces)) + [HBM] * 2,
            out_specs=[VMEM] * len(shapes),
            scratch_shapes=[
                pltpu.VMEM((each, width), jnp.bfloat16),
                pltpu.VMEM(w_up.shape, jnp.bfloat16),
                pltpu.VMEM(w_down.shape, jnp.bfloat16),
                pltpu.SemaphoreType.DMA((2,)),
            ],
            compiler_params=params(26 if rows * hidden < 1 << 17 else 44),
            cost_estimate=cost(6 * rows * width * hidden, 6 * width * hidden),
            name="experts",
        )(last, place, done, *kv_pieces, gain, w_gate, w_up, w_down)
    )
    return [[next(outs) for _ in split] for split in splits]


def add(*terms):
    total = terms[0].astype(jnp.float32)
    for t in terms[1:]:
        total = total + t.astype(jnp.float32)
    return total.astype(jnp.bfloat16)


def combine_kernel(
    late_ref, late_theirs_ref, comb_ref, attended_ref, mine_ref, theirs_ref, out_ref
):
    width = out_ref.shape[1]
    half = width - late_ref.shape[1]
    comb = comb_ref[...]
    high = comb.astype(jnp.bfloat16)
    low = (comb - high.astype(jnp.float32)).astype(jnp.bfloat16)
    both = (((0,), (0,)), ((), ()))

    def finish(rows, begin, end):
        rows = jnp.concatenate(rows, axis=0)
        added = lax.dot_general(
            high, rows, both, preferred_element_type=jnp.float32
        ) + lax.dot_general(low, rows, both, preferred_element_type=jnp.float32)
        out_ref[:, begin:end] = (
            attended_ref[:, begin:end].astype(jnp.float32) + added
        ).astype(jnp.bfloat16)

    finish([mine_ref[:, :half], theirs_ref[:, :half]], 0, half)
    finish(
        [
            add(mine_ref[:, half:], late_ref[...]),
            add(theirs_ref[:, half:], late_theirs_ref[...]),
        ],
        half,
        width,
    )


def across(x, stride):
    n = lax.axis_size("seq")
    return lax.ppermute(x, "seq", [(i, i ^ stride) for i in range(n)])


def swap(x):
    return lax.ppermute(x, "tp", [(0, 1), (1, 0)])


def across_and_swap(x, stride):
    n = lax.axis_size("seq")
    pairs = [
        (2 * i + c, 2 * (i ^ stride) + 1 - c) for i in range(n) for c in range(2)
    ]
    return lax.ppermute(x, ("seq", "tp"), pairs)


def in_hbm(x):
    return pltpu.with_memory_space_constraint(x, pltpu.HBM)


def tied(*values):
    return lax.optimization_barrier(values)


def body(
    queries, keys_values, prompt_lengths, routes, gate_weights, norm_gain, w_gate, w_up, w_down
):
    tokens, width = queries.shape[1:]
    rows_true = keys_values.shape[1]
    pad = -rows_true % TILE
    seq, core = lax.axis_index("seq"), lax.axis_index("tp")
    own_queries = queries[0]
    strides = [1 << b for b in reversed(range(lax.axis_size("seq").bit_length() - 1))]

    kv = keys_values[0].reshape(rows_true, -1)
    if pad:
        kv = jnp.pad(kv, ((0, pad), (0, 0)))
    keep, send, comb = pl.pallas_call(
        pick_kernel,
        out_shape=[
            jax.ShapeDtypeStruct((CAP, width), jnp.bfloat16),
            jax.ShapeDtypeStruct((CAP, width), jnp.bfloat16),
            jax.ShapeDtypeStruct((2 * CAP, tokens), jnp.float32),
        ],
        in_specs=[SMEM] + [VMEM] * 3,
        out_specs=[VMEM] * 3,
        compiler_params=params(16),
        cost_estimate=cost(4 * CAP * tokens * width, 4 * tokens * width),
        name="pick",
    )(core.reshape(1), routes[0].T, gate_weights[0].T, own_queries)
    routed = jnp.concatenate([keep, swap(send)], axis=0)

    kv_blocks, routed_blocks, order = [kv], [routed], [0]
    for stride in strides[:-1]:
        kv_blocks = kv_blocks + [across(b, stride) for b in kv_blocks]
        routed_blocks = routed_blocks + [across(b, stride) for b in routed_blocks]
        order = order + [k ^ stride for k in order]
    first_kv, first_routed = across(kv, strides[-1]), across(routed, strides[-1])
    kv_blocks, routed_blocks, first_kv, first_routed = tied(
        kv_blocks, routed_blocks, first_kv, first_routed
    )
    kv_blocks = kv_blocks + [first_kv] + [across(b, strides[-1]) for b in kv_blocks[1:]]
    routed_blocks = (
        routed_blocks + [first_routed] + [across(b, strides[-1]) for b in routed_blocks[1:]]
    )
    order = order + [k ^ strides[-1] for k in order]

    swapped = [swap(b) for b in kv_blocks[:-1]]
    last, swapped = tied(kv_blocks[-1], swapped)
    rows = kv.shape[0]
    parts = 2 if rows % (2 * TILE) == 0 and not pad else 1
    cuts = range(0, rows, rows // parts)
    pieces = kv_blocks[:-1] + swapped + [last]
    pieces += [swap(last[c : c + rows // parts]) for c in cuts]
    places = [(2 * (seq ^ k) + core) * rows_true for k in order[:-1]]
    places += [(2 * (seq ^ k) + 1 - core) * rows_true for k in order[:-1]]
    places += [(2 * (seq ^ order[-1]) + core) * rows_true]
    places += [(2 * (seq ^ order[-1]) + 1 - core) * rows_true + c for c in cuts]
    place = jnp.stack(places + [prompt_lengths[0]]).astype(jnp.int32)

    gain = norm_gain.reshape(1, width)
    early = [in_hbm(b) for b in routed_blocks[:-1]]
    done = attend_call(place, early, pieces, rows_true, in_hbm(gain))
    parts = expert_call(
        place, done, routed_blocks[-1], pieces, gain, w_gate[0], in_hbm(w_up[0]), in_hbm(w_down[0]), order, rows_true
    )

    own_queries, parts = tied(own_queries, parts)
    attended = attend_call(place, [own_queries], pieces, rows_true)
    parts = dict(zip(order, parts))
    straight = {k: v[0] for k, v in parts.items()}
    cut = cut_of(width)
    held = {k: v[-1][:, cut - width :] for k, v in parts.items()}
    for stride in strides[::-1][:-1]:
        sent = {k: across(v, stride) for k, v in held.items() if k & stride and k != 1}
        held = {
            k: add(v, sent[k ^ stride]) if k ^ stride in sent else v
            for k, v in held.items()
            if not k & stride
        }
    late, attended = tied(held[strides[0]], attended)
    late_mine = across(late[:CAP], strides[0])
    late_theirs = across_and_swap(late[CAP:], strides[0])
    arrived = [across(v, k) for k, v in straight.items() if k]
    arrived, late = tied(arrived, late)
    so_far = [
        jnp.concatenate(
            [
                add(straight[0][rows, :cut], *[a[rows, :cut] for a in arrived]),
                add(
                    held[0][rows],
                    *[a[rows, cut:] for a in arrived if a.shape[1] == width],
                ),
            ],
            axis=1,
        )
        for rows in (slice(None, CAP), slice(CAP, None))
    ]
    theirs = swap(so_far[1])
    mixed = pl.pallas_call(
        combine_kernel,
        out_shape=jax.ShapeDtypeStruct((tokens, width), jnp.bfloat16),
        in_specs=[VMEM] * 6,
        out_specs=VMEM,
        compiler_params=params(16),
        cost_estimate=cost(8 * CAP * tokens * width, 4 * tokens * width),
        name="combine",
    )(late_mine, late_theirs, comb, attended, so_far[0], theirs)
    return mixed[None]


def solution(mesh):
    return jax.shard_map(
        body,
        mesh=mesh,
        in_specs=(
            P(("group", "exp"), ("seq", "tp"), None),
            P(("group", "exp"), ("seq", "tp"), None, None),
            P(("group", "exp")),
            P(("group", "exp"), ("seq", "tp"), None),
            P(("group", "exp"), ("seq", "tp"), None),
            P(),
            P("tp", None, "seq"),
            P("tp", None, "seq"),
            P("tp", "seq", None),
        ),
        out_specs=P(("group", "exp"), ("seq", "tp"), None),
        check_vma=False,
    )
```

```python
import functools
import math

import jax
import jax.numpy as jnp
from jax import lax
from jax.experimental import pallas as pl
from jax.experimental.pallas import tpu as pltpu
from jax.sharding import PartitionSpec as P

HEAD_DIM = 128
PROMPT = 256
CAP = 16
TILE = 16

epsilon = 1e-06
masked_score = -1e30
MIB = 1024 * 1024

VMEM = pl.BlockSpec(memory_space=pltpu.VMEM)
SMEM = pl.BlockSpec(memory_space=pltpu.SMEM)
HBM = pl.BlockSpec(memory_space=pltpu.HBM)


def params(mib):
    return pltpu.CompilerParams(vmem_limit_bytes=mib * MIB)


def cost(flops, moved, transcendentals=0):
    return pl.CostEstimate(
        flops=int(flops), bytes_accessed=int(moved), transcendentals=int(transcendentals)
    )


def pick_kernel(me_ref, routes_ref, gates_ref, q_ref, keep_ref, send_ref, comb_ref):
    top, tokens = routes_ref.shape
    me = me_ref[0]
    routes = routes_ref[...]
    gates = gates_ref[...]

    def of_expert(expert):
        hit = routes == expert
        member = jnp.sum(hit.astype(jnp.float32), axis=0, keepdims=True)
        weight = jnp.sum(jnp.where(hit, gates, 0.0), axis=0, keepdims=True)
        return member, weight

    member_a, weight_a = of_expert(me)
    member_b, weight_b = of_expert(1 - me)
    slot_of = lax.broadcasted_iota(jnp.int32, (2 * CAP, tokens), 0)
    mine = slot_of < CAP
    member = jnp.where(mine, member_a, member_b)
    weight = jnp.where(mine, weight_a, weight_b)
    row = lax.broadcasted_iota(jnp.int32, (tokens, tokens), 0)
    col = lax.broadcasted_iota(jnp.int32, (tokens, tokens), 1)
    before = jnp.where(row < col, 1.0, 0.0).astype(jnp.bfloat16)
    slot = jnp.dot(member.astype(jnp.bfloat16), before, preferred_element_type=jnp.float32)
    wanted = jnp.where(mine, slot_of, slot_of - CAP).astype(jnp.float32)
    taken = jnp.where((member > 0.0) & (slot == wanted), 1.0, 0.0)
    comb_ref[...] = taken * weight
    rows = jnp.dot(
        taken.astype(jnp.bfloat16), q_ref[...], preferred_element_type=jnp.float32
    ).astype(jnp.bfloat16)
    keep_ref[...] = rows[:CAP]
    send_ref[...] = rows[CAP:]


def key_bias(length_ref, kv_refs, origins, rows_true):
    seq, core = lax.axis_index("seq"), lax.axis_index("tp")
    length = length_ref[0]
    parts = []
    for r, (k, side, first) in zip(kv_refs, origins):
        row = lax.broadcasted_iota(jnp.int32, (8, r.shape[0]), 1) + first
        position = row + (2 * (seq ^ k) + (core ^ side)) * rows_true
        allowed = (position >= PROMPT) | (position < length)
        allowed = allowed & (row < rows_true)
        parts.append(jnp.where(allowed, 0.0, masked_score))
    return jnp.concatenate(parts, axis=1)[:1]


def attend(queries, kv_refs, bias, store, per_key, before=None, after=None):
    width = kv_refs[0].shape[1] // 2
    heads = width // HEAD_DIM
    factor = math.log2(math.e) / math.sqrt(HEAD_DIM)

    def one(head, _):
        at = head * HEAD_DIM
        if not isinstance(head, int):
            at = pl.multiple_of(at, HEAD_DIM)
        keys = jnp.concatenate([r[:, pl.ds(at, HEAD_DIM)] for r in kv_refs], axis=0)
        values = jnp.concatenate(
            [r[:, pl.ds(width + at, HEAD_DIM)] for r in kv_refs], axis=0
        )
        values = jnp.concatenate([values, jnp.ones_like(values)], axis=1)
        block = queries(at * per_key, per_key * HEAD_DIM)
        rows = block.shape[0]
        stacked = jnp.concatenate(
            [block[:, j * HEAD_DIM : (j + 1) * HEAD_DIM] for j in range(per_key)], axis=0
        )
        scores = (
            lax.dot_general(
                stacked, keys, (((1,), (1,)), ((), ())), preferred_element_type=jnp.float32
            )
            * factor
            + bias
        )
        largest = jnp.max(scores, axis=1, keepdims=True)
        mine = pl.ds(head * per_key * rows, per_key * rows)
        if before is not None:
            earlier = before[1][mine, :][:, :1]
            largest = jnp.maximum(largest, earlier)
        weights = jnp.exp2(scores - largest)
        summed = jnp.dot(
            weights.astype(jnp.bfloat16), values, preferred_element_type=jnp.float32
        )
        if before is not None:
            summed = summed + before[0][mine, :] * jnp.exp2(earlier - largest)
        if after is not None:
            after[0][mine, :] = summed
            after[1][mine, :] = jnp.broadcast_to(largest, (per_key * rows, HEAD_DIM))
            return
        result = (summed[:, :HEAD_DIM] / summed[:, HEAD_DIM:]).astype(jnp.bfloat16)
        for j in range(per_key):
            store(at * per_key + j * HEAD_DIM, result[j * rows : (j + 1) * rows])

    if bias.shape[1] > 1024 or per_key * HEAD_DIM * heads > 1 << 13:
        lax.fori_loop(0, heads, one, None)
    else:
        for head in range(heads):
            one(head, None)


def norm(rows, gain):
    x = rows.astype(jnp.float32)
    square = jnp.mean(x * x, axis=1, keepdims=True)
    return (x * lax.rsqrt(square + epsilon) * gain).astype(jnp.bfloat16)


def columns_of(q_refs):
    def queries(at, size):
        return jnp.concatenate([r[:, pl.ds(at, size)] for r in q_refs], axis=0)

    return queries


def into(ref):
    def store(at, result):
        ref[:, pl.ds(at, HEAD_DIM)] = result

    return store


def attend_kernel(origins, per_key, rows_true, length_ref, q_ref, *refs):
    kv_refs = refs[: len(origins)]
    bias = key_bias(length_ref, kv_refs, origins, rows_true)
    attend(columns_of([q_ref]), kv_refs, bias, into(refs[-1]), per_key)


def begin_kernel(origins, per_key, rows_true, length_ref, *refs):
    pieces = len(origins)
    kv_refs, after, mark_ref = refs[-pieces - 3 : -3], refs[-3:-1], refs[-1]
    bias = key_bias(length_ref, kv_refs, origins, rows_true)
    attend(columns_of(refs[: -pieces - 3]), kv_refs, bias, None, per_key, after=after)
    mark_ref[...] = jnp.zeros_like(mark_ref)


def finish_kernel(origins, per_key, rows_true, length_ref, *refs):
    pieces = len(origins)
    gain_ref, sums_ref, largest_ref, _, out_ref = refs[-5:]
    kv_refs = refs[-pieces - 5 : -5]
    bias = key_bias(length_ref, kv_refs, origins, rows_true)
    attend(
        columns_of(refs[: -pieces - 5]),
        kv_refs,
        bias,
        into(out_ref),
        per_key,
        before=(sums_ref, largest_ref),
    )
    out_ref[...] = norm(out_ref[...], gain_ref[...])


def attention(kernel, name, length, q_blocks, pieces, rows_true, more, out_shape, price):
    kv_pieces, origins = pieces
    per_key = q_blocks[0].shape[1] // (kv_pieces[0].shape[1] // 2)
    large = sum(q.shape[0] for q in q_blocks) * sum(p.shape[0] for p in kv_pieces)
    count = len(q_blocks) + len(kv_pieces) + len(more)
    return pl.pallas_call(
        functools.partial(kernel, tuple(origins), per_key, rows_true),
        out_shape=out_shape,
        in_specs=[SMEM] + [VMEM] * count,
        out_specs=jax.tree.map(lambda _: VMEM, out_shape),
        compiler_params=params(20 if large < 1 << 17 else 58),
        cost_estimate=price,
        name=name,
    )(length, *q_blocks, *kv_pieces, *more)


def attend_call(length, queries, pieces, rows_true):
    rows, width = queries.shape
    keys = sum(p.shape[0] for p in pieces[0])
    shape = jax.ShapeDtypeStruct((rows, width), jnp.bfloat16)
    price = cost(
        4 * rows * width * keys,
        4 * rows * width + 2 * keys * pieces[0][0].shape[1],
        rows * keys * width // HEAD_DIM,
    )
    return attention(
        attend_kernel, "attend", length, [queries], pieces, rows_true, [], shape, price
    )


def begin_call(length, q_blocks, pieces, rows_true):
    rows = sum(q.shape[0] for q in q_blocks) * q_blocks[0].shape[1] // HEAD_DIM
    shapes = [
        jax.ShapeDtypeStruct((rows, 2 * HEAD_DIM), jnp.float32),
        jax.ShapeDtypeStruct((rows, HEAD_DIM), jnp.float32),
        jax.ShapeDtypeStruct((8, HEAD_DIM), jnp.float32),
    ]
    return attention(
        begin_kernel, "begin", length, q_blocks, pieces, rows_true, [], shapes, cost(1, 1)
    )


def finish_call(length, q_blocks, pieces, rows_true, gain, begun):
    rows = sum(q.shape[0] for q in q_blocks)
    shape = jax.ShapeDtypeStruct((rows, q_blocks[0].shape[1]), jnp.bfloat16)
    more = [gain, *begun]
    return attention(
        finish_kernel, "finish", length, q_blocks, pieces, rows_true, more, shape, cost(1, 1)
    )


def halve_kernel(whole_ref, top_ref, bottom_ref):
    rows = top_ref.shape[0]
    top_ref[...] = whole_ref[:rows]
    bottom_ref[...] = whole_ref[rows:]


def halve_call(whole):
    rows, width = whole.shape
    return pl.pallas_call(
        halve_kernel,
        out_shape=[jax.ShapeDtypeStruct((rows // 2, width), whole.dtype)] * 2,
        in_specs=[VMEM],
        out_specs=[VMEM] * 2,
        compiler_params=params(4),
        cost_estimate=cost(1, 1),
        name="halve",
    )(whole)


def cut_of(width):
    return width * 3 // 8 // HEAD_DIM * HEAD_DIM


def split_of(k, width):
    return [(0, width)] if k < 2 else [(0, cut_of(width)), (cut_of(width), width)]


def expert_kernel(
    origins, order, per_key, rows_true, last_ref, length_ref, done_ref, *refs
):
    pieces = len(origins)
    kv_refs = refs[:pieces]
    gain_ref, gate_ref, up_hbm, down_hbm = refs[pieces : pieces + 4]
    out_refs = refs[pieces + 4 : -4]
    x_ref, up_ref, down_ref, sems = refs[-4:]
    copies = [
        pltpu.make_async_copy(src, dst, sems.at[i])
        for i, (src, dst) in enumerate(
            ((up_hbm, up_ref), (down_hbm, down_ref))
        )
    ]
    for c in copies:
        c.start()
    bias = key_bias(length_ref, kv_refs, origins, rows_true)

    def queries(at, size):
        return last_ref[:, pl.ds(at, size)]

    def store(at, result):
        x_ref[:, pl.ds(at, HEAD_DIM)] = result

    attend(queries, kv_refs, bias, store, per_key)
    normed = jnp.concatenate([done_ref[...], norm(x_ref[...], gain_ref[...])], axis=0)
    gate = jnp.dot(normed, gate_ref[...], preferred_element_type=jnp.float32)
    copies[0].wait()
    up = jnp.dot(normed, up_ref[...], preferred_element_type=jnp.float32)
    hidden = (gate / (1.0 + jnp.exp(-gate)) * up).astype(jnp.bfloat16)
    copies[1].wait()
    part = jnp.dot(hidden, down_ref[...], preferred_element_type=jnp.float32).astype(
        jnp.bfloat16
    )
    each, width = last_ref.shape
    out = iter(out_refs)
    for i, k in enumerate(order):
        for begin, end in split_of(k, width):
            next(out)[...] = part[i * each : (i + 1) * each, begin:end]


def expert_call(length, done, last, pieces, gain, w_gate, w_up, w_down, order, rows_true):
    kv_pieces, origins = pieces
    each, width = last.shape
    rows = len(order) * each
    hidden = w_gate.shape[1]
    per_key = width // (kv_pieces[0].shape[1] // 2)
    splits = [split_of(k, width) for k in order]
    shapes = [
        jax.ShapeDtypeStruct((each, end - begin), jnp.bfloat16)
        for split in splits
        for begin, end in split
    ]
    outs = iter(
        pl.pallas_call(
            functools.partial(expert_kernel, tuple(origins), tuple(order), per_key, rows_true),
            out_shape=shapes,
            in_specs=[VMEM, SMEM] + [VMEM] * (3 + len(kv_pieces)) + [HBM] * 2,
            out_specs=[VMEM] * len(shapes),
            scratch_shapes=[
                pltpu.VMEM((each, width), jnp.bfloat16),
                pltpu.VMEM(w_up.shape, jnp.bfloat16),
                pltpu.VMEM(w_down.shape, jnp.bfloat16),
                pltpu.SemaphoreType.DMA((2,)),
            ],
            compiler_params=params(26 if rows * hidden < 1 << 17 else 44),
            cost_estimate=cost(6 * rows * width * hidden, 6 * width * hidden),
            name="experts",
        )(last, length, done, *kv_pieces, gain, w_gate, w_up, w_down)
    )
    return [[next(outs) for _ in split] for split in splits]


def add(*terms):
    total = terms[0].astype(jnp.float32)
    for t in terms[1:]:
        total = total + t.astype(jnp.float32)
    return total.astype(jnp.bfloat16)


def combine_kernel(
    late_ref, late_theirs_ref, comb_ref, attended_ref, mine_ref, theirs_ref, out_ref
):
    width = out_ref.shape[1]
    half = width - late_ref.shape[1]
    comb = comb_ref[...]
    high = comb.astype(jnp.bfloat16)
    low = (comb - high.astype(jnp.float32)).astype(jnp.bfloat16)
    both = (((0,), (0,)), ((), ()))

    def finish(rows, begin, end):
        rows = jnp.concatenate(rows, axis=0)
        added = lax.dot_general(
            high, rows, both, preferred_element_type=jnp.float32
        ) + lax.dot_general(low, rows, both, preferred_element_type=jnp.float32)
        out_ref[:, begin:end] = (
            attended_ref[:, begin:end].astype(jnp.float32) + added
        ).astype(jnp.bfloat16)

    finish([mine_ref[:, :half], theirs_ref[:, :half]], 0, half)
    finish(
        [
            add(mine_ref[:, half:], late_ref[...]),
            add(theirs_ref[:, half:], late_theirs_ref[...]),
        ],
        half,
        width,
    )


def across(x, stride):
    n = lax.axis_size("seq")
    return lax.ppermute(x, "seq", [(i, i ^ stride) for i in range(n)])


def swap(x):
    return lax.ppermute(x, "tp", [(0, 1), (1, 0)])


def across_and_swap(x, stride):
    n = lax.axis_size("seq")
    pairs = [
        (2 * i + c, 2 * (i ^ stride) + 1 - c) for i in range(n) for c in range(2)
    ]
    return lax.ppermute(x, ("seq", "tp"), pairs)


def in_hbm(x):
    return pltpu.with_memory_space_constraint(x, pltpu.HBM)


def tied(*values):
    return lax.optimization_barrier(values)


def body(
    queries, keys_values, prompt_lengths, routes, gate_weights, norm_gain, w_gate, w_up, w_down
):
    tokens, width = queries.shape[1:]
    rows_true = keys_values.shape[1]
    pad = -rows_true % TILE
    core = lax.axis_index("tp")
    own_queries = queries[0]
    strides = [1 << b for b in reversed(range(lax.axis_size("seq").bit_length() - 1))]

    kv = keys_values[0].reshape(rows_true, -1)
    if pad:
        kv = jnp.pad(kv, ((0, pad), (0, 0)))
    keep, send, comb = pl.pallas_call(
        pick_kernel,
        out_shape=[
            jax.ShapeDtypeStruct((CAP, width), jnp.bfloat16),
            jax.ShapeDtypeStruct((CAP, width), jnp.bfloat16),
            jax.ShapeDtypeStruct((2 * CAP, tokens), jnp.float32),
        ],
        in_specs=[SMEM] + [VMEM] * 3,
        out_specs=[VMEM] * 3,
        compiler_params=params(16),
        cost_estimate=cost(4 * CAP * tokens * width, 4 * tokens * width),
        name="pick",
    )(core.reshape(1), routes[0].T, gate_weights[0].T, own_queries)
    routed = jnp.concatenate([keep, swap(send)], axis=0)

    kv_blocks, routed_blocks, order = [kv], [routed], [0]
    for stride in strides[:-1]:
        kv_blocks = kv_blocks + [across(b, stride) for b in kv_blocks]
        routed_blocks = routed_blocks + [across(b, stride) for b in routed_blocks]
        order = order + [k ^ stride for k in order]
    first_kv, first_routed = across(kv, strides[-1]), across(routed, strides[-1])
    kv_blocks, routed_blocks, first_kv, first_routed = tied(
        kv_blocks, routed_blocks, first_kv, first_routed
    )
    last_kv = [across(b, strides[-1]) for b in kv_blocks[1:]]
    kv_blocks = kv_blocks + [first_kv] + last_kv
    order = order + [k ^ strides[-1] for k in order]
    rows = kv.shape[0]
    shares = 2 if rows % (2 * TILE) == 0 and not pad else 1
    cuts = range(0, rows, rows // shares)
    swapped = [swap(b) for b in kv_blocks[:-1]]

    origins = [(k, side, 0) for side in (0, 1) for k in order[:-1]]
    first_pieces = kv_blocks[:-1] + swapped, origins
    length = prompt_lengths

    early = routed_blocks + [first_routed]
    late_blocks = [across(b, strides[-1]) for b in routed_blocks[1:-1]]
    early += late_blocks
    *begun, mark = begin_call(length, early, first_pieces, rows_true)
    held_back, mark = tied(routed_blocks[-1], mark)
    last_routed = across(held_back, strides[-1])
    last, mark = tied(kv_blocks[-1], mark)
    halves = halve_call(last) if shares == 2 else [last]
    last_pieces = (
        [last] + [swap(h) for h in halves],
        [(order[-1], 0, 0)] + [(order[-1], 1, c) for c in cuts],
    )
    pieces = tuple(a + b for a, b in zip(first_pieces, last_pieces))

    gain = norm_gain.reshape(1, width)
    done = finish_call(length, early, last_pieces, rows_true, gain, [*begun, mark])
    parts = expert_call(
        length, done, last_routed, pieces, gain, w_gate[0], in_hbm(w_up[0]), in_hbm(w_down[0]),
        order, rows_true,
    )

    own_queries, parts = tied(own_queries, parts)
    attended = attend_call(length, own_queries, pieces, rows_true)
    parts = dict(zip(order, parts))
    straight = {k: v[0] for k, v in parts.items()}
    cut = cut_of(width)
    held = {k: v[-1][:, cut - width :] for k, v in parts.items()}
    for stride in strides[::-1][:-1]:
        sent = {k: across(v, stride) for k, v in held.items() if k & stride and k != 1}
        held = {
            k: add(v, sent[k ^ stride]) if k ^ stride in sent else v
            for k, v in held.items()
            if not k & stride
        }
    late, attended = tied(held[strides[0]], attended)
    late_mine = across(late[:CAP], strides[0])
    late_theirs = across_and_swap(late[CAP:], strides[0])
    arrived = [across(v, k) for k, v in straight.items() if k]
    arrived, late = tied(arrived, late)
    so_far = [
        jnp.concatenate(
            [
                add(straight[0][rows, :cut], *[a[rows, :cut] for a in arrived]),
                add(
                    held[0][rows],
                    *[a[rows, cut:] for a in arrived if a.shape[1] == width],
                ),
            ],
            axis=1,
        )
        for rows in (slice(None, CAP), slice(CAP, None))
    ]
    theirs = swap(so_far[1])
    mixed = pl.pallas_call(
        combine_kernel,
        out_shape=jax.ShapeDtypeStruct((tokens, width), jnp.bfloat16),
        in_specs=[VMEM] * 6,
        out_specs=VMEM,
        compiler_params=params(16),
        cost_estimate=cost(8 * CAP * tokens * width, 4 * tokens * width),
        name="combine",
    )(late_mine, late_theirs, comb, attended, so_far[0], theirs)
    return mixed[None]


def solution(mesh):
    return jax.shard_map(
        body,
        mesh=mesh,
        in_specs=(
            P(("group", "exp"), ("seq", "tp"), None),
            P(("group", "exp"), ("seq", "tp"), None, None),
            P(("group", "exp")),
            P(("group", "exp"), ("seq", "tp"), None),
            P(("group", "exp"), ("seq", "tp"), None),
            P(),
            P("tp", None, "seq"),
            P("tp", None, "seq"),
            P("tp", "seq", None),
        ),
        out_specs=P(("group", "exp"), ("seq", "tp"), None),
        check_vma=False,
    )
```

```python
import functools
import math

import jax
import jax.numpy as jnp
from jax import lax
from jax.experimental import pallas as pl
from jax.experimental.pallas import tpu as pltpu
from jax.sharding import PartitionSpec as P

HEAD_DIM = 128
PROMPT = 256
CAP = 16
TILE = 16

epsilon = 1e-06
masked_score = -1e30
MIB = 1024 * 1024

VMEM = pl.BlockSpec(memory_space=pltpu.VMEM)
SMEM = pl.BlockSpec(memory_space=pltpu.SMEM)
HBM = pl.BlockSpec(memory_space=pltpu.HBM)


def params(mib):
    return pltpu.CompilerParams(vmem_limit_bytes=mib * MIB)


def cost(flops, moved, transcendentals=0):
    return pl.CostEstimate(
        flops=int(flops), bytes_accessed=int(moved), transcendentals=int(transcendentals)
    )


def pick_kernel(me_ref, routes_ref, gates_ref, q_ref, keep_ref, send_ref, comb_ref):
    top, tokens = routes_ref.shape
    me = me_ref[0]
    routes = routes_ref[...]
    gates = gates_ref[...]

    def of_expert(expert):
        hit = routes == expert
        member = jnp.sum(hit.astype(jnp.float32), axis=0, keepdims=True)
        weight = jnp.sum(jnp.where(hit, gates, 0.0), axis=0, keepdims=True)
        return member, weight

    member_a, weight_a = of_expert(me)
    member_b, weight_b = of_expert(1 - me)
    slot_of = lax.broadcasted_iota(jnp.int32, (2 * CAP, tokens), 0)
    mine = slot_of < CAP
    member = jnp.where(mine, member_a, member_b)
    weight = jnp.where(mine, weight_a, weight_b)
    row = lax.broadcasted_iota(jnp.int32, (tokens, tokens), 0)
    col = lax.broadcasted_iota(jnp.int32, (tokens, tokens), 1)
    before = jnp.where(row < col, 1.0, 0.0).astype(jnp.bfloat16)
    slot = jnp.dot(member.astype(jnp.bfloat16), before, preferred_element_type=jnp.float32)
    wanted = jnp.where(mine, slot_of, slot_of - CAP).astype(jnp.float32)
    taken = jnp.where((member > 0.0) & (slot == wanted), 1.0, 0.0)
    comb_ref[...] = taken * weight
    rows = jnp.dot(
        taken.astype(jnp.bfloat16), q_ref[...], preferred_element_type=jnp.float32
    ).astype(jnp.bfloat16)
    keep_ref[...] = rows[:CAP]
    send_ref[...] = rows[CAP:]


def key_bias(length_ref, kv_refs, origins, rows_true):
    seq, core = lax.axis_index("seq"), lax.axis_index("tp")
    length = length_ref[0]
    parts = []
    for r, (k, side, first) in zip(kv_refs, origins):
        row = lax.broadcasted_iota(jnp.int32, (8, r.shape[0]), 1) + first
        position = row + (2 * (seq ^ k) + (core ^ side)) * rows_true
        allowed = (position >= PROMPT) | (position < length)
        allowed = allowed & (row < rows_true)
        parts.append(jnp.where(allowed, 0.0, masked_score))
    return jnp.concatenate(parts, axis=1)[:1]


def attend(queries, kv_refs, bias, store, per_key, before=None, after=None):
    width = kv_refs[0].shape[1] // 2
    heads = width // HEAD_DIM
    factor = math.log2(math.e) / math.sqrt(HEAD_DIM)

    def one(head, _):
        at = head * HEAD_DIM
        if not isinstance(head, int):
            at = pl.multiple_of(at, HEAD_DIM)
        keys = jnp.concatenate([r[:, pl.ds(at, HEAD_DIM)] for r in kv_refs], axis=0)
        values = jnp.concatenate(
            [r[:, pl.ds(width + at, HEAD_DIM)] for r in kv_refs], axis=0
        )
        values = jnp.concatenate([values, jnp.ones_like(values)], axis=1)
        block = queries(at * per_key, per_key * HEAD_DIM)
        rows = block.shape[0]
        stacked = jnp.concatenate(
            [block[:, j * HEAD_DIM : (j + 1) * HEAD_DIM] for j in range(per_key)], axis=0
        )
        scores = (
            lax.dot_general(
                stacked, keys, (((1,), (1,)), ((), ())), preferred_element_type=jnp.float32
            )
            * factor
            + bias
        )
        largest = jnp.max(scores, axis=1, keepdims=True)
        mine = pl.ds(head * per_key * rows, per_key * rows)
        if before is not None:
            earlier = before[1][mine, :]
            largest = jnp.maximum(earlier, largest)
            scale = jnp.exp2(earlier - largest)
            count = -(-scores.shape[1] // HEAD_DIM)
            largest = jnp.concatenate([largest] * count, axis=1)[:, : scores.shape[1]]
        weights = jnp.exp2(scores - largest)
        summed = jnp.dot(
            weights.astype(jnp.bfloat16), values, preferred_element_type=jnp.float32
        )
        if before is not None:
            summed = summed + before[0][mine, :] * jnp.concatenate([scale, scale], axis=1)
        if after is not None:
            after[0][mine, :] = summed
            after[1][mine, :] = jnp.broadcast_to(largest, (per_key * rows, HEAD_DIM))
            return
        result = (summed[:, :HEAD_DIM] / summed[:, HEAD_DIM:]).astype(jnp.bfloat16)
        for j in range(per_key):
            store(at * per_key + j * HEAD_DIM, result[j * rows : (j + 1) * rows])

    if bias.shape[1] > 1024 or per_key * HEAD_DIM * heads > 1 << 13:
        lax.fori_loop(0, heads, one, None)
    else:
        for head in range(heads):
            one(head, None)


def norm(rows, gain):
    x = rows.astype(jnp.float32)
    square = jnp.mean(x * x, axis=1, keepdims=True)
    return (x * lax.rsqrt(square + epsilon) * gain).astype(jnp.bfloat16)


def columns_of(q_refs):
    def queries(at, size):
        return jnp.concatenate([r[:, pl.ds(at, size)] for r in q_refs], axis=0)

    return queries


def into(ref):
    def store(at, result):
        ref[:, pl.ds(at, HEAD_DIM)] = result

    return store


def attend_kernel(origins, per_key, rows_true, length_ref, q_ref, *refs):
    kv_refs = refs[: len(origins)]
    bias = key_bias(length_ref, kv_refs, origins, rows_true)
    attend(columns_of([q_ref]), kv_refs, bias, into(refs[-1]), per_key)


def begin_kernel(origins, per_key, rows_true, length_ref, *refs):
    pieces = len(origins)
    kv_refs, after, mark_ref = refs[-pieces - 3 : -3], refs[-3:-1], refs[-1]
    bias = key_bias(length_ref, kv_refs, origins, rows_true)
    attend(columns_of(refs[: -pieces - 3]), kv_refs, bias, None, per_key, after=after)
    mark_ref[...] = jnp.zeros_like(mark_ref)


def finish_kernel(origins, per_key, rows_true, length_ref, *refs):
    pieces = len(origins)
    gain_ref, sums_ref, largest_ref, _, out_ref = refs[-5:]
    kv_refs = refs[-pieces - 5 : -5]
    bias = key_bias(length_ref, kv_refs, origins, rows_true)
    attend(
        columns_of(refs[: -pieces - 5]),
        kv_refs,
        bias,
        into(out_ref),
        per_key,
        before=(sums_ref, largest_ref),
    )
    out_ref[...] = norm(out_ref[...], gain_ref[...])


def attention(kernel, name, length, q_blocks, pieces, rows_true, more, out_shape, price):
    kv_pieces, origins = pieces
    per_key = q_blocks[0].shape[1] // (kv_pieces[0].shape[1] // 2)
    large = sum(q.shape[0] for q in q_blocks) * sum(p.shape[0] for p in kv_pieces)
    count = len(q_blocks) + len(kv_pieces) + len(more)
    return pl.pallas_call(
        functools.partial(kernel, tuple(origins), per_key, rows_true),
        out_shape=out_shape,
        in_specs=[SMEM] + [VMEM] * count,
        out_specs=jax.tree.map(lambda _: VMEM, out_shape),
        compiler_params=params(20 if large < 1 << 17 else 58),
        cost_estimate=price,
        name=name,
    )(length, *q_blocks, *kv_pieces, *more)


def attend_call(length, queries, pieces, rows_true):
    rows, width = queries.shape
    keys = sum(p.shape[0] for p in pieces[0])
    shape = jax.ShapeDtypeStruct((rows, width), jnp.bfloat16)
    price = cost(
        4 * rows * width * keys,
        4 * rows * width + 2 * keys * pieces[0][0].shape[1],
        rows * keys * width // HEAD_DIM,
    )
    return attention(
        attend_kernel, "attend", length, [queries], pieces, rows_true, [], shape, price
    )


def begin_call(length, q_blocks, pieces, rows_true):
    rows = sum(q.shape[0] for q in q_blocks) * q_blocks[0].shape[1] // HEAD_DIM
    shapes = [
        jax.ShapeDtypeStruct((rows, 2 * HEAD_DIM), jnp.float32),
        jax.ShapeDtypeStruct((rows, HEAD_DIM), jnp.float32),
        jax.ShapeDtypeStruct((8, HEAD_DIM), jnp.float32),
    ]
    return attention(
        begin_kernel, "begin", length, q_blocks, pieces, rows_true, [], shapes, cost(1, 1)
    )


def finish_call(length, q_blocks, pieces, rows_true, gain, begun):
    rows = sum(q.shape[0] for q in q_blocks)
    shape = jax.ShapeDtypeStruct((rows, q_blocks[0].shape[1]), jnp.bfloat16)
    more = [gain, *begun]
    return attention(
        finish_kernel, "finish", length, q_blocks, pieces, rows_true, more, shape, cost(1, 1)
    )


def halve_kernel(whole_ref, top_ref, bottom_ref):
    rows = top_ref.shape[0]
    top_ref[...] = whole_ref[:rows]
    bottom_ref[...] = whole_ref[rows:]


def halve_call(whole):
    rows, width = whole.shape
    return pl.pallas_call(
        halve_kernel,
        out_shape=[jax.ShapeDtypeStruct((rows // 2, width), whole.dtype)] * 2,
        in_specs=[VMEM],
        out_specs=[VMEM] * 2,
        compiler_params=params(4),
        cost_estimate=cost(1, 1),
        name="halve",
    )(whole)


def cut_of(width):
    return width * 3 // 8 // HEAD_DIM * HEAD_DIM


def split_of(k, width):
    return [(0, width)] if k < 2 else [(0, cut_of(width)), (cut_of(width), width)]


def expert_kernel(
    origins, order, per_key, rows_true, last_ref, length_ref, done_ref, *refs
):
    pieces = len(origins)
    kv_refs = refs[:pieces]
    gain_ref, gate_ref, up_hbm, down_hbm = refs[pieces : pieces + 4]
    out_refs = refs[pieces + 4 : -4]
    x_ref, up_ref, down_ref, sems = refs[-4:]
    copies = [
        pltpu.make_async_copy(src, dst, sems.at[i])
        for i, (src, dst) in enumerate(
            ((up_hbm, up_ref), (down_hbm, down_ref))
        )
    ]
    for c in copies:
        c.start()
    bias = key_bias(length_ref, kv_refs, origins, rows_true)

    def queries(at, size):
        return last_ref[:, pl.ds(at, size)]

    def store(at, result):
        x_ref[:, pl.ds(at, HEAD_DIM)] = result

    attend(queries, kv_refs, bias, store, per_key)
    normed = jnp.concatenate([done_ref[...], norm(x_ref[...], gain_ref[...])], axis=0)
    gate = jnp.dot(normed, gate_ref[...], preferred_element_type=jnp.float32)
    copies[0].wait()
    up = jnp.dot(normed, up_ref[...], preferred_element_type=jnp.float32)
    hidden = (gate / (1.0 + jnp.exp(-gate)) * up).astype(jnp.bfloat16)
    copies[1].wait()
    part = jnp.dot(hidden, down_ref[...], preferred_element_type=jnp.float32).astype(
        jnp.bfloat16
    )
    each, width = last_ref.shape
    out = iter(out_refs)
    for i, k in enumerate(order):
        for begin, end in split_of(k, width):
            next(out)[...] = part[i * each : (i + 1) * each, begin:end]


def expert_call(length, done, last, pieces, gain, w_gate, w_up, w_down, order, rows_true):
    kv_pieces, origins = pieces
    each, width = last.shape
    rows = len(order) * each
    hidden = w_gate.shape[1]
    per_key = width // (kv_pieces[0].shape[1] // 2)
    splits = [split_of(k, width) for k in order]
    shapes = [
        jax.ShapeDtypeStruct((each, end - begin), jnp.bfloat16)
        for split in splits
        for begin, end in split
    ]
    outs = iter(
        pl.pallas_call(
            functools.partial(expert_kernel, tuple(origins), tuple(order), per_key, rows_true),
            out_shape=shapes,
            in_specs=[VMEM, SMEM] + [VMEM] * (3 + len(kv_pieces)) + [HBM] * 2,
            out_specs=[VMEM] * len(shapes),
            scratch_shapes=[
                pltpu.VMEM((each, width), jnp.bfloat16),
                pltpu.VMEM(w_up.shape, jnp.bfloat16),
                pltpu.VMEM(w_down.shape, jnp.bfloat16),
                pltpu.SemaphoreType.DMA((2,)),
            ],
            compiler_params=params(26 if rows * hidden < 1 << 17 else 44),
            cost_estimate=cost(6 * rows * width * hidden, 6 * width * hidden),
            name="experts",
        )(last, length, done, *kv_pieces, gain, w_gate, w_up, w_down)
    )
    return [[next(outs) for _ in split] for split in splits]


def add(*terms):
    total = terms[0].astype(jnp.float32)
    for t in terms[1:]:
        total = total + t.astype(jnp.float32)
    return total.astype(jnp.bfloat16)


def combine_kernel(
    late_ref, late_theirs_ref, comb_ref, attended_ref, mine_ref, theirs_ref, out_ref
):
    width = out_ref.shape[1]
    half = width - late_ref.shape[1]
    comb = comb_ref[...]
    high = comb.astype(jnp.bfloat16)
    low = (comb - high.astype(jnp.float32)).astype(jnp.bfloat16)
    both = (((0,), (0,)), ((), ()))

    def finish(rows, begin, end):
        rows = jnp.concatenate(rows, axis=0)
        added = lax.dot_general(
            high, rows, both, preferred_element_type=jnp.float32
        ) + lax.dot_general(low, rows, both, preferred_element_type=jnp.float32)
        out_ref[:, begin:end] = (
            attended_ref[:, begin:end].astype(jnp.float32) + added
        ).astype(jnp.bfloat16)

    finish([mine_ref[:, :half], theirs_ref[:, :half]], 0, half)
    finish(
        [
            add(mine_ref[:, half:], late_ref[...]),
            add(theirs_ref[:, half:], late_theirs_ref[...]),
        ],
        half,
        width,
    )


def across(x, stride):
    n = lax.axis_size("seq")
    return lax.ppermute(x, "seq", [(i, i ^ stride) for i in range(n)])


def swap(x):
    return lax.ppermute(x, "tp", [(0, 1), (1, 0)])


def across_and_swap(x, stride):
    n = lax.axis_size("seq")
    pairs = [
        (2 * i + c, 2 * (i ^ stride) + 1 - c) for i in range(n) for c in range(2)
    ]
    return lax.ppermute(x, ("seq", "tp"), pairs)


def in_hbm(x):
    return pltpu.with_memory_space_constraint(x, pltpu.HBM)


def tied(*values):
    return lax.optimization_barrier(values)


def body(
    queries, keys_values, prompt_lengths, routes, gate_weights, norm_gain, w_gate, w_up, w_down
):
    tokens, width = queries.shape[1:]
    rows_true = keys_values.shape[1]
    pad = -rows_true % TILE
    core = lax.axis_index("tp")
    own_queries = queries[0]
    strides = [1 << b for b in reversed(range(lax.axis_size("seq").bit_length() - 1))]

    kv = keys_values[0].reshape(rows_true, -1)
    if pad:
        kv = jnp.pad(kv, ((0, pad), (0, 0)))
    keep, send, comb = pl.pallas_call(
        pick_kernel,
        out_shape=[
            jax.ShapeDtypeStruct((CAP, width), jnp.bfloat16),
            jax.ShapeDtypeStruct((CAP, width), jnp.bfloat16),
            jax.ShapeDtypeStruct((2 * CAP, tokens), jnp.float32),
        ],
        in_specs=[SMEM] + [VMEM] * 3,
        out_specs=[VMEM] * 3,
        compiler_params=params(16),
        cost_estimate=cost(4 * CAP * tokens * width, 4 * tokens * width),
        name="pick",
    )(core.reshape(1), routes[0].T, gate_weights[0].T, own_queries)
    routed = jnp.concatenate([keep, swap(send)], axis=0)

    kv_blocks, routed_blocks, order = [kv], [routed], [0]
    for stride in strides[:-1]:
        kv_blocks = kv_blocks + [across(b, stride) for b in kv_blocks]
        routed_blocks = routed_blocks + [across(b, stride) for b in routed_blocks]
        order = order + [k ^ stride for k in order]
    first_kv, first_routed = across(kv, strides[-1]), across(routed, strides[-1])
    kv_blocks, routed_blocks, first_kv, first_routed = tied(
        kv_blocks, routed_blocks, first_kv, first_routed
    )
    last_kv = [across(b, strides[-1]) for b in kv_blocks[1:]]
    kv_blocks = kv_blocks + [first_kv] + last_kv
    order = order + [k ^ strides[-1] for k in order]
    rows = kv.shape[0]
    shares = 2 if rows % (2 * TILE) == 0 and not pad else 1
    cuts = range(0, rows, rows // shares)
    swapped = [swap(b) for b in kv_blocks[:-1]]

    origins = [(k, side, 0) for side in (0, 1) for k in order[:-1]]
    first_pieces = kv_blocks[:-1] + swapped, origins
    length = prompt_lengths

    early = routed_blocks + [first_routed]
    late_blocks = [across(b, strides[-1]) for b in routed_blocks[1:-1]]
    early += late_blocks
    *begun, mark = begin_call(length, early, first_pieces, rows_true)
    held_back, mark = tied(routed_blocks[-1], mark)
    last_routed = across(held_back, strides[-1])
    last, mark = tied(kv_blocks[-1], mark)
    halves = halve_call(last) if shares == 2 else [last]
    last_pieces = (
        [last] + [swap(h) for h in halves],
        [(order[-1], 0, 0)] + [(order[-1], 1, c) for c in cuts],
    )
    pieces = tuple(a + b for a, b in zip(first_pieces, last_pieces))

    gain = norm_gain.reshape(1, width)
    done = finish_call(length, early, last_pieces, rows_true, gain, [*begun, mark])
    parts = expert_call(
        length, done, last_routed, pieces, gain, w_gate[0], in_hbm(w_up[0]), in_hbm(w_down[0]),
        order, rows_true,
    )

    own_queries, parts = tied(own_queries, parts)
    attended = attend_call(length, own_queries, pieces, rows_true)
    parts = dict(zip(order, parts))
    straight = {k: v[0] for k, v in parts.items()}
    cut = cut_of(width)
    held = {k: v[-1][:, cut - width :] for k, v in parts.items()}
    for stride in strides[::-1][:-1]:
        sent = {k: across(v, stride) for k, v in held.items() if k & stride and k != 1}
        held = {
            k: add(v, sent[k ^ stride]) if k ^ stride in sent else v
            for k, v in held.items()
            if not k & stride
        }
    late, attended = tied(held[strides[0]], attended)
    late_mine = across(late[:CAP], strides[0])
    late_theirs = across_and_swap(late[CAP:], strides[0])
    straight[1], attended = tied(straight[1], attended)
    arrived = [across(v, k) for k, v in straight.items() if k]
    arrived, late = tied(arrived, late)
    so_far = [
        jnp.concatenate(
            [
                add(straight[0][rows, :cut], *[a[rows, :cut] for a in arrived]),
                add(
                    held[0][rows],
                    *[a[rows, cut:] for a in arrived if a.shape[1] == width],
                ),
            ],
            axis=1,
        )
        for rows in (slice(None, CAP), slice(CAP, None))
    ]
    theirs = swap(so_far[1])
    mixed = pl.pallas_call(
        combine_kernel,
        out_shape=jax.ShapeDtypeStruct((tokens, width), jnp.bfloat16),
        in_specs=[VMEM] * 6,
        out_specs=VMEM,
        compiler_params=params(16),
        cost_estimate=cost(8 * CAP * tokens * width, 4 * tokens * width),
        name="combine",
    )(late_mine, late_theirs, comb, attended, so_far[0], theirs)
    return mixed[None]


def solution(mesh):
    return jax.shard_map(
        body,
        mesh=mesh,
        in_specs=(
            P(("group", "exp"), ("seq", "tp"), None),
            P(("group", "exp"), ("seq", "tp"), None, None),
            P(("group", "exp")),
            P(("group", "exp"), ("seq", "tp"), None),
            P(("group", "exp"), ("seq", "tp"), None),
            P(),
            P("tp", None, "seq"),
            P("tp", None, "seq"),
            P("tp", "seq", None),
        ),
        out_specs=P(("group", "exp"), ("seq", "tp"), None),
        check_vma=False,
    )
```

```python
import functools
import math

import jax
import jax.numpy as jnp
from jax import lax
from jax.experimental import pallas as pl
from jax.experimental.pallas import tpu as pltpu
from jax.sharding import PartitionSpec as P

HEAD_DIM = 128
PROMPT = 256
CAP = 16
TILE = 16

epsilon = 1e-06
masked_score = -1e30
MIB = 1024 * 1024

VMEM = pl.BlockSpec(memory_space=pltpu.VMEM)
SMEM = pl.BlockSpec(memory_space=pltpu.SMEM)
HBM = pl.BlockSpec(memory_space=pltpu.HBM)


def params(mib):
    return pltpu.CompilerParams(vmem_limit_bytes=mib * MIB)


def cost(flops, moved, transcendentals=0):
    return pl.CostEstimate(
        flops=int(flops), bytes_accessed=int(moved), transcendentals=int(transcendentals)
    )


def pick_kernel(me_ref, routes_ref, gates_ref, q_ref, keep_ref, send_ref, comb_ref):
    top, tokens = routes_ref.shape
    me = me_ref[0]
    routes = routes_ref[...]
    gates = gates_ref[...]

    def of_expert(expert):
        hit = routes == expert
        member = jnp.sum(hit.astype(jnp.float32), axis=0, keepdims=True)
        weight = jnp.sum(jnp.where(hit, gates, 0.0), axis=0, keepdims=True)
        return member, weight

    member_a, weight_a = of_expert(me)
    member_b, weight_b = of_expert(1 - me)
    slot_of = lax.broadcasted_iota(jnp.int32, (2 * CAP, tokens), 0)
    mine = slot_of < CAP
    member = jnp.where(mine, member_a, member_b)
    weight = jnp.where(mine, weight_a, weight_b)
    row = lax.broadcasted_iota(jnp.int32, (tokens, tokens), 0)
    col = lax.broadcasted_iota(jnp.int32, (tokens, tokens), 1)
    before = jnp.where(row < col, 1.0, 0.0).astype(jnp.bfloat16)
    slot = jnp.dot(member.astype(jnp.bfloat16), before, preferred_element_type=jnp.float32)
    wanted = jnp.where(mine, slot_of, slot_of - CAP).astype(jnp.float32)
    taken = jnp.where((member > 0.0) & (slot == wanted), 1.0, 0.0)
    comb_ref[...] = taken * weight
    rows = jnp.dot(
        taken.astype(jnp.bfloat16), q_ref[...], preferred_element_type=jnp.float32
    ).astype(jnp.bfloat16)
    keep_ref[...] = rows[:CAP]
    send_ref[...] = rows[CAP:]


def key_bias(length_ref, kv_refs, origins, rows_true):
    seq, core = lax.axis_index("seq"), lax.axis_index("tp")
    length = length_ref[0]
    parts = []
    for r, (k, side, first) in zip(kv_refs, origins):
        row = lax.broadcasted_iota(jnp.int32, (8, r.shape[0]), 1) + first
        position = row + (2 * (seq ^ k) + (core ^ side)) * rows_true
        allowed = (position >= PROMPT) | (position < length)
        allowed = allowed & (row < rows_true)
        parts.append(jnp.where(allowed, 0.0, masked_score))
    return jnp.concatenate(parts, axis=1)[:1]


def attend(queries, kv_refs, bias, store, per_key, before=None, after=None):
    width = kv_refs[0].shape[1] // 2
    heads = width // HEAD_DIM
    factor = math.log2(math.e) / math.sqrt(HEAD_DIM)

    def one(head, _):
        at = head * HEAD_DIM
        if not isinstance(head, int):
            at = pl.multiple_of(at, HEAD_DIM)
        keys = jnp.concatenate([r[:, pl.ds(at, HEAD_DIM)] for r in kv_refs], axis=0)
        values = jnp.concatenate(
            [r[:, pl.ds(width + at, HEAD_DIM)] for r in kv_refs], axis=0
        )
        values = jnp.concatenate([values, jnp.ones_like(values)], axis=1)
        block = queries(at * per_key, per_key * HEAD_DIM)
        rows = block.shape[0]
        stacked = jnp.concatenate(
            [block[:, j * HEAD_DIM : (j + 1) * HEAD_DIM] for j in range(per_key)], axis=0
        )
        scores = (
            lax.dot_general(
                stacked, keys, (((1,), (1,)), ((), ())), preferred_element_type=jnp.float32
            )
            * factor
            + bias
        )
        largest = jnp.max(scores, axis=1, keepdims=True)
        mine = pl.ds(head * per_key * rows, per_key * rows)
        if before is not None:
            earlier = before[1][mine, :]
            largest = jnp.maximum(earlier, largest)
            scale = jnp.exp2(earlier - largest)
            count = -(-scores.shape[1] // HEAD_DIM)
            largest = jnp.concatenate([largest] * count, axis=1)[:, : scores.shape[1]]
        weights = jnp.exp2(scores - largest)
        summed = jnp.dot(
            weights.astype(jnp.bfloat16), values, preferred_element_type=jnp.float32
        )
        if before is not None:
            summed = summed + before[0][mine, :] * jnp.concatenate([scale, scale], axis=1)
        if after is not None:
            after[0][mine, :] = summed
            after[1][mine, :] = jnp.broadcast_to(largest, (per_key * rows, HEAD_DIM))
            return
        result = (summed[:, :HEAD_DIM] / summed[:, HEAD_DIM:]).astype(jnp.bfloat16)
        for j in range(per_key):
            store(at * per_key + j * HEAD_DIM, result[j * rows : (j + 1) * rows])

    if bias.shape[1] > 1024:
        lax.fori_loop(0, heads, one, None)
    else:
        for head in range(heads):
            one(head, None)


def norm(rows, gain):
    x = rows.astype(jnp.float32)
    square = jnp.mean(x * x, axis=1, keepdims=True)
    return (x * lax.rsqrt(square + epsilon) * gain).astype(jnp.bfloat16)


def columns_of(q_refs):
    def queries(at, size):
        return jnp.concatenate([r[:, pl.ds(at, size)] for r in q_refs], axis=0)

    return queries


def into(ref):
    def store(at, result):
        ref[:, pl.ds(at, HEAD_DIM)] = result

    return store


def attended_rows(queries, kv_refs, bias, scratch_ref, per_key, before=None):
    parts = []
    if bias.shape[1] > 1024:
        attend(queries, kv_refs, bias, into(scratch_ref), per_key, before)
        return scratch_ref[...]
    attend(queries, kv_refs, bias, lambda at, result: parts.append(result), per_key, before)
    return jnp.concatenate(parts, axis=1)


def attend_kernel(origins, per_key, rows_true, length_ref, q_ref, *refs):
    kv_refs = refs[: len(origins)]
    bias = key_bias(length_ref, kv_refs, origins, rows_true)
    attend(columns_of([q_ref]), kv_refs, bias, into(refs[-1]), per_key)


def begin_kernel(origins, per_key, rows_true, length_ref, *refs):
    pieces = len(origins)
    kv_refs, after, mark_ref = refs[-pieces - 3 : -3], refs[-3:-1], refs[-1]
    bias = key_bias(length_ref, kv_refs, origins, rows_true)
    attend(columns_of(refs[: -pieces - 3]), kv_refs, bias, None, per_key, after=after)
    mark_ref[...] = jnp.zeros_like(mark_ref)


def finish_kernel(origins, per_key, rows_true, length_ref, *refs):
    pieces = len(origins)
    gain_ref, sums_ref, largest_ref, _, out_ref = refs[-5:]
    kv_refs = refs[-pieces - 5 : -5]
    bias = key_bias(length_ref, kv_refs, origins, rows_true)
    queries = columns_of(refs[: -pieces - 5])
    state = sums_ref, largest_ref
    rows = attended_rows(queries, kv_refs, bias, out_ref, per_key, state)
    out_ref[...] = norm(rows, gain_ref[...])


def attention(kernel, name, length, q_blocks, pieces, rows_true, more, out_shape, price):
    kv_pieces, origins = pieces
    per_key = q_blocks[0].shape[1] // (kv_pieces[0].shape[1] // 2)
    large = sum(q.shape[0] for q in q_blocks) * sum(p.shape[0] for p in kv_pieces)
    count = len(q_blocks) + len(kv_pieces) + len(more)
    return pl.pallas_call(
        functools.partial(kernel, tuple(origins), per_key, rows_true),
        out_shape=out_shape,
        in_specs=[SMEM] + [VMEM] * count,
        out_specs=jax.tree.map(lambda _: VMEM, out_shape),
        compiler_params=params(20 if large < 1 << 17 else 58),
        cost_estimate=price,
        name=name,
    )(length, *q_blocks, *kv_pieces, *more)


def attend_call(length, queries, pieces, rows_true):
    rows, width = queries.shape
    keys = sum(p.shape[0] for p in pieces[0])
    shape = jax.ShapeDtypeStruct((rows, width), jnp.bfloat16)
    price = cost(
        4 * rows * width * keys,
        4 * rows * width + 2 * keys * pieces[0][0].shape[1],
        rows * keys * width // HEAD_DIM,
    )
    return attention(
        attend_kernel, "attend", length, [queries], pieces, rows_true, [], shape, price
    )


def begin_call(length, q_blocks, pieces, rows_true):
    rows = sum(q.shape[0] for q in q_blocks) * q_blocks[0].shape[1] // HEAD_DIM
    shapes = [
        jax.ShapeDtypeStruct((rows, 2 * HEAD_DIM), jnp.float32),
        jax.ShapeDtypeStruct((rows, HEAD_DIM), jnp.float32),
        jax.ShapeDtypeStruct((8, HEAD_DIM), jnp.float32),
    ]
    return attention(
        begin_kernel, "begin", length, q_blocks, pieces, rows_true, [], shapes, cost(1, 1)
    )


def finish_call(length, q_blocks, pieces, rows_true, gain, begun):
    rows = sum(q.shape[0] for q in q_blocks)
    shape = jax.ShapeDtypeStruct((rows, q_blocks[0].shape[1]), jnp.bfloat16)
    more = [gain, *begun]
    return attention(
        finish_kernel, "finish", length, q_blocks, pieces, rows_true, more, shape, cost(1, 1)
    )


def halve_kernel(whole_ref, top_ref, bottom_ref):
    rows = top_ref.shape[0]
    top_ref[...] = whole_ref[:rows]
    bottom_ref[...] = whole_ref[rows:]


def halve_call(whole):
    rows, width = whole.shape
    return pl.pallas_call(
        halve_kernel,
        out_shape=[jax.ShapeDtypeStruct((rows // 2, width), whole.dtype)] * 2,
        in_specs=[VMEM],
        out_specs=[VMEM] * 2,
        compiler_params=params(4),
        cost_estimate=cost(1, 1),
        name="halve",
    )(whole)


def cut_of(width):
    return width * 3 // 8 // HEAD_DIM * HEAD_DIM


def split_of(k, width):
    return [(0, width)] if k < 2 else [(0, cut_of(width)), (cut_of(width), width)]


def expert_kernel(
    origins, order, per_key, rows_true, last_ref, length_ref, done_ref, *refs
):
    pieces = len(origins)
    kv_refs = refs[:pieces]
    gain_ref, gate_ref, up_hbm, down_hbm = refs[pieces : pieces + 4]
    out_refs = refs[pieces + 4 : -4]
    x_ref, up_ref, down_ref, sems = refs[-4:]
    copies = [
        pltpu.make_async_copy(src, dst, sems.at[i])
        for i, (src, dst) in enumerate(
            ((up_hbm, up_ref), (down_hbm, down_ref))
        )
    ]
    for c in copies:
        c.start()
    bias = key_bias(length_ref, kv_refs, origins, rows_true)

    last = attended_rows(columns_of([last_ref]), kv_refs, bias, x_ref, per_key)
    normed = jnp.concatenate([done_ref[...], norm(last, gain_ref[...])], axis=0)
    gate = jnp.dot(normed, gate_ref[...], preferred_element_type=jnp.float32)
    copies[0].wait()
    up = jnp.dot(normed, up_ref[...], preferred_element_type=jnp.float32)
    hidden = (gate / (1.0 + jnp.exp(-gate)) * up).astype(jnp.bfloat16)
    copies[1].wait()
    part = jnp.dot(hidden, down_ref[...], preferred_element_type=jnp.float32).astype(
        jnp.bfloat16
    )
    each, width = last_ref.shape
    out = iter(out_refs)
    for i, k in enumerate(order):
        for begin, end in split_of(k, width):
            next(out)[...] = part[i * each : (i + 1) * each, begin:end]


def expert_call(length, done, last, pieces, gain, w_gate, w_up, w_down, order, rows_true):
    kv_pieces, origins = pieces
    each, width = last.shape
    rows = len(order) * each
    hidden = w_gate.shape[1]
    per_key = width // (kv_pieces[0].shape[1] // 2)
    splits = [split_of(k, width) for k in order]
    shapes = [
        jax.ShapeDtypeStruct((each, end - begin), jnp.bfloat16)
        for split in splits
        for begin, end in split
    ]
    outs = iter(
        pl.pallas_call(
            functools.partial(expert_kernel, tuple(origins), tuple(order), per_key, rows_true),
            out_shape=shapes,
            in_specs=[VMEM, SMEM] + [VMEM] * (3 + len(kv_pieces)) + [HBM] * 2,
            out_specs=[VMEM] * len(shapes),
            scratch_shapes=[
                pltpu.VMEM((each, width), jnp.bfloat16),
                pltpu.VMEM(w_up.shape, jnp.bfloat16),
                pltpu.VMEM(w_down.shape, jnp.bfloat16),
                pltpu.SemaphoreType.DMA((2,)),
            ],
            compiler_params=params(26 if rows * hidden < 1 << 17 else 44),
            cost_estimate=cost(6 * rows * width * hidden, 6 * width * hidden),
            name="experts",
        )(last, length, done, *kv_pieces, gain, w_gate, w_up, w_down)
    )
    return [[next(outs) for _ in split] for split in splits]


def add(*terms):
    total = terms[0].astype(jnp.float32)
    for t in terms[1:]:
        total = total + t.astype(jnp.float32)
    return total.astype(jnp.bfloat16)


def combine_kernel(
    late_ref, late_theirs_ref, comb_ref, attended_ref, mine_ref, theirs_ref, out_ref
):
    width = out_ref.shape[1]
    half = width - late_ref.shape[1]
    comb = comb_ref[...]
    high = comb.astype(jnp.bfloat16)
    low = (comb - high.astype(jnp.float32)).astype(jnp.bfloat16)
    both = (((0,), (0,)), ((), ()))

    def finish(rows, begin, end):
        rows = jnp.concatenate(rows, axis=0)
        added = lax.dot_general(
            high, rows, both, preferred_element_type=jnp.float32
        ) + lax.dot_general(low, rows, both, preferred_element_type=jnp.float32)
        out_ref[:, begin:end] = (
            attended_ref[:, begin:end].astype(jnp.float32) + added
        ).astype(jnp.bfloat16)

    finish([mine_ref[:, :half], theirs_ref[:, :half]], 0, half)
    finish(
        [
            add(mine_ref[:, half:], late_ref[...]),
            add(theirs_ref[:, half:], late_theirs_ref[...]),
        ],
        half,
        width,
    )


def across(x, stride):
    n = lax.axis_size("seq")
    return lax.ppermute(x, "seq", [(i, i ^ stride) for i in range(n)])


def swap(x):
    return lax.ppermute(x, "tp", [(0, 1), (1, 0)])


def across_and_swap(x, stride):
    n = lax.axis_size("seq")
    pairs = [
        (2 * i + c, 2 * (i ^ stride) + 1 - c) for i in range(n) for c in range(2)
    ]
    return lax.ppermute(x, ("seq", "tp"), pairs)


def in_hbm(x):
    return pltpu.with_memory_space_constraint(x, pltpu.HBM)


def tied(*values):
    return lax.optimization_barrier(values)


def body(
    queries, keys_values, prompt_lengths, routes, gate_weights, norm_gain, w_gate, w_up, w_down
):
    tokens, width = queries.shape[1:]
    rows_true = keys_values.shape[1]
    pad = -rows_true % TILE
    core = lax.axis_index("tp")
    own_queries = queries[0]
    strides = [1 << b for b in reversed(range(lax.axis_size("seq").bit_length() - 1))]

    kv = keys_values[0].reshape(rows_true, -1)
    if pad:
        kv = jnp.pad(kv, ((0, pad), (0, 0)))
    keep, send, comb = pl.pallas_call(
        pick_kernel,
        out_shape=[
            jax.ShapeDtypeStruct((CAP, width), jnp.bfloat16),
            jax.ShapeDtypeStruct((CAP, width), jnp.bfloat16),
            jax.ShapeDtypeStruct((2 * CAP, tokens), jnp.float32),
        ],
        in_specs=[SMEM] + [VMEM] * 3,
        out_specs=[VMEM] * 3,
        compiler_params=params(16),
        cost_estimate=cost(4 * CAP * tokens * width, 4 * tokens * width),
        name="pick",
    )(core.reshape(1), routes[0].T, gate_weights[0].T, own_queries)
    routed = jnp.concatenate([keep, swap(send)], axis=0)

    kv_blocks, routed_blocks, order = [kv], [routed], [0]
    for stride in strides[:-1]:
        kv_blocks = kv_blocks + [across(b, stride) for b in kv_blocks]
        routed_blocks = routed_blocks + [across(b, stride) for b in routed_blocks]
        order = order + [k ^ stride for k in order]
    first_kv, first_routed = across(kv, strides[-1]), across(routed, strides[-1])
    own_swapped = swap(kv)
    kv_blocks, routed_blocks, first_kv, own_swapped, first_routed = tied(
        kv_blocks, routed_blocks, first_kv, own_swapped, first_routed
    )
    last_kv = [across(b, strides[-1]) for b in kv_blocks[1:]]
    kv_blocks = kv_blocks + [first_kv] + last_kv
    order = order + [k ^ strides[-1] for k in order]
    rows = kv.shape[0]
    shares = 2 if rows % (2 * TILE) == 0 and not pad else 1
    cuts = range(0, rows, rows // shares)
    swapped = [own_swapped] + [swap(b) for b in kv_blocks[1:-1]]

    origins = [(k, side, 0) for side in (0, 1) for k in order[:-1]]
    first_pieces = kv_blocks[:-1] + swapped, origins
    length = prompt_lengths

    early = routed_blocks + [first_routed]
    late_blocks = [across(b, strides[-1]) for b in routed_blocks[1:-1]]
    early += late_blocks
    *begun, mark = begin_call(length, early, first_pieces, rows_true)
    held_back, mark = tied(routed_blocks[-1], mark)
    last_routed = across(held_back, strides[-1])
    last, mark = tied(kv_blocks[-1], mark)
    halves = halve_call(last) if shares == 2 else [last]
    last_pieces = (
        [last] + [swap(h) for h in halves],
        [(order[-1], 0, 0)] + [(order[-1], 1, c) for c in cuts],
    )
    pieces = tuple(a + b for a, b in zip(first_pieces, last_pieces))

    gain = norm_gain.reshape(1, width)
    done = finish_call(length, early, last_pieces, rows_true, gain, [*begun, mark])
    parts = expert_call(
        length, done, last_routed, pieces, gain, w_gate[0], in_hbm(w_up[0]), in_hbm(w_down[0]),
        order, rows_true,
    )

    own_queries, parts = tied(own_queries, parts)
    attended = attend_call(length, own_queries, pieces, rows_true)
    parts = dict(zip(order, parts))
    straight = {k: v[0] for k, v in parts.items()}
    cut = cut_of(width)
    held = {k: v[-1][:, cut - width :] for k, v in parts.items()}
    for stride in strides[::-1][:-1]:
        sent = {k: across(v, stride) for k, v in held.items() if k & stride and k != 1}
        held = {
            k: add(v, sent[k ^ stride]) if k ^ stride in sent else v
            for k, v in held.items()
            if not k & stride
        }
    late, attended = tied(held[strides[0]], attended)
    late_mine = across(late[:CAP], strides[0])
    late_theirs = across_and_swap(late[CAP:], strides[0])
    straight[1], attended = tied(straight[1], attended)
    arrived = [across(v, k) for k, v in straight.items() if k]
    arrived, late = tied(arrived, late)
    so_far = [
        jnp.concatenate(
            [
                add(straight[0][rows, :cut], *[a[rows, :cut] for a in arrived]),
                add(
                    held[0][rows],
                    *[a[rows, cut:] for a in arrived if a.shape[1] == width],
                ),
            ],
            axis=1,
        )
        for rows in (slice(None, CAP), slice(CAP, None))
    ]
    theirs = swap(so_far[1])
    mixed = pl.pallas_call(
        combine_kernel,
        out_shape=jax.ShapeDtypeStruct((tokens, width), jnp.bfloat16),
        in_specs=[VMEM] * 6,
        out_specs=VMEM,
        compiler_params=params(16),
        cost_estimate=cost(8 * CAP * tokens * width, 4 * tokens * width),
        name="combine",
    )(late_mine, late_theirs, comb, attended, so_far[0], theirs)
    return mixed[None]


def solution(mesh):
    return jax.shard_map(
        body,
        mesh=mesh,
        in_specs=(
            P(("group", "exp"), ("seq", "tp"), None),
            P(("group", "exp"), ("seq", "tp"), None, None),
            P(("group", "exp")),
            P(("group", "exp"), ("seq", "tp"), None),
            P(("group", "exp"), ("seq", "tp"), None),
            P(),
            P("tp", None, "seq"),
            P("tp", None, "seq"),
            P("tp", "seq", None),
        ),
        out_specs=P(("group", "exp"), ("seq", "tp"), None),
        check_vma=False,
    )
```

```python
import functools
import math

import jax
import jax.numpy as jnp
from jax import lax
from jax.experimental import pallas as pl
from jax.experimental.pallas import tpu as pltpu
from jax.sharding import PartitionSpec as P

HEAD_DIM = 128
PROMPT = 256
CAP = 16
TILE = 16

epsilon = 1e-06
masked_score = -1e30
MIB = 1024 * 1024

VMEM = pl.BlockSpec(memory_space=pltpu.VMEM)
SMEM = pl.BlockSpec(memory_space=pltpu.SMEM)
HBM = pl.BlockSpec(memory_space=pltpu.HBM)


def params(mib):
    return pltpu.CompilerParams(vmem_limit_bytes=mib * MIB)


def cost(flops, moved, transcendentals=0):
    return pl.CostEstimate(
        flops=int(flops), bytes_accessed=int(moved), transcendentals=int(transcendentals)
    )


def pick_kernel(me_ref, routes_ref, gates_ref, q_ref, keep_ref, send_ref, comb_ref):
    top, tokens = routes_ref.shape
    me = me_ref[0]
    routes = routes_ref[...]
    gates = gates_ref[...]

    def of_expert(expert):
        hit = routes == expert
        member = jnp.sum(hit.astype(jnp.float32), axis=0, keepdims=True)
        weight = jnp.sum(jnp.where(hit, gates, 0.0), axis=0, keepdims=True)
        return member, weight

    member_a, weight_a = of_expert(me)
    member_b, weight_b = of_expert(1 - me)
    slot_of = lax.broadcasted_iota(jnp.int32, (2 * CAP, tokens), 0)
    mine = slot_of < CAP
    member = jnp.where(mine, member_a, member_b)
    weight = jnp.where(mine, weight_a, weight_b)
    row = lax.broadcasted_iota(jnp.int32, (tokens, tokens), 0)
    col = lax.broadcasted_iota(jnp.int32, (tokens, tokens), 1)
    before = jnp.where(row < col, 1.0, 0.0).astype(jnp.bfloat16)
    slot = jnp.dot(member.astype(jnp.bfloat16), before, preferred_element_type=jnp.float32)
    wanted = jnp.where(mine, slot_of, slot_of - CAP).astype(jnp.float32)
    taken = jnp.where((member > 0.0) & (slot == wanted), 1.0, 0.0)
    comb_ref[...] = taken * weight
    rows = jnp.dot(
        taken.astype(jnp.bfloat16), q_ref[...], preferred_element_type=jnp.float32
    ).astype(jnp.bfloat16)
    keep_ref[...] = rows[:CAP]
    send_ref[...] = rows[CAP:]


def key_bias(length_ref, kv_refs, origins, rows_true):
    seq, core = lax.axis_index("seq"), lax.axis_index("tp")
    length = length_ref[0]
    parts = []
    for r, (k, side, first) in zip(kv_refs, origins):
        row = lax.broadcasted_iota(jnp.int32, (8, r.shape[0]), 1) + first
        position = row + (2 * (seq ^ k) + (core ^ side)) * rows_true
        allowed = (position >= PROMPT) | (position < length)
        allowed = allowed & (row < rows_true)
        parts.append(jnp.where(allowed, 0.0, masked_score))
    return jnp.concatenate(parts, axis=1)[:1]


def attend(queries, kv_refs, bias, store, per_key, before=None, after=None):
    width = kv_refs[0].shape[1] // 2
    heads = width // HEAD_DIM
    factor = math.log2(math.e) / math.sqrt(HEAD_DIM)

    def one(head, _):
        at = head * HEAD_DIM
        if not isinstance(head, int):
            at = pl.multiple_of(at, HEAD_DIM)
        keys = jnp.concatenate([r[:, pl.ds(at, HEAD_DIM)] for r in kv_refs], axis=0)
        values = jnp.concatenate(
            [r[:, pl.ds(width + at, HEAD_DIM)] for r in kv_refs], axis=0
        )
        values = jnp.concatenate([values, jnp.ones_like(values)], axis=1)
        block = queries(at * per_key, per_key * HEAD_DIM)
        rows = block.shape[0]
        stacked = jnp.concatenate(
            [block[:, j * HEAD_DIM : (j + 1) * HEAD_DIM] for j in range(per_key)], axis=0
        )
        scores = (
            lax.dot_general(
                stacked, keys, (((1,), (1,)), ((), ())), preferred_element_type=jnp.float32
            )
            * factor
            + bias
        )
        largest = jnp.max(scores, axis=1, keepdims=True)
        mine = pl.ds(head * per_key * rows, per_key * rows)
        if before is not None:
            earlier = before[1][mine, :]
            largest = jnp.maximum(earlier, largest)
            scale = jnp.exp2(earlier - largest)
            count = -(-scores.shape[1] // HEAD_DIM)
            largest = jnp.concatenate([largest] * count, axis=1)[:, : scores.shape[1]]
        weights = jnp.exp2(scores - largest)
        summed = jnp.dot(
            weights.astype(jnp.bfloat16), values, preferred_element_type=jnp.float32
        )
        if before is not None:
            summed = summed + before[0][mine, :] * jnp.concatenate([scale, scale], axis=1)
        if after is not None:
            after[0][mine, :] = summed
            after[1][mine, :] = jnp.broadcast_to(largest, (per_key * rows, HEAD_DIM))
            return
        result = (summed[:, :HEAD_DIM] / summed[:, HEAD_DIM:]).astype(jnp.bfloat16)
        for j in range(per_key):
            store(at * per_key + j * HEAD_DIM, result[j * rows : (j + 1) * rows])

    if bias.shape[1] > 1024:
        lax.fori_loop(0, heads, one, None)
    else:
        for head in range(heads):
            one(head, None)


def norm(rows, gain):
    x = rows.astype(jnp.float32)
    square = jnp.mean(x * x, axis=1, keepdims=True)
    return (x * lax.rsqrt(square + epsilon) * gain).astype(jnp.bfloat16)


def columns_of(q_refs):
    def queries(at, size):
        return jnp.concatenate([r[:, pl.ds(at, size)] for r in q_refs], axis=0)

    return queries


def into(ref):
    def store(at, result):
        ref[:, pl.ds(at, HEAD_DIM)] = result

    return store


def attended_rows(queries, kv_refs, bias, scratch_ref, per_key, before=None):
    parts = []
    if bias.shape[1] > 1024:
        attend(queries, kv_refs, bias, into(scratch_ref), per_key, before)
        return scratch_ref[...]
    attend(queries, kv_refs, bias, lambda at, result: parts.append(result), per_key, before)
    return jnp.concatenate(parts, axis=1)


def attend_kernel(origins, per_key, rows_true, length_ref, q_ref, *refs):
    kv_refs = refs[: len(origins)]
    bias = key_bias(length_ref, kv_refs, origins, rows_true)
    attend(columns_of([q_ref]), kv_refs, bias, into(refs[-1]), per_key)


def begin_kernel(origins, per_key, rows_true, length_ref, *refs):
    pieces = len(origins)
    kv_refs, after, mark_ref = refs[-pieces - 3 : -3], refs[-3:-1], refs[-1]
    bias = key_bias(length_ref, kv_refs, origins, rows_true)
    attend(columns_of(refs[: -pieces - 3]), kv_refs, bias, None, per_key, after=after)
    mark_ref[...] = jnp.zeros_like(mark_ref)


def finish_kernel(origins, per_key, rows_true, length_ref, *refs):
    pieces = len(origins)
    gain_ref, sums_ref, largest_ref, _, out_ref = refs[-5:]
    kv_refs = refs[-pieces - 5 : -5]
    bias = key_bias(length_ref, kv_refs, origins, rows_true)
    queries = columns_of(refs[: -pieces - 5])
    state = sums_ref, largest_ref
    rows = attended_rows(queries, kv_refs, bias, out_ref, per_key, state)
    out_ref[...] = norm(rows, gain_ref[...])


def attention(kernel, name, length, q_blocks, pieces, rows_true, more, out_shape, price):
    kv_pieces, origins = pieces
    per_key = q_blocks[0].shape[1] // (kv_pieces[0].shape[1] // 2)
    large = sum(q.shape[0] for q in q_blocks) * sum(p.shape[0] for p in kv_pieces)
    count = len(q_blocks) + len(kv_pieces) + len(more)
    return pl.pallas_call(
        functools.partial(kernel, tuple(origins), per_key, rows_true),
        out_shape=out_shape,
        in_specs=[SMEM] + [VMEM] * count,
        out_specs=jax.tree.map(lambda _: VMEM, out_shape),
        compiler_params=params(20 if large < 1 << 17 else 58),
        cost_estimate=price,
        name=name,
    )(length, *q_blocks, *kv_pieces, *more)


def attend_call(length, queries, pieces, rows_true):
    rows, width = queries.shape
    keys = sum(p.shape[0] for p in pieces[0])
    shape = jax.ShapeDtypeStruct((rows, width), jnp.bfloat16)
    price = cost(
        4 * rows * width * keys,
        4 * rows * width + 2 * keys * pieces[0][0].shape[1],
        rows * keys * width // HEAD_DIM,
    )
    return attention(
        attend_kernel, "attend", length, [queries], pieces, rows_true, [], shape, price
    )


def begin_call(length, q_blocks, pieces, rows_true):
    rows = sum(q.shape[0] for q in q_blocks) * q_blocks[0].shape[1] // HEAD_DIM
    shapes = [
        jax.ShapeDtypeStruct((rows, 2 * HEAD_DIM), jnp.float32),
        jax.ShapeDtypeStruct((rows, HEAD_DIM), jnp.float32),
        jax.ShapeDtypeStruct((8, HEAD_DIM), jnp.float32),
    ]
    return attention(
        begin_kernel, "begin", length, q_blocks, pieces, rows_true, [], shapes, cost(1, 1)
    )


def finish_call(length, q_blocks, pieces, rows_true, gain, begun):
    rows = sum(q.shape[0] for q in q_blocks)
    shape = jax.ShapeDtypeStruct((rows, q_blocks[0].shape[1]), jnp.bfloat16)
    more = [gain, *begun]
    return attention(
        finish_kernel, "finish", length, q_blocks, pieces, rows_true, more, shape, cost(1, 1)
    )


def halve_kernel(whole_ref, top_ref, bottom_ref):
    rows = top_ref.shape[0]
    top_ref[...] = whole_ref[:rows]
    bottom_ref[...] = whole_ref[rows:]


def halve_call(whole):
    rows, width = whole.shape
    return pl.pallas_call(
        halve_kernel,
        out_shape=[jax.ShapeDtypeStruct((rows // 2, width), whole.dtype)] * 2,
        in_specs=[VMEM],
        out_specs=[VMEM] * 2,
        compiler_params=params(4),
        cost_estimate=cost(1, 1),
        name="halve",
    )(whole)


def cut_of(width):
    return width * 3 // 8 // HEAD_DIM * HEAD_DIM


def split_of(k, width):
    return [(0, width)] if k < 2 else [(0, cut_of(width)), (cut_of(width), width)]


def expert_kernel(
    origins, order, per_key, rows_true, last_ref, length_ref, done_ref, *refs
):
    pieces = len(origins)
    kv_refs = refs[:pieces]
    gain_ref, gate_ref, up_hbm, down_hbm = refs[pieces : pieces + 4]
    out_refs = refs[pieces + 4 : -4]
    x_ref, up_ref, down_ref, sems = refs[-4:]
    copies = [
        pltpu.make_async_copy(src, dst, sems.at[i])
        for i, (src, dst) in enumerate(
            ((up_hbm, up_ref), (down_hbm, down_ref))
        )
    ]
    for c in copies:
        c.start()
    bias = key_bias(length_ref, kv_refs, origins, rows_true)

    last = attended_rows(columns_of([last_ref]), kv_refs, bias, x_ref, per_key)
    normed = jnp.concatenate([done_ref[...], norm(last, gain_ref[...])], axis=0)
    gate = jnp.dot(normed, gate_ref[...], preferred_element_type=jnp.float32)
    copies[0].wait()
    up = jnp.dot(normed, up_ref[...], preferred_element_type=jnp.float32)
    hidden = (gate / (1.0 + jnp.exp(-gate)) * up).astype(jnp.bfloat16)
    copies[1].wait()
    part = jnp.dot(hidden, down_ref[...], preferred_element_type=jnp.float32).astype(
        jnp.bfloat16
    )
    each, width = last_ref.shape
    out = iter(out_refs)
    for i, k in enumerate(order):
        for begin, end in split_of(k, width):
            next(out)[...] = part[i * each : (i + 1) * each, begin:end]


def expert_call(length, done, last, pieces, gain, w_gate, w_up, w_down, order, rows_true):
    kv_pieces, origins = pieces
    each, width = last.shape
    rows = len(order) * each
    hidden = w_gate.shape[1]
    per_key = width // (kv_pieces[0].shape[1] // 2)
    splits = [split_of(k, width) for k in order]
    shapes = [
        jax.ShapeDtypeStruct((each, end - begin), jnp.bfloat16)
        for split in splits
        for begin, end in split
    ]
    outs = iter(
        pl.pallas_call(
            functools.partial(expert_kernel, tuple(origins), tuple(order), per_key, rows_true),
            out_shape=shapes,
            in_specs=[VMEM, SMEM] + [VMEM] * (3 + len(kv_pieces)) + [HBM] * 2,
            out_specs=[VMEM] * len(shapes),
            scratch_shapes=[
                pltpu.VMEM((each, width), jnp.bfloat16),
                pltpu.VMEM(w_up.shape, jnp.bfloat16),
                pltpu.VMEM(w_down.shape, jnp.bfloat16),
                pltpu.SemaphoreType.DMA((2,)),
            ],
            compiler_params=params(26 if rows * hidden < 1 << 17 else 44),
            cost_estimate=cost(6 * rows * width * hidden, 6 * width * hidden),
            name="experts",
        )(last, length, done, *kv_pieces, gain, w_gate, w_up, w_down)
    )
    return [[next(outs) for _ in split] for split in splits]


def add(*terms):
    total = terms[0].astype(jnp.float32)
    for t in terms[1:]:
        total = total + t.astype(jnp.float32)
    return total.astype(jnp.bfloat16)


def weighted(comb_ref, first, rows):
    comb = comb_ref[first : first + CAP, :]
    high = comb.astype(jnp.bfloat16)
    low = (comb - high.astype(jnp.float32)).astype(jnp.bfloat16)
    both = (((0,), (0,)), ((), ()))
    return lax.dot_general(
        high, rows, both, preferred_element_type=jnp.float32
    ) + lax.dot_general(low, rows, both, preferred_element_type=jnp.float32)


def mix_kernel(first, late_ref, comb_ref, base_ref, sums_ref, out_ref):
    width = out_ref.shape[1]
    half = width - late_ref.shape[1]
    for columns, rows in (
        (slice(0, half), sums_ref[:, :half]),
        (slice(half, width), add(sums_ref[:, half:], late_ref[...])),
    ):
        out_ref[:, columns] = (
            base_ref[:, columns].astype(jnp.float32) + weighted(comb_ref, first, rows)
        ).astype(out_ref.dtype)


def mix_call(first, late, comb, base, sums, dtype):
    return pl.pallas_call(
        functools.partial(mix_kernel, first),
        out_shape=jax.ShapeDtypeStruct(base.shape, dtype),
        in_specs=[VMEM] * 4,
        out_specs=VMEM,
        compiler_params=params(16),
        cost_estimate=cost(1, 1),
        name="mix",
    )(late, comb, base, sums)


def across(x, stride):
    n = lax.axis_size("seq")
    return lax.ppermute(x, "seq", [(i, i ^ stride) for i in range(n)])


def swap(x):
    return lax.ppermute(x, "tp", [(0, 1), (1, 0)])


def across_and_swap(x, stride):
    n = lax.axis_size("seq")
    pairs = [
        (2 * i + c, 2 * (i ^ stride) + 1 - c) for i in range(n) for c in range(2)
    ]
    return lax.ppermute(x, ("seq", "tp"), pairs)


def in_hbm(x):
    return pltpu.with_memory_space_constraint(x, pltpu.HBM)


def tied(*values):
    return lax.optimization_barrier(values)


def body(
    queries, keys_values, prompt_lengths, routes, gate_weights, norm_gain, w_gate, w_up, w_down
):
    tokens, width = queries.shape[1:]
    rows_true = keys_values.shape[1]
    pad = -rows_true % TILE
    core = lax.axis_index("tp")
    own_queries = queries[0]
    strides = [1 << b for b in reversed(range(lax.axis_size("seq").bit_length() - 1))]

    kv = keys_values[0].reshape(rows_true, -1)
    if pad:
        kv = jnp.pad(kv, ((0, pad), (0, 0)))
    keep, send, comb = pl.pallas_call(
        pick_kernel,
        out_shape=[
            jax.ShapeDtypeStruct((CAP, width), jnp.bfloat16),
            jax.ShapeDtypeStruct((CAP, width), jnp.bfloat16),
            jax.ShapeDtypeStruct((2 * CAP, tokens), jnp.float32),
        ],
        in_specs=[SMEM] + [VMEM] * 3,
        out_specs=[VMEM] * 3,
        compiler_params=params(16),
        cost_estimate=cost(4 * CAP * tokens * width, 4 * tokens * width),
        name="pick",
    )(core.reshape(1), routes[0].T, gate_weights[0].T, own_queries)
    routed = jnp.concatenate([keep, swap(send)], axis=0)

    kv_blocks, routed_blocks, order = [kv], [routed], [0]
    for stride in strides[:-1]:
        kv_blocks = kv_blocks + [across(b, stride) for b in kv_blocks]
        routed_blocks = routed_blocks + [across(b, stride) for b in routed_blocks]
        order = order + [k ^ stride for k in order]
    first_kv, first_routed = across(kv, strides[-1]), across(routed, strides[-1])
    own_swapped = swap(kv)
    kv_blocks, routed_blocks, first_kv, own_swapped, first_routed = tied(
        kv_blocks, routed_blocks, first_kv, own_swapped, first_routed
    )
    last_kv = [across(b, strides[-1]) for b in kv_blocks[1:]]
    kv_blocks = kv_blocks + [first_kv] + last_kv
    order = order + [k ^ strides[-1] for k in order]
    rows = kv.shape[0]
    shares = 2 if rows % (2 * TILE) == 0 and not pad else 1
    cuts = range(0, rows, rows // shares)
    swapped = [own_swapped] + [swap(b) for b in kv_blocks[1:-1]]

    origins = [(k, side, 0) for side in (0, 1) for k in order[:-1]]
    first_pieces = kv_blocks[:-1] + swapped, origins
    length = prompt_lengths

    early = routed_blocks + [first_routed]
    late_blocks = [across(b, strides[-1]) for b in routed_blocks[1:-1]]
    early += late_blocks
    *begun, mark = begin_call(length, early, first_pieces, rows_true)
    held_back, mark = tied(routed_blocks[-1], mark)
    last_routed = across(held_back, strides[-1])
    last, mark = tied(kv_blocks[-1], mark)
    halves = halve_call(last) if shares == 2 else [last]
    last_pieces = (
        [last] + [swap(h) for h in halves],
        [(order[-1], 0, 0)] + [(order[-1], 1, c) for c in cuts],
    )
    pieces = tuple(a + b for a, b in zip(first_pieces, last_pieces))

    gain = norm_gain.reshape(1, width)
    done = finish_call(length, early, last_pieces, rows_true, gain, [*begun, mark])
    parts = expert_call(
        length, done, last_routed, pieces, gain, w_gate[0], in_hbm(w_up[0]), in_hbm(w_down[0]),
        order, rows_true,
    )

    own_queries, parts = tied(own_queries, parts)
    attended = attend_call(length, own_queries, pieces, rows_true)
    parts = dict(zip(order, parts))
    straight = {k: v[0] for k, v in parts.items()}
    cut = cut_of(width)
    held = {k: v[-1][:, cut - width :] for k, v in parts.items()}
    for stride in strides[::-1][:-1]:
        sent = {k: across(v, stride) for k, v in held.items() if k & stride and k != 1}
        held = {
            k: add(v, sent[k ^ stride]) if k ^ stride in sent else v
            for k, v in held.items()
            if not k & stride
        }
    late, attended = tied(held[strides[0]], attended)
    late_mine = across(late[:CAP], strides[0])
    late_theirs = across_and_swap(late[CAP:], strides[0])
    straight[1], attended = tied(straight[1], attended)
    arrived = [across(v, k) for k, v in straight.items() if k]
    arrived, late = tied(arrived, late)
    so_far = [
        jnp.concatenate(
            [
                add(straight[0][rows, :cut], *[a[rows, :cut] for a in arrived]),
                add(
                    held[0][rows],
                    *[a[rows, cut:] for a in arrived if a.shape[1] == width],
                ),
            ],
            axis=1,
        )
        for rows in (slice(None, CAP), slice(CAP, None))
    ]
    theirs = swap(so_far[1])
    mixed = mix_call(0, late_mine, comb, attended, so_far[0], jnp.float32)
    mixed = mix_call(CAP, late_theirs, comb, mixed, theirs, jnp.bfloat16)
    return mixed[None]


def solution(mesh):
    return jax.shard_map(
        body,
        mesh=mesh,
        in_specs=(
            P(("group", "exp"), ("seq", "tp"), None),
            P(("group", "exp"), ("seq", "tp"), None, None),
            P(("group", "exp")),
            P(("group", "exp"), ("seq", "tp"), None),
            P(("group", "exp"), ("seq", "tp"), None),
            P(),
            P("tp", None, "seq"),
            P("tp", None, "seq"),
            P("tp", "seq", None),
        ),
        out_specs=P(("group", "exp"), ("seq", "tp"), None),
        check_vma=False,
    )
```

```python
import functools
import math

import jax
import jax.numpy as jnp
from jax import lax
from jax.experimental import pallas as pl
from jax.experimental.pallas import tpu as pltpu
from jax.sharding import PartitionSpec as P

HEAD_DIM = 128
PROMPT = 256
CAP = 16
TILE = 16

epsilon = 1e-06
masked_score = -1e30
MIB = 1024 * 1024

VMEM = pl.BlockSpec(memory_space=pltpu.VMEM)
SMEM = pl.BlockSpec(memory_space=pltpu.SMEM)
HBM = pl.BlockSpec(memory_space=pltpu.HBM)


def params(mib):
    return pltpu.CompilerParams(vmem_limit_bytes=mib * MIB)


def cost(flops, moved, transcendentals=0):
    return pl.CostEstimate(
        flops=int(flops), bytes_accessed=int(moved), transcendentals=int(transcendentals)
    )


def pick_kernel(me_ref, routes_ref, gates_ref, q_ref, keep_ref, send_ref, comb_ref):
    top, tokens = routes_ref.shape
    me = me_ref[0]
    routes = routes_ref[...]
    gates = gates_ref[...]

    def of_expert(expert):
        hit = routes == expert
        member = jnp.sum(hit.astype(jnp.float32), axis=0, keepdims=True)
        weight = jnp.sum(jnp.where(hit, gates, 0.0), axis=0, keepdims=True)
        return member, weight

    member_a, weight_a = of_expert(me)
    member_b, weight_b = of_expert(1 - me)
    slot_of = lax.broadcasted_iota(jnp.int32, (2 * CAP, tokens), 0)
    mine = slot_of < CAP
    member = jnp.where(mine, member_a, member_b)
    weight = jnp.where(mine, weight_a, weight_b)
    row = lax.broadcasted_iota(jnp.int32, (tokens, tokens), 0)
    col = lax.broadcasted_iota(jnp.int32, (tokens, tokens), 1)
    before = jnp.where(row < col, 1.0, 0.0).astype(jnp.bfloat16)
    slot = jnp.dot(member.astype(jnp.bfloat16), before, preferred_element_type=jnp.float32)
    wanted = jnp.where(mine, slot_of, slot_of - CAP).astype(jnp.float32)
    taken = jnp.where((member > 0.0) & (slot == wanted), 1.0, 0.0)
    comb_ref[...] = taken * weight
    rows = jnp.dot(
        taken.astype(jnp.bfloat16), q_ref[...], preferred_element_type=jnp.float32
    ).astype(jnp.bfloat16)
    keep_ref[...] = rows[:CAP]
    send_ref[...] = rows[CAP:]


def key_bias(length_ref, kv_refs, origins, rows_true):
    seq, core = lax.axis_index("seq"), lax.axis_index("tp")
    length = length_ref[0]
    parts = []
    for r, (k, side, first) in zip(kv_refs, origins):
        row = lax.broadcasted_iota(jnp.int32, (8, r.shape[0]), 1) + first
        position = row + (2 * (seq ^ k) + (core ^ side)) * rows_true
        allowed = (position >= PROMPT) | (position < length)
        allowed = allowed & (row < rows_true)
        parts.append(jnp.where(allowed, 0.0, masked_score))
    return jnp.concatenate(parts, axis=1)[:1]


def attend(queries, kv_refs, bias, store, per_key, before=None, after=None):
    width = kv_refs[0].shape[1] // 2
    heads = width // HEAD_DIM
    factor = math.log2(math.e) / math.sqrt(HEAD_DIM)

    def one(head, _):
        at = head * HEAD_DIM
        if not isinstance(head, int):
            at = pl.multiple_of(at, HEAD_DIM)
        keys = jnp.concatenate([r[:, pl.ds(at, HEAD_DIM)] for r in kv_refs], axis=0)
        values = jnp.concatenate(
            [r[:, pl.ds(width + at, HEAD_DIM)] for r in kv_refs], axis=0
        )
        values = jnp.concatenate([values, jnp.ones_like(values)], axis=1)
        block = queries(at * per_key, per_key * HEAD_DIM)
        rows = block.shape[0]
        stacked = jnp.concatenate(
            [block[:, j * HEAD_DIM : (j + 1) * HEAD_DIM] for j in range(per_key)], axis=0
        )
        scores = (
            lax.dot_general(
                stacked, keys, (((1,), (1,)), ((), ())), preferred_element_type=jnp.float32
            )
            * factor
            + bias
        )
        largest = jnp.max(scores, axis=1, keepdims=True)
        mine = pl.ds(head * per_key * rows, per_key * rows)
        if before is not None:
            earlier = before[1][mine, :]
            largest = jnp.maximum(earlier, largest)
            scale = jnp.exp2(earlier - largest)
            count = -(-scores.shape[1] // HEAD_DIM)
            largest = jnp.concatenate([largest] * count, axis=1)[:, : scores.shape[1]]
        weights = jnp.exp2(scores - largest)
        summed = jnp.dot(
            weights.astype(jnp.bfloat16), values, preferred_element_type=jnp.float32
        )
        if before is not None:
            summed = summed + before[0][mine, :] * jnp.concatenate([scale, scale], axis=1)
        if after is not None:
            after[0][mine, :] = summed
            after[1][mine, :] = jnp.broadcast_to(largest, (per_key * rows, HEAD_DIM))
            return
        result = (summed[:, :HEAD_DIM] / summed[:, HEAD_DIM:]).astype(jnp.bfloat16)
        for j in range(per_key):
            store(at * per_key + j * HEAD_DIM, result[j * rows : (j + 1) * rows])

    if bias.shape[1] > 1024:
        lax.fori_loop(0, heads, one, None)
    else:
        for head in range(heads):
            one(head, None)


def norm(rows, gain):
    x = rows.astype(jnp.float32)
    square = jnp.mean(x * x, axis=1, keepdims=True)
    return (x * lax.rsqrt(square + epsilon) * gain).astype(jnp.bfloat16)


def columns_of(q_refs):
    def queries(at, size):
        return jnp.concatenate([r[:, pl.ds(at, size)] for r in q_refs], axis=0)

    return queries


def into(ref):
    def store(at, result):
        ref[:, pl.ds(at, HEAD_DIM)] = result

    return store


def attended_rows(queries, kv_refs, bias, scratch_ref, per_key, before=None):
    parts = []
    if bias.shape[1] > 1024:
        attend(queries, kv_refs, bias, into(scratch_ref), per_key, before)
        return scratch_ref[...]
    attend(queries, kv_refs, bias, lambda at, result: parts.append(result), per_key, before)
    return jnp.concatenate(parts, axis=1)


def attend_kernel(origins, per_key, rows_true, length_ref, q_ref, *refs):
    kv_refs = refs[: len(origins)]
    bias = key_bias(length_ref, kv_refs, origins, rows_true)
    attend(columns_of([q_ref]), kv_refs, bias, into(refs[-1]), per_key)


def begin_kernel(origins, per_key, rows_true, length_ref, *refs):
    pieces = len(origins)
    kv_refs, after, mark_ref = refs[-pieces - 3 : -3], refs[-3:-1], refs[-1]
    bias = key_bias(length_ref, kv_refs, origins, rows_true)
    attend(columns_of(refs[: -pieces - 3]), kv_refs, bias, None, per_key, after=after)
    mark_ref[...] = jnp.zeros_like(mark_ref)


def finish_kernel(origins, per_key, rows_true, length_ref, *refs):
    pieces = len(origins)
    gain_ref, sums_ref, largest_ref, _, out_ref = refs[-5:]
    kv_refs = refs[-pieces - 5 : -5]
    bias = key_bias(length_ref, kv_refs, origins, rows_true)
    queries = columns_of(refs[: -pieces - 5])
    state = sums_ref, largest_ref
    rows = attended_rows(queries, kv_refs, bias, out_ref, per_key, state)
    out_ref[...] = norm(rows, gain_ref[...])


def attention(kernel, name, length, q_blocks, pieces, rows_true, more, out_shape, price):
    kv_pieces, origins = pieces
    per_key = q_blocks[0].shape[1] // (kv_pieces[0].shape[1] // 2)
    large = sum(q.shape[0] for q in q_blocks) * sum(p.shape[0] for p in kv_pieces)
    count = len(q_blocks) + len(kv_pieces) + len(more)
    return pl.pallas_call(
        functools.partial(kernel, tuple(origins), per_key, rows_true),
        out_shape=out_shape,
        in_specs=[SMEM] + [VMEM] * count,
        out_specs=jax.tree.map(lambda _: VMEM, out_shape),
        compiler_params=params(20 if large < 1 << 17 else 58),
        cost_estimate=price,
        name=name,
    )(length, *q_blocks, *kv_pieces, *more)


def attend_call(length, queries, pieces, rows_true):
    rows, width = queries.shape
    keys = sum(p.shape[0] for p in pieces[0])
    shape = jax.ShapeDtypeStruct((rows, width), jnp.bfloat16)
    price = cost(
        4 * rows * width * keys,
        4 * rows * width + 2 * keys * pieces[0][0].shape[1],
        rows * keys * width // HEAD_DIM,
    )
    return attention(
        attend_kernel, "attend", length, [queries], pieces, rows_true, [], shape, price
    )


def begin_call(length, q_blocks, pieces, rows_true):
    rows = sum(q.shape[0] for q in q_blocks) * q_blocks[0].shape[1] // HEAD_DIM
    shapes = [
        jax.ShapeDtypeStruct((rows, 2 * HEAD_DIM), jnp.float32),
        jax.ShapeDtypeStruct((rows, HEAD_DIM), jnp.float32),
        jax.ShapeDtypeStruct((8, HEAD_DIM), jnp.float32),
    ]
    return attention(
        begin_kernel, "begin", length, q_blocks, pieces, rows_true, [], shapes, cost(1, 1)
    )


def finish_call(length, q_blocks, pieces, rows_true, gain, begun):
    rows = sum(q.shape[0] for q in q_blocks)
    shape = jax.ShapeDtypeStruct((rows, q_blocks[0].shape[1]), jnp.bfloat16)
    more = [gain, *begun]
    return attention(
        finish_kernel, "finish", length, q_blocks, pieces, rows_true, more, shape, cost(1, 1)
    )


def halve_kernel(whole_ref, top_ref, bottom_ref):
    rows = top_ref.shape[0]
    top_ref[...] = whole_ref[:rows]
    bottom_ref[...] = whole_ref[rows:]


def halve_call(whole):
    rows, width = whole.shape
    return pl.pallas_call(
        halve_kernel,
        out_shape=[jax.ShapeDtypeStruct((rows // 2, width), whole.dtype)] * 2,
        in_specs=[VMEM],
        out_specs=[VMEM] * 2,
        compiler_params=params(4),
        cost_estimate=cost(1, 1),
        name="halve",
    )(whole)


def cut_of(width):
    return width // 2 // HEAD_DIM * HEAD_DIM


def split_of(k, width):
    return [(0, width)] if k < 2 else [(0, cut_of(width)), (cut_of(width), width)]


def expert_kernel(
    origins, order, per_key, rows_true, last_ref, length_ref, done_ref, *refs
):
    pieces = len(origins)
    kv_refs = refs[:pieces]
    gain_ref, gate_ref, up_hbm, down_hbm = refs[pieces : pieces + 4]
    out_refs = refs[pieces + 4 : -4]
    x_ref, up_ref, down_ref, sems = refs[-4:]
    copies = [
        pltpu.make_async_copy(src, dst, sems.at[i])
        for i, (src, dst) in enumerate(
            ((up_hbm, up_ref), (down_hbm, down_ref))
        )
    ]
    for c in copies:
        c.start()
    bias = key_bias(length_ref, kv_refs, origins, rows_true)

    last = attended_rows(columns_of([last_ref]), kv_refs, bias, x_ref, per_key)
    normed = jnp.concatenate([done_ref[...], norm(last, gain_ref[...])], axis=0)
    gate = jnp.dot(normed, gate_ref[...], preferred_element_type=jnp.float32)
    copies[0].wait()
    up = jnp.dot(normed, up_ref[...], preferred_element_type=jnp.float32)
    hidden = (gate / (1.0 + jnp.exp(-gate)) * up).astype(jnp.bfloat16)
    copies[1].wait()
    part = jnp.dot(hidden, down_ref[...], preferred_element_type=jnp.float32).astype(
        jnp.bfloat16
    )
    each, width = last_ref.shape
    out = iter(out_refs)
    for i, k in enumerate(order):
        for begin, end in split_of(k, width):
            next(out)[...] = part[i * each : (i + 1) * each, begin:end]


def expert_call(length, done, last, pieces, gain, w_gate, w_up, w_down, order, rows_true):
    kv_pieces, origins = pieces
    each, width = last.shape
    rows = len(order) * each
    hidden = w_gate.shape[1]
    per_key = width // (kv_pieces[0].shape[1] // 2)
    splits = [split_of(k, width) for k in order]
    shapes = [
        jax.ShapeDtypeStruct((each, end - begin), jnp.bfloat16)
        for split in splits
        for begin, end in split
    ]
    outs = iter(
        pl.pallas_call(
            functools.partial(expert_kernel, tuple(origins), tuple(order), per_key, rows_true),
            out_shape=shapes,
            in_specs=[VMEM, SMEM] + [VMEM] * (3 + len(kv_pieces)) + [HBM] * 2,
            out_specs=[VMEM] * len(shapes),
            scratch_shapes=[
                pltpu.VMEM((each, width), jnp.bfloat16),
                pltpu.VMEM(w_up.shape, jnp.bfloat16),
                pltpu.VMEM(w_down.shape, jnp.bfloat16),
                pltpu.SemaphoreType.DMA((2,)),
            ],
            compiler_params=params(26 if rows * hidden < 1 << 17 else 44),
            cost_estimate=cost(6 * rows * width * hidden, 6 * width * hidden),
            name="experts",
        )(last, length, done, *kv_pieces, gain, w_gate, w_up, w_down)
    )
    return [[next(outs) for _ in split] for split in splits]


def add(*terms):
    total = terms[0].astype(jnp.float32)
    for t in terms[1:]:
        total = total + t.astype(jnp.float32)
    return total.astype(jnp.bfloat16)


def combine_kernel(
    late_ref, late_theirs_ref, comb_ref, attended_ref, mine_ref, theirs_ref, out_ref
):
    width = out_ref.shape[1]
    half = width - late_ref.shape[1]
    comb = comb_ref[...]
    high = comb.astype(jnp.bfloat16)
    low = (comb - high.astype(jnp.float32)).astype(jnp.bfloat16)
    both = (((0,), (0,)), ((), ()))

    def finish(rows, begin, end):
        rows = jnp.concatenate(rows, axis=0)
        added = lax.dot_general(
            high, rows, both, preferred_element_type=jnp.float32
        ) + lax.dot_general(low, rows, both, preferred_element_type=jnp.float32)
        out_ref[:, begin:end] = (
            attended_ref[:, begin:end].astype(jnp.float32) + added
        ).astype(jnp.bfloat16)

    finish([mine_ref[:, :half], theirs_ref[:, :half]], 0, half)
    finish(
        [
            add(mine_ref[:, half:], late_ref[...]),
            add(theirs_ref[:, half:], late_theirs_ref[...]),
        ],
        half,
        width,
    )


def across(x, stride):
    n = lax.axis_size("seq")
    return lax.ppermute(x, "seq", [(i, i ^ stride) for i in range(n)])


def swap(x):
    return lax.ppermute(x, "tp", [(0, 1), (1, 0)])


def across_and_swap(x, stride):
    n = lax.axis_size("seq")
    pairs = [
        (2 * i + c, 2 * (i ^ stride) + 1 - c) for i in range(n) for c in range(2)
    ]
    return lax.ppermute(x, ("seq", "tp"), pairs)


def in_hbm(x):
    return pltpu.with_memory_space_constraint(x, pltpu.HBM)


def tied(*values):
    return lax.optimization_barrier(values)


def body(
    queries, keys_values, prompt_lengths, routes, gate_weights, norm_gain, w_gate, w_up, w_down
):
    tokens, width = queries.shape[1:]
    rows_true = keys_values.shape[1]
    pad = -rows_true % TILE
    core = lax.axis_index("tp")
    own_queries = queries[0]
    strides = [1 << b for b in reversed(range(lax.axis_size("seq").bit_length() - 1))]

    kv = keys_values[0].reshape(rows_true, -1)
    if pad:
        kv = jnp.pad(kv, ((0, pad), (0, 0)))
    keep, send, comb = pl.pallas_call(
        pick_kernel,
        out_shape=[
            jax.ShapeDtypeStruct((CAP, width), jnp.bfloat16),
            jax.ShapeDtypeStruct((CAP, width), jnp.bfloat16),
            jax.ShapeDtypeStruct((2 * CAP, tokens), jnp.float32),
        ],
        in_specs=[SMEM] + [VMEM] * 3,
        out_specs=[VMEM] * 3,
        compiler_params=params(16),
        cost_estimate=cost(4 * CAP * tokens * width, 4 * tokens * width),
        name="pick",
    )(core.reshape(1), routes[0].T, gate_weights[0].T, own_queries)
    routed = jnp.concatenate([keep, swap(send)], axis=0)

    kv_blocks, routed_blocks, order = [kv], [routed], [0]
    for stride in strides[:-1]:
        kv_blocks = kv_blocks + [across(b, stride) for b in kv_blocks]
        routed_blocks = routed_blocks + [across(b, stride) for b in routed_blocks]
        order = order + [k ^ stride for k in order]
    first_kv, first_routed = across(kv, strides[-1]), across(routed, strides[-1])
    own_swapped = swap(kv)
    kv_blocks, routed_blocks, first_kv, own_swapped, first_routed = tied(
        kv_blocks, routed_blocks, first_kv, own_swapped, first_routed
    )
    last_kv = [across(b, strides[-1]) for b in kv_blocks[1:]]
    kv_blocks = kv_blocks + [first_kv] + last_kv
    order = order + [k ^ strides[-1] for k in order]
    rows = kv.shape[0]
    shares = 2 if rows % (2 * TILE) == 0 and not pad else 1
    cuts = range(0, rows, rows // shares)
    swapped = [own_swapped] + [swap(b) for b in kv_blocks[1:-1]]

    origins = [(k, side, 0) for side in (0, 1) for k in order[:-1]]
    first_pieces = kv_blocks[:-1] + swapped, origins
    length = prompt_lengths

    early = routed_blocks + [first_routed]
    late_blocks = [across(b, strides[-1]) for b in routed_blocks[1:-1]]
    early += late_blocks
    *begun, mark = begin_call(length, early, first_pieces, rows_true)
    held_back, mark = tied(routed_blocks[-1], mark)
    last_routed = across(held_back, strides[-1])
    last, mark = tied(kv_blocks[-1], mark)
    halves = halve_call(last) if shares == 2 else [last]
    last_pieces = (
        [last] + [swap(h) for h in halves],
        [(order[-1], 0, 0)] + [(order[-1], 1, c) for c in cuts],
    )
    pieces = tuple(a + b for a, b in zip(first_pieces, last_pieces))

    gain = norm_gain.reshape(1, width)
    done = finish_call(length, early, last_pieces, rows_true, gain, [*begun, mark])
    parts = expert_call(
        length, done, last_routed, pieces, gain, w_gate[0], in_hbm(w_up[0]), in_hbm(w_down[0]),
        order, rows_true,
    )

    own_queries, parts = tied(own_queries, parts)
    attended = attend_call(length, own_queries, pieces, rows_true)
    parts = dict(zip(order, parts))
    straight = {k: v[0] for k, v in parts.items()}
    cut = cut_of(width)
    held = {k: v[-1][:, cut - width :] for k, v in parts.items()}
    for stride in strides[::-1][:-1]:
        sent = {k: across(v, stride) for k, v in held.items() if k & stride and k != 1}
        held = {
            k: add(v, sent[k ^ stride]) if k ^ stride in sent else v
            for k, v in held.items()
            if not k & stride
        }
    late, attended = tied(held[strides[0]], attended)
    late_mine = across(late[:CAP], strides[0])
    late_theirs = across_and_swap(late[CAP:], strides[0])
    straight[1], attended = tied(straight[1], attended)
    arrived = [across(v, k) for k, v in straight.items() if k]
    arrived, late = tied(arrived, late)
    so_far = [
        jnp.concatenate(
            [
                add(straight[0][rows, :cut], *[a[rows, :cut] for a in arrived]),
                add(
                    held[0][rows],
                    *[a[rows, cut:] for a in arrived if a.shape[1] == width],
                ),
            ],
            axis=1,
        )
        for rows in (slice(None, CAP), slice(CAP, None))
    ]
    theirs = swap(so_far[1])
    mixed = pl.pallas_call(
        combine_kernel,
        out_shape=jax.ShapeDtypeStruct((tokens, width), jnp.bfloat16),
        in_specs=[VMEM] * 6,
        out_specs=VMEM,
        compiler_params=params(16),
        cost_estimate=cost(8 * CAP * tokens * width, 4 * tokens * width),
        name="combine",
    )(late_mine, late_theirs, comb, attended, so_far[0], theirs)
    return mixed[None]


def solution(mesh):
    return jax.shard_map(
        body,
        mesh=mesh,
        in_specs=(
            P(("group", "exp"), ("seq", "tp"), None),
            P(("group", "exp"), ("seq", "tp"), None, None),
            P(("group", "exp")),
            P(("group", "exp"), ("seq", "tp"), None),
            P(("group", "exp"), ("seq", "tp"), None),
            P(),
            P("tp", None, "seq"),
            P("tp", None, "seq"),
            P("tp", "seq", None),
        ),
        out_specs=P(("group", "exp"), ("seq", "tp"), None),
        check_vma=False,
    )
```

```python
import functools
import math

import jax
import jax.numpy as jnp
from jax import lax
from jax.experimental import pallas as pl
from jax.experimental.pallas import tpu as pltpu
from jax.sharding import PartitionSpec as P

HEAD_DIM = 128
PROMPT = 256
CAP = 16
TILE = 16

epsilon = 1e-06
masked_score = -1e30
MIB = 1024 * 1024

VMEM = pl.BlockSpec(memory_space=pltpu.VMEM)
SMEM = pl.BlockSpec(memory_space=pltpu.SMEM)
HBM = pl.BlockSpec(memory_space=pltpu.HBM)
ANY = pl.BlockSpec(memory_space=pl.ANY)


def params(mib):
    return pltpu.CompilerParams(vmem_limit_bytes=mib * MIB)


def cost(flops, moved, transcendentals=0):
    return pl.CostEstimate(
        flops=int(flops), bytes_accessed=int(moved), transcendentals=int(transcendentals)
    )


def pick_kernel(me_ref, routes_ref, gates_ref, q_ref, keep_ref, send_ref, comb_ref):
    top, tokens = routes_ref.shape
    me = me_ref[0]
    routes = routes_ref[...]
    gates = gates_ref[...]

    def of_expert(expert):
        hit = routes == expert
        member = jnp.sum(hit.astype(jnp.float32), axis=0, keepdims=True)
        weight = jnp.sum(jnp.where(hit, gates, 0.0), axis=0, keepdims=True)
        return member, weight

    member_a, weight_a = of_expert(me)
    member_b, weight_b = of_expert(1 - me)
    slot_of = lax.broadcasted_iota(jnp.int32, (2 * CAP, tokens), 0)
    mine = slot_of < CAP
    member = jnp.where(mine, member_a, member_b)
    weight = jnp.where(mine, weight_a, weight_b)
    row = lax.broadcasted_iota(jnp.int32, (tokens, tokens), 0)
    col = lax.broadcasted_iota(jnp.int32, (tokens, tokens), 1)
    before = jnp.where(row < col, 1.0, 0.0).astype(jnp.bfloat16)
    slot = jnp.dot(member.astype(jnp.bfloat16), before, preferred_element_type=jnp.float32)
    wanted = jnp.where(mine, slot_of, slot_of - CAP).astype(jnp.float32)
    taken = jnp.where((member > 0.0) & (slot == wanted), 1.0, 0.0)
    comb_ref[...] = taken * weight
    rows = jnp.dot(
        taken.astype(jnp.bfloat16), q_ref[...], preferred_element_type=jnp.float32
    ).astype(jnp.bfloat16)
    keep_ref[...] = rows[:CAP]
    send_ref[...] = rows[CAP:]


def key_bias(length_ref, kv_refs, origins, rows_true):
    seq, core = lax.axis_index("seq"), lax.axis_index("tp")
    length = length_ref[0]
    parts = []
    for r, (k, side, first) in zip(kv_refs, origins):
        row = lax.broadcasted_iota(jnp.int32, (8, r.shape[0]), 1) + first
        position = row + (2 * (seq ^ k) + (core ^ side)) * rows_true
        allowed = (position >= PROMPT) | (position < length)
        allowed = allowed & (row < rows_true)
        parts.append(jnp.where(allowed, 0.0, masked_score))
    return jnp.concatenate(parts, axis=1)[:1]


def attend(queries, kv_refs, bias, store, per_key, before=None, after=None):
    width = kv_refs[0].shape[1] // 2
    heads = width // HEAD_DIM
    factor = math.log2(math.e) / math.sqrt(HEAD_DIM)

    def one(head, _):
        at = head * HEAD_DIM
        if not isinstance(head, int):
            at = pl.multiple_of(at, HEAD_DIM)
        keys = jnp.concatenate([r[:, pl.ds(at, HEAD_DIM)] for r in kv_refs], axis=0)
        values = jnp.concatenate(
            [r[:, pl.ds(width + at, HEAD_DIM)] for r in kv_refs], axis=0
        )
        values = jnp.concatenate([values, jnp.ones_like(values)], axis=1)
        block = queries(at * per_key, per_key * HEAD_DIM)
        rows = block.shape[0]
        stacked = jnp.concatenate(
            [block[:, j * HEAD_DIM : (j + 1) * HEAD_DIM] for j in range(per_key)], axis=0
        )
        scores = (
            lax.dot_general(
                stacked, keys, (((1,), (1,)), ((), ())), preferred_element_type=jnp.float32
            )
            * factor
            + bias
        )
        largest = jnp.max(scores, axis=1, keepdims=True)
        mine = pl.ds(head * per_key * rows, per_key * rows)
        if before is not None:
            earlier = before[1][mine, :]
            largest = jnp.maximum(earlier, largest)
            scale = jnp.exp2(earlier - largest)
            count = -(-scores.shape[1] // HEAD_DIM)
            largest = jnp.concatenate([largest] * count, axis=1)[:, : scores.shape[1]]
        weights = jnp.exp2(scores - largest)
        summed = jnp.dot(
            weights.astype(jnp.bfloat16), values, preferred_element_type=jnp.float32
        )
        if before is not None:
            summed = summed + before[0][mine, :] * jnp.concatenate([scale, scale], axis=1)
        if after is not None:
            after[0][mine, :] = summed
            after[1][mine, :] = jnp.broadcast_to(largest, (per_key * rows, HEAD_DIM))
            return
        result = (summed[:, :HEAD_DIM] / summed[:, HEAD_DIM:]).astype(jnp.bfloat16)
        for j in range(per_key):
            store(at * per_key + j * HEAD_DIM, result[j * rows : (j + 1) * rows])

    if bias.shape[1] > 1024:
        lax.fori_loop(0, heads, one, None)
    else:
        for head in range(heads):
            one(head, None)


def norm(rows, gain):
    x = rows.astype(jnp.float32)
    square = jnp.mean(x * x, axis=1, keepdims=True)
    return (x * lax.rsqrt(square + epsilon) * gain).astype(jnp.bfloat16)


def columns_of(q_refs):
    def queries(at, size):
        return jnp.concatenate([r[:, pl.ds(at, size)] for r in q_refs], axis=0)

    return queries


def into(ref):
    def store(at, result):
        ref[:, pl.ds(at, HEAD_DIM)] = result

    return store


def attended_rows(queries, kv_refs, bias, scratch_ref, per_key, before=None):
    parts = []
    if bias.shape[1] > 1024:
        attend(queries, kv_refs, bias, into(scratch_ref), per_key, before)
        return scratch_ref[...]
    attend(queries, kv_refs, bias, lambda at, result: parts.append(result), per_key, before)
    return jnp.concatenate(parts, axis=1)


def attend_kernel(origins, per_key, rows_true, length_ref, q_ref, *refs):
    kv_refs = refs[: len(origins)]
    bias = key_bias(length_ref, kv_refs, origins, rows_true)
    attend(columns_of([q_ref]), kv_refs, bias, into(refs[-1]), per_key)


def begin_kernel(origins, per_key, rows_true, length_ref, *refs):
    pieces = len(origins)
    kv_refs, after, mark_ref = refs[-pieces - 3 : -3], refs[-3:-1], refs[-1]
    bias = key_bias(length_ref, kv_refs, origins, rows_true)
    attend(columns_of(refs[: -pieces - 3]), kv_refs, bias, None, per_key, after=after)
    mark_ref[...] = jnp.zeros_like(mark_ref)


def finish_kernel(origins, per_key, rows_true, length_ref, *refs):
    pieces = len(origins)
    gain_ref, sums_ref, largest_ref, _, out_ref = refs[-5:]
    kv_refs = refs[-pieces - 5 : -5]
    bias = key_bias(length_ref, kv_refs, origins, rows_true)
    queries = columns_of(refs[: -pieces - 5])
    state = sums_ref, largest_ref
    rows = attended_rows(queries, kv_refs, bias, out_ref, per_key, state)
    out_ref[...] = norm(rows, gain_ref[...])


def attention(kernel, name, length, q_blocks, pieces, rows_true, more, out_shape, price):
    kv_pieces, origins = pieces
    per_key = q_blocks[0].shape[1] // (kv_pieces[0].shape[1] // 2)
    large = sum(q.shape[0] for q in q_blocks) * sum(p.shape[0] for p in kv_pieces)
    count = len(q_blocks) + len(kv_pieces) + len(more)
    return pl.pallas_call(
        functools.partial(kernel, tuple(origins), per_key, rows_true),
        out_shape=out_shape,
        in_specs=[SMEM] + [VMEM] * count,
        out_specs=jax.tree.map(lambda _: VMEM, out_shape),
        compiler_params=params(20 if large < 1 << 17 else 58),
        cost_estimate=price,
        name=name,
    )(length, *q_blocks, *kv_pieces, *more)


def attend_call(length, queries, pieces, rows_true):
    rows, width = queries.shape
    keys = sum(p.shape[0] for p in pieces[0])
    shape = jax.ShapeDtypeStruct((rows, width), jnp.bfloat16)
    price = cost(
        4 * rows * width * keys,
        4 * rows * width + 2 * keys * pieces[0][0].shape[1],
        rows * keys * width // HEAD_DIM,
    )
    return attention(
        attend_kernel, "attend", length, [queries], pieces, rows_true, [], shape, price
    )


def begin_call(length, q_blocks, pieces, rows_true):
    rows = sum(q.shape[0] for q in q_blocks) * q_blocks[0].shape[1] // HEAD_DIM
    shapes = [
        jax.ShapeDtypeStruct((rows, 2 * HEAD_DIM), jnp.float32),
        jax.ShapeDtypeStruct((rows, HEAD_DIM), jnp.float32),
        jax.ShapeDtypeStruct((8, HEAD_DIM), jnp.float32),
    ]
    return attention(
        begin_kernel, "begin", length, q_blocks, pieces, rows_true, [], shapes, cost(1, 1)
    )


def finish_call(length, q_blocks, pieces, rows_true, gain, begun):
    rows = sum(q.shape[0] for q in q_blocks)
    shape = jax.ShapeDtypeStruct((rows, q_blocks[0].shape[1]), jnp.bfloat16)
    more = [gain, *begun]
    return attention(
        finish_kernel, "finish", length, q_blocks, pieces, rows_true, more, shape, cost(1, 1)
    )


def halve_kernel(whole_ref, top_ref, bottom_ref):
    rows = top_ref.shape[0]
    top_ref[...] = whole_ref[:rows]
    bottom_ref[...] = whole_ref[rows:]


def halve_call(whole):
    rows, width = whole.shape
    return pl.pallas_call(
        halve_kernel,
        out_shape=[jax.ShapeDtypeStruct((rows // 2, width), whole.dtype)] * 2,
        in_specs=[VMEM],
        out_specs=[VMEM] * 2,
        compiler_params=params(4),
        cost_estimate=cost(1, 1),
        name="halve",
    )(whole)


def cut_of(width):
    return width * 3 // 8 // HEAD_DIM * HEAD_DIM


def split_of(k, width):
    return [(0, width)] if k < 2 else [(0, cut_of(width)), (cut_of(width), width)]


def expert_kernel(
    origins, order, per_key, rows_true, last_ref, length_ref, done_ref, *refs
):
    pieces = len(origins)
    kv_refs = refs[:pieces]
    gain_ref, gate_ref, up_hbm, down_hbm = refs[pieces : pieces + 4]
    out_refs = refs[pieces + 4 : -4]
    x_ref, up_ref, down_ref, sems = refs[-4:]
    copies = [
        pltpu.make_async_copy(src, dst, sems.at[i])
        for i, (src, dst) in enumerate(
            ((up_hbm, up_ref), (down_hbm, down_ref))
        )
    ]
    for c in copies:
        c.start()
    bias = key_bias(length_ref, kv_refs, origins, rows_true)

    last = attended_rows(columns_of([last_ref]), kv_refs, bias, x_ref, per_key)
    normed = jnp.concatenate([done_ref[...], norm(last, gain_ref[...])], axis=0)
    gate = jnp.dot(normed, gate_ref[...], preferred_element_type=jnp.float32)
    copies[0].wait()
    up = jnp.dot(normed, up_ref[...], preferred_element_type=jnp.float32)
    hidden = (gate / (1.0 + jnp.exp(-gate)) * up).astype(jnp.bfloat16)
    copies[1].wait()
    part = jnp.dot(hidden, down_ref[...], preferred_element_type=jnp.float32).astype(
        jnp.bfloat16
    )
    each, width = last_ref.shape
    out = iter(out_refs)
    for i, k in enumerate(order):
        for begin, end in split_of(k, width):
            next(out)[...] = part[i * each : (i + 1) * each, begin:end]


def expert_call(length, done, last, pieces, gain, w_gate, w_up, w_down, order, rows_true):
    kv_pieces, origins = pieces
    each, width = last.shape
    rows = len(order) * each
    hidden = w_gate.shape[1]
    per_key = width // (kv_pieces[0].shape[1] // 2)
    splits = [split_of(k, width) for k in order]
    shapes = [
        jax.ShapeDtypeStruct((each, end - begin), jnp.bfloat16)
        for split in splits
        for begin, end in split
    ]
    outs = iter(
        pl.pallas_call(
            functools.partial(expert_kernel, tuple(origins), tuple(order), per_key, rows_true),
            out_shape=shapes,
            in_specs=[VMEM, SMEM] + [VMEM] * (3 + len(kv_pieces)) + [HBM] * 2,
            out_specs=[VMEM] * len(shapes),
            scratch_shapes=[
                pltpu.VMEM((each, width), jnp.bfloat16),
                pltpu.VMEM(w_up.shape, jnp.bfloat16),
                pltpu.VMEM(w_down.shape, jnp.bfloat16),
                pltpu.SemaphoreType.DMA((2,)),
            ],
            compiler_params=params(26 if rows * hidden < 1 << 17 else 44),
            cost_estimate=cost(6 * rows * width * hidden, 6 * width * hidden),
            name="experts",
        )(last, length, done, *kv_pieces, gain, w_gate, w_up, w_down)
    )
    return [[next(outs) for _ in split] for split in splits]


def add(*terms):
    total = terms[0].astype(jnp.float32)
    for t in terms[1:]:
        total = total + t.astype(jnp.float32)
    return total.astype(jnp.bfloat16)


def combine_kernel(
    late_ref, late_theirs_ref, comb_ref, attended_ref, mine_ref, theirs_ref, out_hbm, out_ref, sems
):
    width = out_ref.shape[1]
    half = width - late_ref.shape[1]
    comb = comb_ref[...]
    high = comb.astype(jnp.bfloat16)
    low = (comb - high.astype(jnp.float32)).astype(jnp.bfloat16)
    both = (((0,), (0,)), ((), ()))

    copies = []

    def finish(rows, begin, end):
        rows = jnp.concatenate(rows, axis=0)
        added = lax.dot_general(
            high, rows, both, preferred_element_type=jnp.float32
        ) + lax.dot_general(low, rows, both, preferred_element_type=jnp.float32)
        out_ref[:, begin:end] = (
            attended_ref[:, begin:end].astype(jnp.float32) + added
        ).astype(jnp.bfloat16)
        columns = pl.ds(begin, end - begin)
        copies.append(
            pltpu.make_async_copy(
                out_ref.at[:, columns], out_hbm.at[:, columns], sems.at[len(copies)]
            )
        )
        copies[-1].start()

    finish([mine_ref[:, :half], theirs_ref[:, :half]], 0, half)
    finish(
        [
            add(mine_ref[:, half:], late_ref[...]),
            add(theirs_ref[:, half:], late_theirs_ref[...]),
        ],
        half,
        width,
    )
    for c in copies:
        c.wait()


def across(x, stride):
    n = lax.axis_size("seq")
    return lax.ppermute(x, "seq", [(i, i ^ stride) for i in range(n)])


def swap(x):
    return lax.ppermute(x, "tp", [(0, 1), (1, 0)])


def across_and_swap(x, stride):
    n = lax.axis_size("seq")
    pairs = [
        (2 * i + c, 2 * (i ^ stride) + 1 - c) for i in range(n) for c in range(2)
    ]
    return lax.ppermute(x, ("seq", "tp"), pairs)


def in_hbm(x):
    return pltpu.with_memory_space_constraint(x, pltpu.HBM)


def tied(*values):
    return lax.optimization_barrier(values)


def body(
    queries, keys_values, prompt_lengths, routes, gate_weights, norm_gain, w_gate, w_up, w_down
):
    tokens, width = queries.shape[1:]
    rows_true = keys_values.shape[1]
    pad = -rows_true % TILE
    core = lax.axis_index("tp")
    own_queries = queries[0]
    strides = [1 << b for b in reversed(range(lax.axis_size("seq").bit_length() - 1))]

    kv = keys_values[0].reshape(rows_true, -1)
    if pad:
        kv = jnp.pad(kv, ((0, pad), (0, 0)))
    keep, send, comb = pl.pallas_call(
        pick_kernel,
        out_shape=[
            jax.ShapeDtypeStruct((CAP, width), jnp.bfloat16),
            jax.ShapeDtypeStruct((CAP, width), jnp.bfloat16),
            jax.ShapeDtypeStruct((2 * CAP, tokens), jnp.float32),
        ],
        in_specs=[SMEM] + [VMEM] * 3,
        out_specs=[VMEM] * 3,
        compiler_params=params(16),
        cost_estimate=cost(4 * CAP * tokens * width, 4 * tokens * width),
        name="pick",
    )(core.reshape(1), routes[0].T, gate_weights[0].T, own_queries)
    routed = jnp.concatenate([keep, swap(send)], axis=0)

    kv_blocks, routed_blocks, order = [kv], [routed], [0]
    for stride in strides[:-1]:
        kv_blocks = kv_blocks + [across(b, stride) for b in kv_blocks]
        routed_blocks = routed_blocks + [across(b, stride) for b in routed_blocks]
        order = order + [k ^ stride for k in order]
    first_kv, first_routed = across(kv, strides[-1]), across(routed, strides[-1])
    own_swapped = swap(kv)
    kv_blocks, routed_blocks, first_kv, own_swapped, first_routed = tied(
        kv_blocks, routed_blocks, first_kv, own_swapped, first_routed
    )
    last_kv = [across(b, strides[-1]) for b in kv_blocks[1:]]
    kv_blocks = kv_blocks + [first_kv] + last_kv
    order = order + [k ^ strides[-1] for k in order]
    rows = kv.shape[0]
    shares = 2 if rows % (2 * TILE) == 0 and not pad else 1
    cuts = range(0, rows, rows // shares)
    swapped = [own_swapped] + [swap(b) for b in kv_blocks[1:-1]]

    origins = [(k, side, 0) for side in (0, 1) for k in order[:-1]]
    first_pieces = kv_blocks[:-1] + swapped, origins
    length = prompt_lengths

    early = routed_blocks + [first_routed]
    late_blocks = [across(b, strides[-1]) for b in routed_blocks[1:-1]]
    early += late_blocks
    *begun, mark = begin_call(length, early, first_pieces, rows_true)
    held_back, mark = tied(routed_blocks[-1], mark)
    last_routed = across(held_back, strides[-1])
    last, mark = tied(kv_blocks[-1], mark)
    halves = halve_call(last) if shares == 2 else [last]
    last_pieces = (
        [last] + [swap(h) for h in halves],
        [(order[-1], 0, 0)] + [(order[-1], 1, c) for c in cuts],
    )
    pieces = tuple(a + b for a, b in zip(first_pieces, last_pieces))

    gain = norm_gain.reshape(1, width)
    done = finish_call(length, early, last_pieces, rows_true, gain, [*begun, mark])
    parts = expert_call(
        length, done, last_routed, pieces, gain, w_gate[0], in_hbm(w_up[0]), in_hbm(w_down[0]),
        order, rows_true,
    )

    own_queries, parts = tied(own_queries, parts)
    attended = attend_call(length, own_queries, pieces, rows_true)
    parts = dict(zip(order, parts))
    straight = {k: v[0] for k, v in parts.items()}
    cut = cut_of(width)
    held = {k: v[-1][:, cut - width :] for k, v in parts.items()}
    for stride in strides[::-1][:-1]:
        sent = {k: across(v, stride) for k, v in held.items() if k & stride and k != 1}
        held = {
            k: add(v, sent[k ^ stride]) if k ^ stride in sent else v
            for k, v in held.items()
            if not k & stride
        }
    late, attended = tied(held[strides[0]], attended)
    late_mine = across(late[:CAP], strides[0])
    late_theirs = across_and_swap(late[CAP:], strides[0])
    straight[1], attended = tied(straight[1], attended)
    arrived = [across(v, k) for k, v in straight.items() if k]
    arrived, late = tied(arrived, late)
    so_far = [
        jnp.concatenate(
            [
                add(straight[0][rows, :cut], *[a[rows, :cut] for a in arrived]),
                add(
                    held[0][rows],
                    *[a[rows, cut:] for a in arrived if a.shape[1] == width],
                ),
            ],
            axis=1,
        )
        for rows in (slice(None, CAP), slice(CAP, None))
    ]
    theirs = swap(so_far[1])
    mixed = pl.pallas_call(
        combine_kernel,
        out_shape=jax.ShapeDtypeStruct((tokens, width), jnp.bfloat16),
        in_specs=[VMEM] * 6,
        out_specs=ANY,
        scratch_shapes=[
            pltpu.VMEM((tokens, width), jnp.bfloat16),
            pltpu.SemaphoreType.DMA((2,)),
        ],
        compiler_params=params(16),
        cost_estimate=cost(8 * CAP * tokens * width, 4 * tokens * width),
        name="combine",
    )(late_mine, late_theirs, comb, attended, so_far[0], theirs)
    return mixed[None]


def solution(mesh):
    return jax.shard_map(
        body,
        mesh=mesh,
        in_specs=(
            P(("group", "exp"), ("seq", "tp"), None),
            P(("group", "exp"), ("seq", "tp"), None, None),
            P(("group", "exp")),
            P(("group", "exp"), ("seq", "tp"), None),
            P(("group", "exp"), ("seq", "tp"), None),
            P(),
            P("tp", None, "seq"),
            P("tp", None, "seq"),
            P("tp", "seq", None),
        ),
        out_specs=P(("group", "exp"), ("seq", "tp"), None),
        check_vma=False,
    )
```

```python
import functools
import math

import jax
import jax.numpy as jnp
from jax import lax
from jax.experimental import pallas as pl
from jax.experimental.pallas import tpu as pltpu
from jax.sharding import PartitionSpec as P

HEAD_DIM = 128
PROMPT = 256
CAP = 16
TILE = 16

epsilon = 1e-06
masked_score = -1e30
MIB = 1024 * 1024

VMEM = pl.BlockSpec(memory_space=pltpu.VMEM)
SMEM = pl.BlockSpec(memory_space=pltpu.SMEM)
HBM = pl.BlockSpec(memory_space=pltpu.HBM)
ANY = pl.BlockSpec(memory_space=pl.ANY)


def params(mib):
    return pltpu.CompilerParams(vmem_limit_bytes=mib * MIB)


def cost(flops, moved, transcendentals=0):
    return pl.CostEstimate(
        flops=int(flops), bytes_accessed=int(moved), transcendentals=int(transcendentals)
    )


def pick_kernel(me_ref, routes_ref, gates_ref, q_ref, keep_ref, send_ref, comb_ref):
    top, tokens = routes_ref.shape
    me = me_ref[0]
    routes = routes_ref[...]
    gates = gates_ref[...]

    def of_expert(expert):
        hit = routes == expert
        member = jnp.sum(hit.astype(jnp.float32), axis=0, keepdims=True)
        weight = jnp.sum(jnp.where(hit, gates, 0.0), axis=0, keepdims=True)
        return member, weight

    member_a, weight_a = of_expert(me)
    member_b, weight_b = of_expert(1 - me)
    slot_of = lax.broadcasted_iota(jnp.int32, (2 * CAP, tokens), 0)
    mine = slot_of < CAP
    member = jnp.where(mine, member_a, member_b)
    weight = jnp.where(mine, weight_a, weight_b)
    row = lax.broadcasted_iota(jnp.int32, (tokens, tokens), 0)
    col = lax.broadcasted_iota(jnp.int32, (tokens, tokens), 1)
    before = jnp.where(row < col, 1.0, 0.0).astype(jnp.bfloat16)
    slot = jnp.dot(member.astype(jnp.bfloat16), before, preferred_element_type=jnp.float32)
    wanted = jnp.where(mine, slot_of, slot_of - CAP).astype(jnp.float32)
    taken = jnp.where((member > 0.0) & (slot == wanted), 1.0, 0.0)
    comb_ref[...] = taken * weight
    rows = jnp.dot(
        taken.astype(jnp.bfloat16), q_ref[...], preferred_element_type=jnp.float32
    ).astype(jnp.bfloat16)
    keep_ref[...] = rows[:CAP]
    send_ref[...] = rows[CAP:]


def key_bias(length_ref, kv_refs, origins, rows_true):
    seq, core = lax.axis_index("seq"), lax.axis_index("tp")
    length = length_ref[0]
    parts = []
    for r, (k, side, first) in zip(kv_refs, origins):
        row = lax.broadcasted_iota(jnp.int32, (8, r.shape[0]), 1) + first
        position = row + (2 * (seq ^ k) + (core ^ side)) * rows_true
        allowed = (position >= PROMPT) | (position < length)
        allowed = allowed & (row < rows_true)
        parts.append(jnp.where(allowed, 0.0, masked_score))
    return jnp.concatenate(parts, axis=1)[:1]


def attend(queries, kv_refs, bias, store, per_key, before=None, after=None):
    width = kv_refs[0].shape[1] // 2
    heads = width // HEAD_DIM
    factor = math.log2(math.e) / math.sqrt(HEAD_DIM)

    def one(head, _):
        at = head * HEAD_DIM
        if not isinstance(head, int):
            at = pl.multiple_of(at, HEAD_DIM)
        keys = jnp.concatenate([r[:, pl.ds(at, HEAD_DIM)] for r in kv_refs], axis=0)
        values = jnp.concatenate(
            [r[:, pl.ds(width + at, HEAD_DIM)] for r in kv_refs], axis=0
        )
        values = jnp.concatenate([values, jnp.ones_like(values)], axis=1)
        block = queries(at * per_key, per_key * HEAD_DIM)
        rows = block.shape[0]
        stacked = jnp.concatenate(
            [block[:, j * HEAD_DIM : (j + 1) * HEAD_DIM] for j in range(per_key)], axis=0
        )
        scores = (
            lax.dot_general(
                stacked, keys, (((1,), (1,)), ((), ())), preferred_element_type=jnp.float32
            )
            * factor
            + bias
        )
        largest = jnp.max(scores, axis=1, keepdims=True)
        mine = pl.ds(head * per_key * rows, per_key * rows)
        if before is not None:
            earlier = before[1][mine, :]
            largest = jnp.maximum(earlier, largest)
            scale = jnp.exp2(earlier - largest)
            count = -(-scores.shape[1] // HEAD_DIM)
            largest = jnp.concatenate([largest] * count, axis=1)[:, : scores.shape[1]]
        weights = jnp.exp2(scores - largest)
        summed = jnp.dot(
            weights.astype(jnp.bfloat16), values, preferred_element_type=jnp.float32
        )
        if before is not None:
            summed = summed + before[0][mine, :] * jnp.concatenate([scale, scale], axis=1)
        if after is not None:
            after[0][mine, :] = summed
            after[1][mine, :] = jnp.broadcast_to(largest, (per_key * rows, HEAD_DIM))
            return
        result = (summed[:, :HEAD_DIM] / summed[:, HEAD_DIM:]).astype(jnp.bfloat16)
        for j in range(per_key):
            store(at * per_key + j * HEAD_DIM, result[j * rows : (j + 1) * rows])

    if bias.shape[1] > 1024:
        lax.fori_loop(0, heads, one, None)
    else:
        for head in range(heads):
            one(head, None)


def norm(rows, gain):
    x = rows.astype(jnp.float32)
    square = jnp.mean(x * x, axis=1, keepdims=True)
    return (x * lax.rsqrt(square + epsilon) * gain).astype(jnp.bfloat16)


def columns_of(q_refs):
    def queries(at, size):
        return jnp.concatenate([r[:, pl.ds(at, size)] for r in q_refs], axis=0)

    return queries


def into(ref):
    def store(at, result):
        ref[:, pl.ds(at, HEAD_DIM)] = result

    return store


def attended_rows(queries, kv_refs, bias, scratch_ref, per_key, before=None):
    parts = []
    if bias.shape[1] > 1024:
        attend(queries, kv_refs, bias, into(scratch_ref), per_key, before)
        return scratch_ref[...]
    attend(queries, kv_refs, bias, lambda at, result: parts.append(result), per_key, before)
    return jnp.concatenate(parts, axis=1)


def attend_kernel(origins, per_key, rows_true, length_ref, q_ref, *refs):
    kv_refs = refs[: len(origins)]
    bias = key_bias(length_ref, kv_refs, origins, rows_true)
    attend(columns_of([q_ref]), kv_refs, bias, into(refs[-1]), per_key)


def begin_kernel(origins, per_key, rows_true, length_ref, *refs):
    pieces = len(origins)
    kv_refs, after, mark_ref = refs[-pieces - 3 : -3], refs[-3:-1], refs[-1]
    bias = key_bias(length_ref, kv_refs, origins, rows_true)
    attend(columns_of(refs[: -pieces - 3]), kv_refs, bias, None, per_key, after=after)
    mark_ref[...] = jnp.zeros_like(mark_ref)


def finish_kernel(origins, per_key, rows_true, length_ref, *refs):
    pieces = len(origins)
    gain_ref, sums_ref, largest_ref, _, out_ref = refs[-5:]
    kv_refs = refs[-pieces - 5 : -5]
    bias = key_bias(length_ref, kv_refs, origins, rows_true)
    queries = columns_of(refs[: -pieces - 5])
    state = sums_ref, largest_ref
    rows = attended_rows(queries, kv_refs, bias, out_ref, per_key, state)
    out_ref[...] = norm(rows, gain_ref[...])


def attention(kernel, name, length, q_blocks, pieces, rows_true, more, out_shape, price):
    kv_pieces, origins = pieces
    per_key = q_blocks[0].shape[1] // (kv_pieces[0].shape[1] // 2)
    large = sum(q.shape[0] for q in q_blocks) * sum(p.shape[0] for p in kv_pieces)
    count = len(q_blocks) + len(kv_pieces) + len(more)
    return pl.pallas_call(
        functools.partial(kernel, tuple(origins), per_key, rows_true),
        out_shape=out_shape,
        in_specs=[SMEM] + [VMEM] * count,
        out_specs=jax.tree.map(lambda _: VMEM, out_shape),
        compiler_params=params(20 if large < 1 << 17 else 58),
        cost_estimate=price,
        name=name,
    )(length, *q_blocks, *kv_pieces, *more)


def attend_call(length, queries, pieces, rows_true):
    rows, width = queries.shape
    keys = sum(p.shape[0] for p in pieces[0])
    shape = jax.ShapeDtypeStruct((rows, width), jnp.bfloat16)
    price = cost(
        4 * rows * width * keys,
        4 * rows * width + 2 * keys * pieces[0][0].shape[1],
        rows * keys * width // HEAD_DIM,
    )
    return attention(
        attend_kernel, "attend", length, [queries], pieces, rows_true, [], shape, price
    )


def begin_call(length, q_blocks, pieces, rows_true):
    rows = sum(q.shape[0] for q in q_blocks) * q_blocks[0].shape[1] // HEAD_DIM
    shapes = [
        jax.ShapeDtypeStruct((rows, 2 * HEAD_DIM), jnp.float32),
        jax.ShapeDtypeStruct((rows, HEAD_DIM), jnp.float32),
        jax.ShapeDtypeStruct((8, HEAD_DIM), jnp.float32),
    ]
    return attention(
        begin_kernel, "begin", length, q_blocks, pieces, rows_true, [], shapes, cost(1, 1)
    )


def finish_call(length, q_blocks, pieces, rows_true, gain, begun):
    rows = sum(q.shape[0] for q in q_blocks)
    shape = jax.ShapeDtypeStruct((rows, q_blocks[0].shape[1]), jnp.bfloat16)
    more = [gain, *begun]
    return attention(
        finish_kernel, "finish", length, q_blocks, pieces, rows_true, more, shape, cost(1, 1)
    )


def halve_kernel(whole_ref, top_ref, bottom_ref):
    rows = top_ref.shape[0]
    top_ref[...] = whole_ref[:rows]
    bottom_ref[...] = whole_ref[rows:]


def halve_call(whole):
    rows, width = whole.shape
    return pl.pallas_call(
        halve_kernel,
        out_shape=[jax.ShapeDtypeStruct((rows // 2, width), whole.dtype)] * 2,
        in_specs=[VMEM],
        out_specs=[VMEM] * 2,
        compiler_params=params(4),
        cost_estimate=cost(1, 1),
        name="halve",
    )(whole)


def cut_of(width):
    return width * 3 // 8 // HEAD_DIM * HEAD_DIM


def split_of(k, width):
    return [(0, width)] if k < 2 else [(0, cut_of(width)), (cut_of(width), width)]


def expert_kernel(
    origins, order, per_key, rows_true, last_ref, length_ref, done_ref, *refs
):
    pieces = len(origins)
    kv_refs = refs[:pieces]
    gain_ref, gate_ref, up_ref, down_hbm = refs[pieces : pieces + 4]
    out_refs = refs[pieces + 4 : -3]
    x_ref, down_ref, sems = refs[-3:]
    copies = [
        pltpu.make_async_copy(src, dst, sems.at[i])
        for i, (src, dst) in enumerate(
            ((down_hbm, down_ref),)
        )
    ]
    for c in copies:
        c.start()
    bias = key_bias(length_ref, kv_refs, origins, rows_true)

    last = attended_rows(columns_of([last_ref]), kv_refs, bias, x_ref, per_key)
    normed = jnp.concatenate([done_ref[...], norm(last, gain_ref[...])], axis=0)
    gate = jnp.dot(normed, gate_ref[...], preferred_element_type=jnp.float32)
    up = jnp.dot(normed, up_ref[...], preferred_element_type=jnp.float32)
    hidden = (gate / (1.0 + jnp.exp(-gate)) * up).astype(jnp.bfloat16)
    copies[0].wait()
    part = jnp.dot(hidden, down_ref[...], preferred_element_type=jnp.float32).astype(
        jnp.bfloat16
    )
    each, width = last_ref.shape
    out = iter(out_refs)
    for i, k in enumerate(order):
        for begin, end in split_of(k, width):
            next(out)[...] = part[i * each : (i + 1) * each, begin:end]


def expert_call(length, done, last, pieces, gain, w_gate, w_up, w_down, order, rows_true):
    kv_pieces, origins = pieces
    each, width = last.shape
    rows = len(order) * each
    hidden = w_gate.shape[1]
    per_key = width // (kv_pieces[0].shape[1] // 2)
    splits = [split_of(k, width) for k in order]
    shapes = [
        jax.ShapeDtypeStruct((each, end - begin), jnp.bfloat16)
        for split in splits
        for begin, end in split
    ]
    outs = iter(
        pl.pallas_call(
            functools.partial(expert_kernel, tuple(origins), tuple(order), per_key, rows_true),
            out_shape=shapes,
            in_specs=[VMEM, SMEM] + [VMEM] * (4 + len(kv_pieces)) + [HBM],
            out_specs=[VMEM] * len(shapes),
            scratch_shapes=[
                pltpu.VMEM((each, width), jnp.bfloat16),
                pltpu.VMEM(w_down.shape, jnp.bfloat16),
                pltpu.SemaphoreType.DMA((2,)),
            ],
            compiler_params=params(26 if rows * hidden < 1 << 17 else 44),
            cost_estimate=cost(6 * rows * width * hidden, 6 * width * hidden),
            name="experts",
        )(last, length, done, *kv_pieces, gain, w_gate, w_up, w_down)
    )
    return [[next(outs) for _ in split] for split in splits]


def add(*terms):
    total = terms[0].astype(jnp.float32)
    for t in terms[1:]:
        total = total + t.astype(jnp.float32)
    return total.astype(jnp.bfloat16)


def combine_kernel(
    late_ref, late_theirs_ref, comb_ref, attended_ref, mine_ref, theirs_ref, out_hbm, out_ref, sems
):
    width = out_ref.shape[1]
    half = width - late_ref.shape[1]
    comb = comb_ref[...]
    high = comb.astype(jnp.bfloat16)
    low = (comb - high.astype(jnp.float32)).astype(jnp.bfloat16)
    both = (((0,), (0,)), ((), ()))

    copies = []

    def finish(rows, begin, end):
        rows = jnp.concatenate(rows, axis=0)
        added = lax.dot_general(
            high, rows, both, preferred_element_type=jnp.float32
        ) + lax.dot_general(low, rows, both, preferred_element_type=jnp.float32)
        out_ref[:, begin:end] = (
            attended_ref[:, begin:end].astype(jnp.float32) + added
        ).astype(jnp.bfloat16)
        columns = pl.ds(begin, end - begin)
        copies.append(
            pltpu.make_async_copy(
                out_ref.at[:, columns], out_hbm.at[:, columns], sems.at[len(copies)]
            )
        )
        copies[-1].start()

    finish([mine_ref[:, :half], theirs_ref[:, :half]], 0, half)
    finish(
        [
            add(mine_ref[:, half:], late_ref[...]),
            add(theirs_ref[:, half:], late_theirs_ref[...]),
        ],
        half,
        width,
    )
    for c in copies:
        c.wait()


def across(x, stride):
    n = lax.axis_size("seq")
    return lax.ppermute(x, "seq", [(i, i ^ stride) for i in range(n)])


def swap(x):
    return lax.ppermute(x, "tp", [(0, 1), (1, 0)])


def across_and_swap(x, stride):
    n = lax.axis_size("seq")
    pairs = [
        (2 * i + c, 2 * (i ^ stride) + 1 - c) for i in range(n) for c in range(2)
    ]
    return lax.ppermute(x, ("seq", "tp"), pairs)


def in_hbm(x):
    return pltpu.with_memory_space_constraint(x, pltpu.HBM)


def tied(*values):
    return lax.optimization_barrier(values)


def body(
    queries, keys_values, prompt_lengths, routes, gate_weights, norm_gain, w_gate, w_up, w_down
):
    tokens, width = queries.shape[1:]
    rows_true = keys_values.shape[1]
    pad = -rows_true % TILE
    core = lax.axis_index("tp")
    own_queries = queries[0]
    strides = [1 << b for b in reversed(range(lax.axis_size("seq").bit_length() - 1))]

    kv = keys_values[0].reshape(rows_true, -1)
    if pad:
        kv = jnp.pad(kv, ((0, pad), (0, 0)))
    keep, send, comb = pl.pallas_call(
        pick_kernel,
        out_shape=[
            jax.ShapeDtypeStruct((CAP, width), jnp.bfloat16),
            jax.ShapeDtypeStruct((CAP, width), jnp.bfloat16),
            jax.ShapeDtypeStruct((2 * CAP, tokens), jnp.float32),
        ],
        in_specs=[SMEM] + [VMEM] * 3,
        out_specs=[VMEM] * 3,
        compiler_params=params(16),
        cost_estimate=cost(4 * CAP * tokens * width, 4 * tokens * width),
        name="pick",
    )(core.reshape(1), routes[0].T, gate_weights[0].T, own_queries)
    routed = jnp.concatenate([keep, swap(send)], axis=0)

    kv_blocks, routed_blocks, order = [kv], [routed], [0]
    for stride in strides[:-1]:
        kv_blocks = kv_blocks + [across(b, stride) for b in kv_blocks]
        routed_blocks = routed_blocks + [across(b, stride) for b in routed_blocks]
        order = order + [k ^ stride for k in order]
    first_kv, first_routed = across(kv, strides[-1]), across(routed, strides[-1])
    own_swapped = swap(kv)
    kv_blocks, routed_blocks, first_kv, own_swapped, first_routed = tied(
        kv_blocks, routed_blocks, first_kv, own_swapped, first_routed
    )
    last_kv = [across(b, strides[-1]) for b in kv_blocks[1:]]
    kv_blocks = kv_blocks + [first_kv] + last_kv
    order = order + [k ^ strides[-1] for k in order]
    rows = kv.shape[0]
    shares = 2 if rows % (2 * TILE) == 0 and not pad else 1
    cuts = range(0, rows, rows // shares)
    swapped = [own_swapped] + [swap(b) for b in kv_blocks[1:-1]]

    origins = [(k, side, 0) for side in (0, 1) for k in order[:-1]]
    first_pieces = kv_blocks[:-1] + swapped, origins
    length = prompt_lengths

    early = routed_blocks + [first_routed]
    late_blocks = [across(b, strides[-1]) for b in routed_blocks[1:-1]]
    early += late_blocks
    *begun, mark = begin_call(length, early, first_pieces, rows_true)
    held_back, mark = tied(routed_blocks[-1], mark)
    last_routed = across(held_back, strides[-1])
    last, mark = tied(kv_blocks[-1], mark)
    halves = halve_call(last) if shares == 2 else [last]
    last_pieces = (
        [last] + [swap(h) for h in halves],
        [(order[-1], 0, 0)] + [(order[-1], 1, c) for c in cuts],
    )
    pieces = tuple(a + b for a, b in zip(first_pieces, last_pieces))

    gain = norm_gain.reshape(1, width)
    done = finish_call(length, early, last_pieces, rows_true, gain, [*begun, mark])
    parts = expert_call(
        length, done, last_routed, pieces, gain, w_gate[0], w_up[0], in_hbm(w_down[0]),
        order, rows_true,
    )

    own_queries, parts = tied(own_queries, parts)
    attended = attend_call(length, own_queries, pieces, rows_true)
    parts = dict(zip(order, parts))
    straight = {k: v[0] for k, v in parts.items()}
    cut = cut_of(width)
    held = {k: v[-1][:, cut - width :] for k, v in parts.items()}
    for stride in strides[::-1][:-1]:
        sent = {k: across(v, stride) for k, v in held.items() if k & stride and k != 1}
        held = {
            k: add(v, sent[k ^ stride]) if k ^ stride in sent else v
            for k, v in held.items()
            if not k & stride
        }
    late, attended = tied(held[strides[0]], attended)
    late_mine = across(late[:CAP], strides[0])
    late_theirs = across_and_swap(late[CAP:], strides[0])
    straight[1], attended = tied(straight[1], attended)
    arrived = [across(v, k) for k, v in straight.items() if k]
    arrived, late = tied(arrived, late)
    so_far = [
        jnp.concatenate(
            [
                add(straight[0][rows, :cut], *[a[rows, :cut] for a in arrived]),
                add(
                    held[0][rows],
                    *[a[rows, cut:] for a in arrived if a.shape[1] == width],
                ),
            ],
            axis=1,
        )
        for rows in (slice(None, CAP), slice(CAP, None))
    ]
    theirs = swap(so_far[1])
    mixed = pl.pallas_call(
        combine_kernel,
        out_shape=jax.ShapeDtypeStruct((tokens, width), jnp.bfloat16),
        in_specs=[VMEM] * 6,
        out_specs=ANY,
        scratch_shapes=[
            pltpu.VMEM((tokens, width), jnp.bfloat16),
            pltpu.SemaphoreType.DMA((2,)),
        ],
        compiler_params=params(16),
        cost_estimate=cost(8 * CAP * tokens * width, 4 * tokens * width),
        name="combine",
    )(late_mine, late_theirs, comb, attended, so_far[0], theirs)
    return mixed[None]


def solution(mesh):
    return jax.shard_map(
        body,
        mesh=mesh,
        in_specs=(
            P(("group", "exp"), ("seq", "tp"), None),
            P(("group", "exp"), ("seq", "tp"), None, None),
            P(("group", "exp")),
            P(("group", "exp"), ("seq", "tp"), None),
            P(("group", "exp"), ("seq", "tp"), None),
            P(),
            P("tp", None, "seq"),
            P("tp", None, "seq"),
            P("tp", "seq", None),
        ),
        out_specs=P(("group", "exp"), ("seq", "tp"), None),
        check_vma=False,
    )
```
